32 devices in a mesh: macro: 8 (over y, x, core), grid: 4 (over z).
Axes of the slice: x: 2, y: 2, z: 4, core: 2. Of those that a mesh axis runs over, the one named last changes fastest.
Arguments:
- orbitals: float32 [8, 2, 16, 32, 1024], P('macro', None, None, 'grid'), may hold values from -45 to 45
- local_potential: float32 [32, 1024], P('grid'), may hold values from -8 to 2
- atom_sites: int32 [8, 3], replicated, may hold values from 0 to 31, as said below
- host_point: int32 [8], P('macro'), may hold values from 0 to 511, as said below
- fields: float32 [2, 512], P(None, 'macro'), may hold values from -4 to 4
Outputs:
- orbitals_out: float32 [8, 2, 16, 32, 1024], P('macro', None, None, 'grid')
- fields_out: float32 [2, 512], P(None, 'macro')
The draws below stay inside these ranges and needn't reach their ends.
Inputs may be any that keep to these rules, and one draw needn't show every extreme that they name: `host_point`: distinct macroscopic points; for every index g of macro the points g * 64 to (g + 1) * 64 - 1 hold exactly one of them. `atom_sites`: two atoms may share a position.
All inputs are finite; a program needn't handle non-finite values.
Results may differ from the reference program's by a relative error of at most 0.0003.
Values sent between devices are 32-bit elements; how exact they have to be, the bound alone decides.
No kernel may reach another device: no remote copies, remote signals or barrier semaphores. Data moves between devices by JAX's collectives and lax.ppermute only.
A program may use at most 128 MiB of HBM per device.

```python
import jax
import jax.numpy as jnp
from jax import lax

G = 32
NORB = 16
NATOM = 8
MPT = 64
ORDER = 4
STEPS = 2
NMAC = 512
NMIC = 8
GG = 1024


def draw_orbitals(key, part):
    key = jax.random.fold_in(key, 11)
    keys = jax.random.split(key, 9)
    shape = (NMIC, 2, NORB, G, G * G)
    noise = 0.15 * jnp.clip(jax.random.normal(keys[1], shape, jnp.float32), -4.0, 4.0)
    rise = 2.3
    pattern_size = 2.2
    smooth_size = 0.25
    region_size = 0.4
    turn = 6.283185307179586
    plane_index = lax.broadcasted_iota(jnp.int32, (G, G * G), 0)
    cell_index = lax.broadcasted_iota(jnp.int32, (G, G * G), 1)
    row_index = cell_index // G
    column_index = cell_index % G
    parity = (plane_index + row_index + column_index) % 2
    checker = 1.0 - 2.0 * parity.astype(jnp.float32)
    plane_float = plane_index.astype(jnp.float32)
    row_float = row_index.astype(jnp.float32)
    column_float = column_index.astype(jnp.float32)
    phase = jax.random.uniform(keys[2], (NMIC, NORB, 1, 1), jnp.float32, -3.14159, 3.14159)
    jitter = jax.random.uniform(keys[3], (NMIC, NORB, G, G * G), jnp.float32, 0.9, 1.1)
    coefficients = jax.random.uniform(keys[4], (NMIC, 2, NORB, 1, 1), jnp.float32, 0.5, 1.5)
    first_shift = jax.random.uniform(keys[5], (NMIC, 1, 1, 1), jnp.float32, -3.14159, 3.14159)
    second_shift = jax.random.uniform(keys[6], (NMIC, 1, 1, 1), jnp.float32, -3.14159, 3.14159)
    third_shift = jax.random.uniform(keys[7], (NMIC, 1, 1, 1), jnp.float32, -3.14159, 3.14159)
    region = jnp.exp(region_size * (jnp.sin(turn * row_float / G + first_shift) + jnp.sin(turn * column_float / G + second_shift)))
    smooth = 1.0 + 0.5 * jnp.sin(turn * (plane_float + row_float + column_float) / G + third_shift)
    orbital_scale = jnp.exp(jax.random.uniform(keys[8], (NMIC, NORB, 1, 1), jnp.float32, -0.6, 0.56))
    wave = pattern_size * checker * jitter
    values_first = wave * jnp.cos(phase) + noise[:, 0] + smooth_size * coefficients[:, 0] * smooth
    values_second = wave * jnp.sin(phase) + noise[:, 1] + smooth_size * coefficients[:, 1] * smooth
    envelope = jnp.sqrt(1.0 + rise * plane_float / (G - 1))
    angle = turn * plane_float / G
    scale = orbital_scale * region * envelope
    cosine = jnp.cos(angle)
    sine = jnp.sin(angle)
    first_part = scale * (values_first * cosine - values_second * sine)
    second_part = scale * (values_first * sine + values_second * cosine)
    return jnp.stack([first_part, second_part], axis=1)


def draw_atom_sites(key, part):
    key = jax.random.fold_in(key, 37)
    sites = jax.random.randint(key, (NATOM, 3), 0, G, jnp.int32)
    sites = sites.at[0, 0].set(0)
    sites = sites.at[1, 0].set(G - 1)
    return sites


def draw_host_point(key, part):
    key = jax.random.fold_in(key, 23)
    systems = lax.broadcasted_iota(jnp.int32, (NMIC,), 0)
    halfway = NMIC // 2
    blocks = jnp.where(systems == 0, 1, jnp.where(systems == 1, 0, systems))
    blocks = jnp.where(systems == 2, 2 + halfway, jnp.where(systems == 2 + halfway, 2, blocks))
    offsets = jax.random.randint(key, (NMIC,), 0, MPT, jnp.int32)
    offsets = jnp.where(blocks == NMIC - 1, MPT - 1, offsets)
    offsets = jnp.where(blocks == 0, 0, offsets)
    return (blocks * MPT + offsets).astype(jnp.int32)


def level_of(rng, dims, cuts, low, top_value):
    gain, own = 1.0, jax.random.fold_in(rng, 6)
    for dim, parts in cuts:
        draws = jnp.exp(jax.random.uniform(jax.random.fold_in(own, dim), (parts,), jnp.float32, low / len(cuts), top_value / len(cuts)))
        gain = gain * jnp.repeat(draws, dims[dim] // parts).reshape([-1 if axis == dim else 1 for axis in range(len(dims))])
    return gain


def normal_values(stream_key, dims, scale, most, pieces=(), held_as=jnp.bfloat16):
    entries = jax.random.normal(stream_key, dims, jnp.float32) * scale
    if len(pieces) > 0:
        entries = level_of(stream_key, dims, pieces, -0.22, 0.18) * entries
    return jnp.clip(entries, min=-most, max=most).astype(held_as)


def setup_inputs(seed: int = 0) -> dict:
    key_of = jax.random.split(jax.random.key(seed), 6)
    return {
        "orbitals": draw_orbitals(jax.random.fold_in(key_of[5], 71), 0),
        "local_potential": jnp.clip(-8.0 + 10.0 * jax.random.uniform(key_of[1], (G, GG), jnp.float32) ** level_of(key_of[1], (G, GG), ((0, 4),), -0.2, 0.2), -8.0, 2.0),
        "atom_sites": draw_atom_sites(jax.random.fold_in(key_of[5], 71), 0),
        "host_point": draw_host_point(jax.random.fold_in(key_of[5], 71), 0),
        "fields": normal_values(key_of[4], (2, NMAC), 1.0, 4.0, ((1, 8),), jnp.float32),
    }


second_weights = (-205.0 / 72.0, 8.0 / 5.0, -1.0 / 5.0, 8.0 / 315.0, -1.0 / 560.0)
first_weights = (4.0 / 5.0, -1.0 / 5.0, 4.0 / 105.0, -1.0 / 280.0)
spacing = 0.3206
time_step = 0.02
courant_square = 0.81
source_weight = 0.1
radial_strength = 0.3
polar_strength = -0.2
projector_width = 2.5
highest = lax.Precision.HIGHEST


def along_last(field, offset, width):
    position = lax.broadcasted_iota(jnp.int32, (field.shape[-1],), 0) % width
    direct = jnp.roll(field, -offset, axis=-1)
    if offset > 0:
        wrapped = jnp.roll(field, width - offset, axis=-1)
        inside = position + offset < width
    else:
        wrapped = jnp.roll(field, -offset - width, axis=-1)
        inside = position + offset >= 0
    return jnp.where(inside, direct, wrapped)


def first_derivative(along_first):
    total = first_weights[0] * (along_first(1) - along_first(-1))
    for reach in range(2, 5):
        total = total + first_weights[reach - 1] * (along_first(reach) - along_first(-reach))
    return total / spacing


def laplacian(field, along_first, width):
    total = 3.0 * second_weights[0] * field
    for reach in range(1, 5):
        beside_all = along_first(reach) + along_first(-reach)
        beside_all = beside_all + jnp.roll(field, -reach * width, axis=-1) + jnp.roll(field, reach * width, axis=-1)
        beside_all = beside_all + along_last(field, reach, width) + along_last(field, -reach, width)
        total = total + second_weights[reach] * beside_all
    return total / (spacing * spacing)


def hamiltonian(field, along_first, potential, vector_value, project, width):
    derivative = first_derivative(along_first)
    drift = jnp.stack([vector_value * derivative[1], -vector_value * derivative[0]])
    local = (0.5 * vector_value * vector_value + potential) * field
    return -0.5 * laplacian(field, along_first, width) + drift + local + project(field)


def propagate(field, neighbours, potential, vector_value, project, width, order_count):
    total = field
    term = field
    for order in range(1, order_count + 1):
        image = hamiltonian(term, neighbours(term), potential, vector_value, project, width)
        term = (time_step / order) * jnp.stack([image[1], -image[0]])
        total = total + term
    return total


def projector_tables(atom_sites, width):
    positions = lax.broadcasted_iota(jnp.int32, (1, width), 1)
    tables = []
    for axis_number in range(3):
        offset = jnp.mod(positions - atom_sites[:, axis_number:axis_number + 1] + width // 2, width) - width // 2
        distance = offset.astype(jnp.float32)
        bell = jnp.exp(-0.5 * distance * distance / (projector_width * projector_width))
        rows = [bell, bell, bell, bell]
        rows[axis_number + 1] = (distance / projector_width) * bell
        tables.append(jnp.stack(rows, axis=1).reshape(-1, width))
    count = tables[1].shape[0]
    cross = (tables[1][:, :, None] * tables[2][:, None, :]).reshape(count, width * width)
    pattern = jnp.array([radial_strength, polar_strength, polar_strength, polar_strength], jnp.float32)
    strengths = jnp.tile(pattern, atom_sites.shape[0])
    return tables[0], cross, strengths


def nonlocal_part(field, first_table, cross_table, strengths, finish):
    inner = jnp.einsum("coxr,pr->coxp", field, cross_table, precision=highest)
    projection = finish(jnp.einsum("coxp,px->cop", inner, first_table, precision=highest))
    spread = jnp.einsum("cop,px->coxp", projection * strengths, first_table, precision=highest)
    return jnp.einsum("coxp,pr->coxr", spread, cross_table, precision=highest)


def reference(orbitals, local_potential, atom_sites, host_point, fields):
    width = local_potential.shape[0]
    first_table, cross_table, strengths = projector_tables(atom_sites, width)

    def project(field):
        return nonlocal_part(field, first_table, cross_table, strengths, lambda value: value)

    def neighbours(term):
        return lambda reach: jnp.roll(term, -reach, axis=2)

    def micro_step(packed):
        field, vector_value = packed
        moved = propagate(field, neighbours, local_potential, vector_value, project, width, ORDER)
        derivative = first_derivative(neighbours(moved))
        flow = jnp.sum(moved[0] * derivative[1] - moved[1] * derivative[0])
        density = jnp.sum(moved * moved)
        return moved, (flow + vector_value * density) / (width ** 3 * NORB)

    previous = fields[0]
    present = fields[1]
    points = lax.broadcasted_iota(jnp.int32, (fields.shape[1],), 0)
    state = orbitals
    for step in range(STEPS):
        vector_values = present[host_point]
        state, currents = lax.map(micro_step, (state, vector_values))
        source = jnp.sum(jnp.where(points[None, :] == host_point[:, None], currents[:, None], 0.0), axis=0)
        padded = jnp.pad(present, 1)
        following = 2.0 * present - previous + courant_square * (padded[2:] - 2.0 * present + padded[:-2]) - source_weight * source
        previous, present = present, following
    return state, jnp.stack([previous, present])
```

```python
import functools

import jax
import jax.numpy as jnp
import numpy as np
from jax import lax
from jax.experimental import pallas as pl
from jax.experimental.pallas import tpu as pltpu
from jax.sharding import PartitionSpec as P

ORDER = 4
STEPS = 2
spacing = 0.3206
time_step = 0.02
courant_square = 0.81
source_weight = 0.1
radial_strength = 0.3
polar_strength = -0.2
projector_width = 2.5

SECOND = (-14350.0, 8064.0, -1008.0, 128.0, -9.0)
FIRST = (672.0, -168.0, 32.0, -3.0)
KINETIC = 1.0 / (2.0 * 5040.0 * spacing * spacing)
SLOPE = 1.0 / (840.0 * spacing)

LANES = 128
ROWS = 8
LIMIT = 24 * 1024 * 1024


def stencil_weights(width):
    group = LANES // width
    total = np.zeros((LANES, 3 * LANES), np.float32)
    for y_in in range(group):
        for z_in in range(width):
            for y_out in range(group):
                for part, step in enumerate((0, group, -group)):
                    reach = abs(step + y_in - y_out)
                    if 1 <= reach <= 4:
                        total[y_in * width + z_in, part * LANES + y_out * width + z_in] += SECOND[reach]
            for reach in range(1, 5):
                for z_out in ((z_in + reach) % width, (z_in - reach) % width):
                    total[y_in * width + z_in, y_in * width + z_out] += SECOND[reach]
    return jnp.asarray(np.concatenate([total, total], axis=0), jnp.bfloat16)


def periodic(distance, width):
    return ((distance + width // 2) & (width - 1)) - width // 2


def bell_of(offset):
    distance = offset.astype(jnp.float32)
    bell = jnp.exp(-0.5 * distance * distance / (projector_width * projector_width))
    return bell, distance / projector_width * bell


def tables_kernel(atoms, planes, site_ref, grid_ref, stencil_ref, yz_ref, zy_ref, xbell_ref, xslope_ref, y_ref):
    width = xbell_ref.shape[0]
    kinds = 2 * atoms
    group = LANES // width

    def site_of(column, axis_number):
        atom = (column % kinds) // 2
        position = jnp.zeros(column.shape, jnp.int32)
        for number in range(atoms):
            position = jnp.where(atom == number, site_ref[number, axis_number], position)
        return position

    def factor(coordinate, column):
        bell, slope = bell_of(periodic(coordinate - site_of(column, 2), width))
        value = jnp.where(column % 2 == 0, bell, slope)
        high = value.astype(jnp.bfloat16).astype(jnp.float32)
        return jnp.where(column % LANES < LANES // 2, high, value - high)

    def groups_agree(point, column):
        return (point % LANES) // width == (column // kinds) % group

    shape = (2 * LANES, LANES)
    first = lax.broadcasted_iota(jnp.int32, shape, 0)
    last = lax.broadcasted_iota(jnp.int32, shape, 1)
    yz_ref[:, : 3 * LANES] = stencil_ref[...]
    inward = jnp.where(groups_agree(first, last), factor(first % width, last), 0.0)
    yz_ref[:, 3 * LANES :] = inward.astype(jnp.bfloat16)
    outward = jnp.where(groups_agree(last, first), factor(last % width, first), 0.0)
    zy_ref[...] = outward.astype(jnp.bfloat16)

    shape = (width, ROWS, LANES)
    plane = lax.broadcasted_iota(jnp.int32, shape, 0) + grid_ref[0] * planes
    column = lax.broadcasted_iota(jnp.int32, shape, 2)
    bell, slope = bell_of(periodic(plane - site_of(column, 0), width))
    xbell_ref[...] = bell
    xslope_ref[...] = slope

    shape = (ROWS, LANES)
    column = lax.broadcasted_iota(jnp.int32, shape, 1)
    row = lax.broadcasted_iota(jnp.int32, shape, 0) * group + (column // kinds) % group
    bell, slope = bell_of(periodic(row - site_of(column, 1), width))
    scale = -1.0 / KINETIC
    even = column % 2 == 0
    y_ref[0] = bell
    y_ref[1] = slope
    y_ref[2] = bell * jnp.where(even, scale * radial_strength, scale * polar_strength)
    y_ref[3] = bell * jnp.where(even, scale * polar_strength, 0.0)
    y_ref[4] = slope * jnp.where(even, scale * polar_strength, 0.0)


def vector_kernel(blocks, host_ref, *refs):
    out_ref = refs[blocks]
    owned = refs[0].shape[1]
    host = host_ref[0]
    here = host_ref[1]
    sums = [jnp.zeros((1, owned), jnp.float32) for _ in range(4)]
    for number in range(blocks):
        start = lax.rem(here + number, blocks) * owned
        position = lax.broadcasted_iota(jnp.int32, (1, owned), 1) + start
        previous = refs[number][0:1, :]
        present = refs[number][1:2, :]
        for index, (value, place) in enumerate(
            ((present, host), (previous, host), (present, host - 1), (present, host + 1))
        ):
            sums[index] = sums[index] + jnp.where(position == place, value, 0.0)
    present, previous, left, right = [jnp.sum(value) for value in sums]
    out_ref[0] = present
    out_ref[1] = 2.0 * present - previous + courant_square * (right - 2.0 * present + left)


def pack_kernel(parts, share, grid_ref, source_ref, *refs):
    outs, sems = refs[:-1], refs[-1]
    copies = []
    for part in range(parts):
        owner = lax.rem(grid_ref[0] + part, parts)
        for orbital in range(share):
            number = part * share + orbital
            copies.append(
                pltpu.make_async_copy(
                    source_ref.at[:, owner * share + orbital], outs[number], sems.at[number]
                )
            )
    for copy in copies:
        copy.start()
    for copy in copies:
        copy.wait()


def unpack_kernel(parts, share, grid_ref, *refs):
    pieces, out_ref, sems = refs[: parts * share], refs[parts * share], refs[parts * share + 1]
    copies = []
    for part in range(parts):
        owner = lax.rem(grid_ref[0] + parts - part, parts)
        for orbital in range(share):
            number = part * share + orbital
            copies.append(
                pltpu.make_async_copy(
                    pieces[number], out_ref.at[:, owner * share + orbital], sems.at[number]
                )
            )
    for copy in copies:
        copy.start()
    for copy in copies:
        copy.wait()


def roll_rows(value, shift):
    return pltpu.roll(value, shift % ROWS, 1)


def total_of_groups(value, kinds):
    for shift in (4, 2, 1):
        value = value + pltpu.roll(value, shift, 0)
    shift = LANES // 2
    while shift >= kinds:
        value = value + pltpu.roll(value, shift, 1)
        shift //= 2
    return value


def fold(values):
    while len(values) > 1:
        half = len(values) // 2
        values = [values[number] + values[number + half] for number in range(half)]
    return values[0]


def propagate_in_kernel(
    vector_value, field_ref, total_ref, potential_ref, tables, scratch, width, kinds
):
    yz_ref, zy_ref, xbell_ref, xslope_ref, y_ref = tables
    split_ref, product_ref, partial_ref, drift_ref, spread_ref, diagonal_ref = scratch
    diagonal_ref[...] = (3.0 * SECOND[0] - 0.5 * vector_value * vector_value / KINETIC) - potential_ref[
        ...
    ] * (1.0 / KINETIC)
    block = ROWS
    slab = block * ROWS

    def split(part, start, planes):
        rows = planes.reshape(slab, LANES)
        high = rows.astype(jnp.bfloat16)
        low = (rows - high.astype(jnp.float32)).astype(jnp.bfloat16)
        where = pl.ds((part * width + start) * ROWS, slab)
        return where, high, low

    for part in range(2):
        for start in range(0, width, block):
            planes = field_ref[part, start : start + block]
            where, high, low = split(part, start, planes)
            split_ref[where, :LANES] = high
            split_ref[where, LANES:] = low

    def one_order(order, carry):
        inverse = jnp.where(order == 1, 1.0, jnp.where(order == 2, 0.5, jnp.where(order == 3, 1.0 / 3.0, 0.25)))
        step_scale = inverse * time_step
        kinetic = step_scale * KINETIC
        drift = step_scale * SLOPE * vector_value
        slopes = [drift * weight for weight in FIRST]
        product_ref[...] = jnp.dot(split_ref[...], yz_ref[...], preferred_element_type=jnp.float32)
        bells = [jnp.zeros((ROWS, LANES), jnp.float32)] * 2
        inclines = [jnp.zeros((ROWS, LANES), jnp.float32)] * 2
        for start in range(0, width, block):
            for part in range(2):
                rows = pl.ds((part * width + start) * ROWS, slab)
                near = {
                    plane: field_ref[part, plane % width] for plane in range(start - 4, start + block + 4)
                }
                for index in range(block):
                    plane = start + index
                    line = pl.ds((part * width + plane) * ROWS, ROWS)
                    total = product_ref[line, :LANES]
                    total = total + pltpu.roll(product_ref[line, LANES : 2 * LANES], ROWS - 1, 0)
                    total = total + pltpu.roll(product_ref[line, 2 * LANES : 3 * LANES], 1, 0)
                    inner = product_ref[line, 3 * LANES :]
                    bells[part] = bells[part] + inner * xbell_ref[plane]
                    inclines[part] = inclines[part] + inner * xslope_ref[plane]
                    total = total + diagonal_ref[plane] * near[plane]
                    moved = None
                    for reach in range(1, 5):
                        ahead, behind = near[plane + reach], near[plane - reach]
                        total = total + SECOND[reach] * (ahead + behind)
                        term = slopes[reach - 1] * (ahead - behind)
                        moved = term if moved is None else moved + term
                    partial_ref[part, plane] = total
                    drift_ref[part, plane] = moved
        outers = []
        for part in range(2):
            first = total_of_groups(bells[part] * y_ref[0], kinds)
            second = total_of_groups(inclines[part] * y_ref[0], kinds)
            third = total_of_groups(bells[part] * y_ref[1], kinds)
            outers.append((first * y_ref[2] + third * y_ref[4], second * y_ref[3]))
        for part in range(2):
            for start in range(0, width, block):
                spread = (
                    xbell_ref[start : start + block] * outers[part][0][None]
                    + xslope_ref[start : start + block] * outers[part][1][None]
                )
                where, high, low = split(part, start, spread)
                spread_ref[where, :LANES] = high
                spread_ref[where, LANES:] = low
        product_ref[:, :LANES] = jnp.dot(spread_ref[...], zy_ref[...], preferred_element_type=jnp.float32)
        for start in range(0, width, block):
            images = []
            for part in range(2):
                rows = pl.ds((part * width + start) * ROWS, slab)
                images.append(
                    partial_ref[part, start : start + block]
                    + product_ref[rows, :LANES].reshape(block, ROWS, LANES)
                )
            new = (
                -kinetic * images[1] - drift_ref[0, start : start + block],
                kinetic * images[0] - drift_ref[1, start : start + block],
            )
            for part in range(2):
                field_ref[part, start : start + block] = new[part]
                total_ref[part, start : start + block] += new[part]
                where, high, low = split(part, start, new[part])
                split_ref[where, :LANES] = high
                split_ref[where, LANES:] = low
        return carry

    lax.fori_loop(1, ORDER + 1, one_order, 0)


def sums_in_kernel(total_ref, width):
    flow = jnp.zeros((ROWS, LANES), jnp.float32)
    density = jnp.zeros((ROWS, LANES), jnp.float32)
    for plane in range(width):
        real = total_ref[0, plane]
        imaginary = total_ref[1, plane]
        moved = None
        for reach in range(1, 5):
            ahead = total_ref[1, (plane + reach) % width]
            behind = total_ref[1, (plane - reach) % width]
            term = FIRST[reach - 1] * (ahead - behind)
            moved = term if moved is None else moved + term
        flow = flow + real * moved
        density = density + (real * real + imaginary * imaginary)
    return (2.0 * SLOPE) * flow, density


def first_kernel(parts, kinds, scalar_ref, *refs):
    pieces, refs = refs[:parts], refs[parts:]
    potential_ref, *tables, sums_ref, total_ref, out_ref, field_ref = refs[:10]
    scratch = refs[10:]
    width = total_ref.shape[1]
    planes = width // parts
    for part in range(2):
        for number in range(parts):
            for index in range(planes):
                plane = pieces[number][part, pl.ds(index, ROWS, stride=planes), :]
                field_ref[part, number * planes + index] = plane
                total_ref[part, number * planes + index] = plane
    propagate_in_kernel(scalar_ref[0], field_ref, total_ref, potential_ref, tables, scratch, width, kinds)
    flow, density = sums_in_kernel(total_ref, width)
    out_ref[0] = sums_ref[0] + flow
    out_ref[1] = sums_ref[1] + density


def second_kernel(parts, kinds, points, scalar_ref, *refs):
    seen, refs = refs[:parts], refs[parts:]
    psi_ref, potential_ref, *tables, sums_ref = refs[:8]
    refs = refs[8:]
    pieces, refs = refs[:parts], refs[parts:]
    out_ref, vector_ref, field_ref, total_ref = refs[:4]
    scratch = refs[4:]
    width = total_ref.shape[1]
    planes = width // parts
    flow = jnp.sum(fold([ref[0] for ref in seen]))
    density = jnp.sum(fold([ref[1] for ref in seen]))
    current = (flow + scalar_ref[0] * density) * (1.0 / points)
    vector_value = scalar_ref[1] - source_weight * current
    vector_ref[0] = vector_value
    field_ref[...] = psi_ref[...]
    total_ref[...] = psi_ref[...]
    propagate_in_kernel(vector_value, field_ref, total_ref, potential_ref, tables, scratch, width, kinds)
    flow, density = sums_in_kernel(total_ref, width)
    out_ref[0] = sums_ref[0] + flow
    out_ref[1] = sums_ref[1] + density
    for part in range(2):
        for number in range(parts):
            for index in range(planes):
                pieces[number][part, pl.ds(index, ROWS, stride=planes), :] = total_ref[
                    part, number * planes + index
                ]


def vmem():
    return pl.BlockSpec(memory_space=pltpu.VMEM)


def smem():
    return pl.BlockSpec(memory_space=pltpu.SMEM)


def anywhere():
    return pl.BlockSpec(memory_space=pl.ANY)


def float_array(*shape):
    return jax.ShapeDtypeStruct(shape, jnp.float32)


def shifted(value, axis_name, count, shift):
    return lax.ppermute(value, axis_name, [((index + shift) % count, index) for index in range(count)])


def per_device(parts, blocks, orbitals, local_potential, atom_sites, host_point, fields):
    norb = orbitals.shape[2]
    planes, points = local_potential.shape
    width = planes * parts
    share = norb // parts
    owned = fields.shape[1]
    atoms = atom_sites.shape[0]
    kinds = 2 * atoms
    here = lax.axis_index("grid").astype(jnp.int32)[None]
    params = pltpu.CompilerParams(vmem_limit_bytes=LIMIT)

    def rows_of(value):
        lead = value.shape[:-2]
        value = value.reshape(*lead, planes, ROWS, LANES)
        return jnp.swapaxes(value, -3, -2).reshape(*lead, ROWS * planes, LANES)

    def planes_of(value):
        lead = value.shape[:-2]
        value = value.reshape(*lead, ROWS, planes, LANES)
        return jnp.swapaxes(value, -3, -2)

    field_blocks = [fields] + [shifted(fields, "macro", blocks, step) for step in range(1, blocks)]

    piece = float_array(2, ROWS * planes, LANES)
    packed = pl.pallas_call(
        functools.partial(pack_kernel, parts, share),
        out_shape=[piece] * (parts * share),
        in_specs=[smem(), anywhere()],
        out_specs=[anywhere()] * (parts * share),
        scratch_shapes=[pltpu.SemaphoreType.DMA((parts * share,))],
        compiler_params=params,
    )(here, rows_of(orbitals[0]))
    arrived = []
    potentials = [local_potential]
    for orbital in range(share):
        row = [packed[orbital]]
        for part in range(1, parts):
            row.append(shifted(packed[part * share + orbital], "grid", parts, -part % parts))
        arrived.append(row)
        if orbital == 0:
            for part in range(1, parts):
                potentials.append(shifted(local_potential, "grid", parts, part))
    arrived = [[row[0]] + row[:0:-1] for row in arrived]
    potential = jnp.concatenate(
        [value.reshape(planes, ROWS, LANES) for value in potentials], axis=0
    )

    tables = pl.pallas_call(
        functools.partial(tables_kernel, atoms, planes),
        out_shape=[
            jax.ShapeDtypeStruct((2 * LANES, 4 * LANES), jnp.bfloat16),
            jax.ShapeDtypeStruct((2 * LANES, LANES), jnp.bfloat16),
            float_array(width, ROWS, LANES),
            float_array(width, ROWS, LANES),
            float_array(5, ROWS, LANES),
        ],
        in_specs=[smem(), smem(), vmem()],
        out_specs=[vmem()] * 5,
        compiler_params=params,
    )(atom_sites, here, stencil_weights(width))

    block = lax.axis_index("macro").astype(jnp.int32)
    scalars = pl.pallas_call(
        functools.partial(vector_kernel, blocks),
        out_shape=float_array(2),
        in_specs=[smem()] + [vmem()] * blocks,
        out_specs=smem(),
        compiler_params=params,
    )(jnp.stack([host_point[0], block]), *field_blocks)

    scratch = [
        pltpu.VMEM((2 * width * ROWS, 2 * LANES), jnp.bfloat16),
        pltpu.VMEM((2 * width * ROWS, 4 * LANES), jnp.float32),
        pltpu.VMEM((2, width, ROWS, LANES), jnp.float32),
        pltpu.VMEM((2, width, ROWS, LANES), jnp.float32),
        pltpu.VMEM((2 * width * ROWS, 2 * LANES), jnp.bfloat16),
        pltpu.VMEM((width, ROWS, LANES), jnp.float32),
    ]
    cell = float_array(2, width, ROWS, LANES)
    cell_scratch = pltpu.VMEM((2, width, ROWS, LANES), jnp.float32)
    sums_shape = float_array(2, ROWS, LANES)
    cost = pl.CostEstimate(flops=3 * 2 * 512 * 256 * 256 * ORDER, bytes_accessed=2 * 1024 * 1024, transcendentals=0)

    sums = jnp.zeros((2, ROWS, LANES), jnp.float32)
    moved = []
    for orbital in range(share):
        psi, sums = pl.pallas_call(
            functools.partial(first_kernel, parts, kinds),
            out_shape=[cell, sums_shape],
            in_specs=[smem()] + [vmem()] * (parts + 7),
            out_specs=[vmem()] * 2,
            scratch_shapes=[cell_scratch] + scratch,
            compiler_params=params,
            cost_estimate=cost,
        )(scalars, *arrived[orbital], potential, *tables, sums)
        moved.append(psi)
    first_sums = sums
    seen = [first_sums] + [shifted(first_sums, "grid", parts, part) for part in range(1, parts)]

    sums = jnp.zeros((2, ROWS, LANES), jnp.float32)
    returned = [None] * (parts * share)
    for orbital in range(share):
        *pieces, sums, vector_value = pl.pallas_call(
            functools.partial(second_kernel, parts, kinds, float(width**3 * norb)),
            out_shape=[piece] * parts + [sums_shape, float_array(1)],
            in_specs=[smem()] + [vmem()] * (parts + 8),
            out_specs=[vmem()] * (parts + 1) + [smem()],
            scratch_shapes=[cell_scratch, cell_scratch] + scratch,
            compiler_params=params,
            cost_estimate=cost,
        )(scalars, *seen, moved[orbital], potential, *tables, sums)
        returned[orbital] = pieces[0]
        for part in range(1, parts):
            returned[part * share + orbital] = shifted(pieces[part], "grid", parts, -part % parts)
    second_sums = sums

    unpacked = pl.pallas_call(
        functools.partial(unpack_kernel, parts, share),
        out_shape=float_array(2, norb, ROWS * planes, LANES),
        in_specs=[smem()] + [anywhere()] * (parts * share),
        out_specs=anywhere(),
        scratch_shapes=[pltpu.SemaphoreType.DMA((parts * share,))],
        compiler_params=params,
    )(here, *returned)
    orbitals_out = planes_of(unpacked).reshape(2, norb, planes, points)

    length = blocks * owned
    positions = lax.broadcasted_iota(jnp.int32, (length,), 0)
    values = jnp.stack([scalars[0], vector_value[0]])
    flows = jnp.stack([jnp.sum(first_sums[0]), jnp.sum(second_sums[0])])
    densities = jnp.stack([jnp.sum(first_sums[1]), jnp.sum(second_sums[1])])
    currents = (flows + values * densities) / (width**3 * norb)
    sources = lax.psum(
        jnp.where(positions[None] == host_point[0], currents[:, None], 0.0), ("macro", "grid")
    )
    turned = jnp.concatenate(field_blocks, axis=1)
    start = block * owned
    whole = lax.dynamic_slice_in_dim(
        jnp.concatenate([turned, turned], axis=1), length - start, length, axis=1
    )
    previous, present = whole[0], whole[1]
    for step in range(STEPS):
        rim = jnp.pad(present, 1)
        following = (
            2.0 * present
            - previous
            + courant_square * (rim[2:] - 2.0 * present + rim[:-2])
            - source_weight * sources[step]
        )
        previous, present = present, following
    fields_out = lax.dynamic_slice_in_dim(jnp.stack([previous, present]), start, owned, axis=1)
    return orbitals_out[None], fields_out


def solution(mesh):
    in_specs = (
        P("macro", None, None, "grid", None),
        P("grid", None),
        P(),
        P("macro"),
        P(None, "macro"),
    )
    out_specs = (P("macro", None, None, "grid", None), P(None, "macro"))
    return jax.shard_map(
        functools.partial(per_device, mesh.shape["grid"], mesh.shape["macro"]),
        mesh=mesh,
        in_specs=in_specs,
        out_specs=out_specs,
        check_vma=False,
    )
```

```python
import functools

import jax
import jax.numpy as jnp
import numpy as np
from jax import lax
from jax.experimental import pallas as pl
from jax.experimental.pallas import tpu as pltpu
from jax.sharding import PartitionSpec as P

ORDER = 4
STEPS = 2
spacing = 0.3206
time_step = 0.02
courant_square = 0.81
source_weight = 0.1
radial_strength = 0.3
polar_strength = -0.2
projector_width = 2.5

SECOND = (-14350.0, 8064.0, -1008.0, 128.0, -9.0)
FIRST = (672.0, -168.0, 32.0, -3.0)
KINETIC = 1.0 / (2.0 * 5040.0 * spacing * spacing)
SLOPE = 1.0 / (840.0 * spacing)

LANES = 128
ROWS = 8
LIMIT = 24 * 1024 * 1024


def stencil_weights(width):
    group = LANES // width
    total = np.zeros((LANES, 3 * LANES), np.float32)
    for y_in in range(group):
        for z_in in range(width):
            for y_out in range(group):
                for part, step in enumerate((0, group, -group)):
                    reach = abs(step + y_in - y_out)
                    if 1 <= reach <= 4:
                        total[y_in * width + z_in, part * LANES + y_out * width + z_in] += SECOND[reach]
            for reach in range(1, 5):
                for z_out in ((z_in + reach) % width, (z_in - reach) % width):
                    total[y_in * width + z_in, y_in * width + z_out] += SECOND[reach]
    return jnp.asarray(np.concatenate([total, total], axis=0), jnp.bfloat16)


def periodic(distance, width):
    return ((distance + width // 2) & (width - 1)) - width // 2


def bell_of(offset):
    distance = offset.astype(jnp.float32)
    bell = jnp.exp(-0.5 * distance * distance / (projector_width * projector_width))
    return bell, distance / projector_width * bell


def tables_kernel(atoms, site_ref, stencil_ref, near_ref, far_ref, zy_ref, xbell_ref, xslope_ref, y_ref):
    width = xbell_ref.shape[0]
    kinds = 2 * atoms
    group = LANES // width

    def site_of(column, axis_number):
        atom = (column % kinds) // 2
        position = jnp.zeros(column.shape, jnp.int32)
        for number in range(atoms):
            position = jnp.where(atom == number, site_ref[number, axis_number], position)
        return position

    def factor(coordinate, column):
        bell, slope = bell_of(periodic(coordinate - site_of(column, 2), width))
        value = jnp.where(column % 2 == 0, bell, slope)
        high = value.astype(jnp.bfloat16).astype(jnp.float32)
        return jnp.where(column % LANES < LANES // 2, high, value - high)

    def groups_agree(point, column):
        return (point % LANES) // width == (column // kinds) % group

    shape = (2 * LANES, LANES)
    first = lax.broadcasted_iota(jnp.int32, shape, 0)
    last = lax.broadcasted_iota(jnp.int32, shape, 1)
    near_ref[:, :LANES] = stencil_ref[:, :LANES]
    far_ref[...] = stencil_ref[:, LANES:]
    inward = jnp.where(groups_agree(first, last), factor(first % width, last), 0.0)
    near_ref[:, LANES:] = inward.astype(jnp.bfloat16)
    outward = jnp.where(groups_agree(last, first), factor(last % width, first), 0.0)
    zy_ref[...] = outward.astype(jnp.bfloat16)

    shape = (width, ROWS, LANES)
    plane = lax.broadcasted_iota(jnp.int32, shape, 0)
    column = lax.broadcasted_iota(jnp.int32, shape, 2)
    bell, slope = bell_of(periodic(plane - site_of(column, 0), width))
    xbell_ref[...] = bell
    xslope_ref[...] = slope

    shape = (ROWS, LANES)
    column = lax.broadcasted_iota(jnp.int32, shape, 1)
    row = lax.broadcasted_iota(jnp.int32, shape, 0) * group + (column // kinds) % group
    bell, slope = bell_of(periodic(row - site_of(column, 1), width))
    scale = -1.0 / KINETIC
    even = column % 2 == 0
    y_ref[0] = bell
    y_ref[1] = slope
    y_ref[2] = bell * jnp.where(even, scale * radial_strength, scale * polar_strength)
    y_ref[3] = bell * jnp.where(even, scale * polar_strength, 0.0)
    y_ref[4] = slope * jnp.where(even, scale * polar_strength, 0.0)


def vector_kernel(host_ref, seen_ref, out_ref):
    blocks, _, owned = seen_ref.shape
    host = host_ref[0]
    position = lax.broadcasted_iota(jnp.int32, (blocks, owned), 0) * owned + lax.broadcasted_iota(
        jnp.int32, (blocks, owned), 1
    )
    before, now = seen_ref[:, 0, :], seen_ref[:, 1, :]
    present = jnp.sum(jnp.where(position == host, now, 0.0))
    previous = jnp.sum(jnp.where(position == host, before, 0.0))
    beside = jnp.sum(jnp.where((position == host - 1) | (position == host + 1), now, 0.0))
    out_ref[0] = present
    out_ref[1] = 2.0 * present - previous + courant_square * (beside - 2.0 * present)


def pack_kernel(parts, share, count, first, with_potential, source_ref, *refs):
    out_ref, sems = refs[-2:]
    copies = []
    for owner in range(parts):
        for part in range(2):
            copies.append(
                (source_ref.at[part, pl.ds(owner * share + first, count)], out_ref.at[owner, pl.ds(part * count, count)])
            )
        if with_potential:
            copies.append((refs[0], out_ref.at[owner, 2 * count]))
    copies = [
        pltpu.make_async_copy(source, target, sems.at[number]) for number, (source, target) in enumerate(copies)
    ]
    for copy in copies:
        copy.start()
    for copy in copies:
        copy.wait()


def unpack_kernel(parts, share, count, first, piece_ref, *refs):
    out_ref, sems = refs[-2:]
    copies = []
    for owner in range(parts):
        for part in range(2):
            copies.append(
                pltpu.make_async_copy(
                    piece_ref.at[owner, pl.ds(part * count, count)],
                    out_ref.at[part, pl.ds(owner * share + first, count)],
                    sems.at[2 * owner + part],
                )
            )
    for copy in copies:
        copy.start()
    for copy in copies:
        copy.wait()


def total_of_groups(value, kinds):
    for shift in (4, 2, 1):
        value = value + pltpu.roll(value, shift, 0)
    shift = LANES // 2
    while shift >= kinds:
        value = value + pltpu.roll(value, shift, 1)
        shift //= 2
    return value


def propagate_in_kernel(
    count, vector_value, field_ref, total_ref, potential_ref, tables, scratch, width, kinds
):
    near_ref, far_ref, zy_ref, xbell_ref, xslope_ref, y_ref = tables
    split_ref, first_ref, second_ref, partial_ref, drift_ref, spread_ref, diagonal_ref = scratch
    diagonal_ref[...] = (3.0 * SECOND[0] - 0.5 * vector_value * vector_value / KINETIC) - potential_ref[
        ...
    ] * (1.0 / KINETIC)
    block = ROWS
    slab = block * ROWS
    cell_rows = width * ROWS
    numbers = [(orbital, part, part * count + orbital) for orbital in range(count) for part in range(2)]

    def split(planes):
        rows = planes.reshape(slab, LANES)
        high = rows.astype(jnp.bfloat16)
        low = (rows - high.astype(jnp.float32)).astype(jnp.bfloat16)
        return high, low

    def store_split(ref, number, start, planes):
        rows = pl.ds(number * cell_rows + start * ROWS, slab)
        high, low = split(planes)
        ref[rows, :LANES] = high
        ref[rows, LANES:] = low

    for number in range(2 * count):
        for start in range(0, width, block):
            store_split(split_ref, number, start, field_ref[number, start : start + block])

    def one_order(order, carry):
        inverse = jnp.where(order == 1, 1.0, jnp.where(order == 2, 0.5, jnp.where(order == 3, 1.0 / 3.0, 0.25)))
        step_scale = inverse * time_step
        kinetic = step_scale * KINETIC
        drift = step_scale * SLOPE * vector_value
        slopes = [drift * weight for weight in FIRST]
        outers = {}
        for orbital in range(count):
            for part in range(2):
                number = part * count + orbital
                rows = pl.ds(number * cell_rows, cell_rows)
                first_ref[rows, :] = jnp.dot(
                    split_ref[rows, :], near_ref[...], preferred_element_type=jnp.float32
                )
                bells = [jnp.zeros((ROWS, LANES), jnp.float32) for _ in range(2)]
                inclines = [jnp.zeros((ROWS, LANES), jnp.float32) for _ in range(2)]
                for plane in range(width):
                    inner = first_ref[pl.ds(number * cell_rows + plane * ROWS, ROWS), LANES:]
                    turn = plane % 2
                    bells[turn] = bells[turn] + inner * xbell_ref[plane]
                    inclines[turn] = inclines[turn] + inner * xslope_ref[plane]
                bell = bells[0] + bells[1]
                incline = inclines[0] + inclines[1]
                first = total_of_groups(bell * y_ref[0], kinds)
                second = total_of_groups(incline * y_ref[0], kinds)
                third = total_of_groups(bell * y_ref[1], kinds)
                outers[number] = (first * y_ref[2] + third * y_ref[4], second * y_ref[3])
        for orbital in range(count):
            for part in range(2):
                number = part * count + orbital
                rows = pl.ds(number * cell_rows, cell_rows)
                second_ref[rows, :] = jnp.dot(
                    split_ref[rows, :], far_ref[...], preferred_element_type=jnp.float32
                )
                for start in range(0, width, block):
                    near = {
                        plane: field_ref[number, plane % width] for plane in range(start - 4, start + block + 4)
                    }
                    for plane in range(start, start + block):
                        line = pl.ds(number * cell_rows + plane * ROWS, ROWS)
                        total = first_ref[line, :LANES]
                        total = total + pltpu.roll(second_ref[line, :LANES], ROWS - 1, 0)
                        total = total + pltpu.roll(second_ref[line, LANES:], 1, 0)
                        total = total + diagonal_ref[plane] * near[plane]
                        moved = None
                        for reach in range(1, 5):
                            ahead, behind = near[plane + reach], near[plane - reach]
                            total = total + SECOND[reach] * (ahead + behind)
                            term = slopes[reach - 1] * (ahead - behind)
                            moved = term if moved is None else moved + term
                        partial_ref[number, plane] = total
                        drift_ref[number, plane] = moved
        for orbital in range(count):
            for part in range(2):
                number = part * count + orbital
                rows = pl.ds(number * cell_rows, cell_rows)
                for start in range(0, width, block):
                    spread = (
                        xbell_ref[start : start + block] * outers[number][0][None]
                        + xslope_ref[start : start + block] * outers[number][1][None]
                    )
                    store_split(spread_ref, number, start, spread)
                first_ref[rows, :LANES] = jnp.dot(
                    spread_ref[rows, :], zy_ref[...], preferred_element_type=jnp.float32
                )
            real, imaginary = orbital, count + orbital
            for start in range(0, width, block):
                images = []
                for number in (real, imaginary):
                    rows = pl.ds(number * cell_rows + start * ROWS, slab)
                    images.append(
                        partial_ref[number, start : start + block]
                        + first_ref[rows, :LANES].reshape(block, ROWS, LANES)
                    )
                new = (
                    -kinetic * images[1] - drift_ref[real, start : start + block],
                    kinetic * images[0] - drift_ref[imaginary, start : start + block],
                )
                for number, value in zip((real, imaginary), new):
                    field_ref[number, start : start + block] = value
                    total_ref[number, start : start + block] += value
                    store_split(split_ref, number, start, value)
        return carry

    lax.fori_loop(1, ORDER + 1, one_order, 0)


def sums_in_kernel(count, total_ref, width):
    flow = jnp.zeros((ROWS, LANES), jnp.float32)
    density = jnp.zeros((ROWS, LANES), jnp.float32)
    for orbital in range(count):
        for plane in range(width):
            real = total_ref[orbital, plane]
            imaginary = total_ref[count + orbital, plane]
            moved = None
            for reach in range(1, 5):
                ahead = total_ref[count + orbital, (plane + reach) % width]
                behind = total_ref[count + orbital, (plane - reach) % width]
                term = FIRST[reach - 1] * (ahead - behind)
                moved = term if moved is None else moved + term
            flow = flow + real * moved
            density = density + (real * real + imaginary * imaginary)
    return (2.0 * SLOPE) * flow, density


def first_kernel(parts, count, kinds, copies, scalar_ref, piece_ref, *refs):
    opening = piece_ref.shape[1] > 2 * count
    if opening:
        *tables, total_ref, out_ref, potential_ref, field_ref = refs[:10]
        scratch = refs[10:]
    else:
        potential_ref, *tables, sums_ref, total_ref, out_ref, field_ref = refs[:11]
        scratch = refs[11:]
    width = total_ref.shape[1]
    planes = width // parts
    for owner in range(parts):
        for index in range(planes):
            rows = pl.ds(index, ROWS, stride=planes)
            plane = owner * planes + index
            for number in range(2 * count):
                value = piece_ref[owner, number, rows, :]
                field_ref[number, plane] = value
                total_ref[number, plane] = value
            if opening:
                potential_ref[plane] = piece_ref[owner, 2 * count, rows, :]
    propagate_in_kernel(
        count, scalar_ref[0], field_ref, total_ref, potential_ref, tables, scratch, width, kinds
    )
    flow, density = sums_in_kernel(count, total_ref, width)
    if not opening:
        flow, density = sums_ref[0, 0] + flow, sums_ref[0, 1] + density
    for copy in range(copies):
        out_ref[copy, 0] = flow
        out_ref[copy, 1] = density


def second_kernel(parts, count, kinds, points, copies, scalar_ref, seen_ref, *refs):
    psi_ref, potential_ref, *tables, sums_ref, piece_ref, out_ref, field_ref, total_ref = refs[:13]
    scratch = refs[13:]
    width = total_ref.shape[1]
    planes = width // parts
    seen = [seen_ref[owner] for owner in range(parts)]
    seen = functools.reduce(lambda left, right: left + right, seen)
    current = (jnp.sum(seen[0]) + scalar_ref[0] * jnp.sum(seen[1])) * (1.0 / points)
    vector_value = scalar_ref[1] - source_weight * current
    field_ref[...] = psi_ref[...]
    total_ref[...] = psi_ref[...]
    propagate_in_kernel(
        count, vector_value, field_ref, total_ref, potential_ref, tables, scratch, width, kinds
    )
    flow, density = sums_in_kernel(count, total_ref, width)
    flow, density = sums_ref[0, 0] + flow, sums_ref[0, 1] + density
    if copies == 1:
        out_ref[0, 0] = flow
        out_ref[0, 1] = density
    else:
        row = lax.broadcasted_iota(jnp.int32, (ROWS, LANES), 0)
        own = sums_ref[1, 0] + scalar_ref[0] * sums_ref[1, 1]
        following = flow + vector_value * density
        message = jnp.where(
            row == 0,
            jnp.sum(own, axis=0, keepdims=True) * (1.0 / points),
            jnp.where(row == 1, jnp.sum(following, axis=0, keepdims=True) * (1.0 / points), scalar_ref[2]),
        )
        for copy in range(copies):
            out_ref[copy] = message
    for owner in range(parts):
        for number in range(2 * count):
            for index in range(planes):
                piece_ref[owner, number, pl.ds(index, ROWS, stride=planes), :] = total_ref[
                    number, owner * planes + index
                ]


def vmem():
    return pl.BlockSpec(memory_space=pltpu.VMEM)


def smem():
    return pl.BlockSpec(memory_space=pltpu.SMEM)


def anywhere():
    return pl.BlockSpec(memory_space=pl.ANY)


def float_array(*shape):
    return jax.ShapeDtypeStruct(shape, jnp.float32)


def exchanged(value, axes):
    return lax.all_to_all(value, axes, split_axis=0, concat_axis=0, tiled=True)


def per_device(parts, blocks, orbitals, local_potential, atom_sites, host_point, fields):
    norb = orbitals.shape[2]
    planes, points = local_potential.shape
    width = planes * parts
    share = norb // parts
    count = min(2, share)
    chunks = share // count
    owned = fields.shape[1]
    atoms = atom_sites.shape[0]
    kinds = 2 * atoms
    held = ROWS * planes
    total_points = float(width**3 * norb)
    params = pltpu.CompilerParams(vmem_limit_bytes=LIMIT)

    def rows_of(value):
        lead = value.shape[:-2]
        value = value.reshape(*lead, planes, ROWS, LANES)
        return jnp.swapaxes(value, -3, -2).reshape(*lead, held, LANES)

    def planes_of(value):
        lead = value.shape[:-2]
        value = value.reshape(*lead, ROWS, planes, LANES)
        return jnp.swapaxes(value, -3, -2)

    source = rows_of(orbitals[0])
    arrived = []
    for chunk in range(chunks):
        extra = [rows_of(local_potential)] if chunk == 0 else []
        packed = pl.pallas_call(
            functools.partial(pack_kernel, parts, share, count, chunk * count, chunk == 0),
            out_shape=float_array(parts, 2 * count + len(extra), held, LANES),
            in_specs=[anywhere()] * (1 + len(extra)),
            out_specs=anywhere(),
            scratch_shapes=[pltpu.SemaphoreType.DMA((parts * (2 + len(extra)),))],
            compiler_params=params,
        )(source, *extra)
        arrived.append(exchanged(packed, "grid"))
        if chunk == 0:
            seen_fields = exchanged(jnp.broadcast_to(fields[None], (blocks, 2, owned)), "macro")

    tables = pl.pallas_call(
        functools.partial(tables_kernel, atoms),
        out_shape=[
            jax.ShapeDtypeStruct((2 * LANES, 2 * LANES), jnp.bfloat16),
            jax.ShapeDtypeStruct((2 * LANES, 2 * LANES), jnp.bfloat16),
            jax.ShapeDtypeStruct((2 * LANES, LANES), jnp.bfloat16),
            float_array(width, ROWS, LANES),
            float_array(width, ROWS, LANES),
            float_array(5, ROWS, LANES),
        ],
        in_specs=[smem(), vmem()],
        out_specs=[vmem()] * 6,
        compiler_params=params,
    )(atom_sites, stencil_weights(width))

    near_scalars = pl.pallas_call(
        vector_kernel,
        out_shape=float_array(2),
        in_specs=[smem(), vmem()],
        out_specs=smem(),
        compiler_params=params,
    )(host_point, seen_fields)
    scalars = jnp.concatenate([near_scalars, host_point.astype(jnp.float32)])

    rows = 2 * count * width * ROWS
    cell_scratch = pltpu.VMEM((2 * count, width, ROWS, LANES), jnp.float32)
    scratch = [
        pltpu.VMEM((rows, 2 * LANES), jnp.bfloat16),
        pltpu.VMEM((rows, 2 * LANES), jnp.float32),
        pltpu.VMEM((rows, 2 * LANES), jnp.float32),
        cell_scratch,
        cell_scratch,
        pltpu.VMEM((rows, 2 * LANES), jnp.bfloat16),
        pltpu.VMEM((width, ROWS, LANES), jnp.float32),
    ]
    cell = float_array(2 * count, width, ROWS, LANES)
    cost = pl.CostEstimate(
        flops=count * 3 * 2 * 512 * 256 * 256 * ORDER, bytes_accessed=4 * 1024 * 1024, transcendentals=0
    )

    potential, sums = None, None
    moved = []
    for chunk in range(chunks):
        copies = parts if chunk == chunks - 1 else 1
        inputs = [scalars, arrived[chunk]]
        outputs = [cell, float_array(copies, 2, ROWS, LANES)]
        if chunk == 0:
            inputs += list(tables)
            outputs += [float_array(width, ROWS, LANES)]
        else:
            inputs += [potential, *tables, sums]
        psi, sums, *rest = pl.pallas_call(
            functools.partial(first_kernel, parts, count, kinds, copies),
            out_shape=outputs,
            in_specs=[smem()] + [vmem()] * (len(inputs) - 1),
            out_specs=[vmem()] * len(outputs),
            scratch_shapes=[cell_scratch] + scratch,
            compiler_params=params,
            cost_estimate=cost,
        )(*inputs)
        if chunk == 0:
            potential = rest[0]
        moved.append(psi)
    own_sums = sums[:1]
    seen = exchanged(sums, "grid")

    sums = jnp.concatenate([jnp.zeros_like(own_sums), own_sums])
    result = None
    for chunk in range(chunks):
        last = chunk == chunks - 1
        copies = blocks * parts if last else 1
        if last and chunks > 1:
            sums = jnp.concatenate([sums, own_sums])
        pieces, sums = pl.pallas_call(
            functools.partial(second_kernel, parts, count, kinds, total_points, copies),
            out_shape=[
                float_array(parts, 2 * count, held, LANES),
                float_array(copies, ROWS, LANES) if last else float_array(1, 2, ROWS, LANES),
            ],
            in_specs=[smem()] + [vmem()] * 10,
            out_specs=[vmem()] * 2,
            scratch_shapes=[cell_scratch, cell_scratch] + scratch,
            compiler_params=params,
            cost_estimate=cost,
        )(scalars, seen, moved[chunk], potential, *tables, sums)
        returned = exchanged(pieces, "grid")
        result = pl.pallas_call(
            functools.partial(unpack_kernel, parts, share, count, chunk * count),
            out_shape=float_array(2, norb, held, LANES),
            in_specs=[anywhere()] * (1 if chunk == 0 else 2),
            out_specs=anywhere(),
            scratch_shapes=[pltpu.SemaphoreType.DMA((2 * parts,))],
            input_output_aliases={} if chunk == 0 else {1: 0},
            compiler_params=params,
        )(*([returned] if chunk == 0 else [returned, result]))
    orbitals_out = planes_of(result).reshape(2, norb, planes, points)

    messages = exchanged(sums, ("macro", "grid")).reshape(blocks, parts, ROWS, LANES)
    currents = jnp.sum(messages[:, :, :2], axis=(1, 3))
    hosts = messages[:, 0, 2, 0].astype(jnp.int32)
    length = blocks * owned
    positions = lax.broadcasted_iota(jnp.int32, (length,), 0)
    sources = jnp.sum(
        jnp.where(positions[None, None] == hosts[:, None, None], currents[:, :, None], 0.0), axis=0
    )
    whole = jnp.swapaxes(seen_fields, 0, 1).reshape(2, length)
    previous, present = whole[0], whole[1]
    for step in range(STEPS):
        rim = jnp.pad(present, 1)
        following = (
            2.0 * present
            - previous
            + courant_square * (rim[2:] - 2.0 * present + rim[:-2])
            - source_weight * sources[step]
        )
        previous, present = present, following
    start = lax.axis_index("macro") * owned
    fields_out = lax.dynamic_slice_in_dim(jnp.stack([previous, present]), start, owned, axis=1)
    return orbitals_out[None], fields_out


def solution(mesh):
    in_specs = (
        P("macro", None, None, "grid", None),
        P("grid", None),
        P(),
        P("macro"),
        P(None, "macro"),
    )
    out_specs = (P("macro", None, None, "grid", None), P(None, "macro"))
    return jax.shard_map(
        functools.partial(per_device, mesh.shape["grid"], mesh.shape["macro"]),
        mesh=mesh,
        in_specs=in_specs,
        out_specs=out_specs,
        check_vma=False,
    )
```

```python
import functools

import jax
import jax.numpy as jnp
import numpy as np
from jax import lax
from jax.experimental import pallas as pl
from jax.experimental.pallas import tpu as pltpu
from jax.sharding import PartitionSpec as P

ORDER = 4
STEPS = 2
spacing = 0.3206
time_step = 0.02
courant_square = 0.81
source_weight = 0.1
radial_strength = 0.3
polar_strength = -0.2
projector_width = 2.5

SECOND = (-14350.0, 8064.0, -1008.0, 128.0, -9.0)
FIRST = (672.0, -168.0, 32.0, -3.0)
KINETIC = 1.0 / (2.0 * 5040.0 * spacing * spacing)
SLOPE = 1.0 / (840.0 * spacing)

LANES = 128
ROWS = 8
LIMIT = 24 * 1024 * 1024


def stencil_weights(width):
    group = LANES // width
    total = np.zeros((LANES, 3 * LANES), np.float32)
    for y_in in range(group):
        for z_in in range(width):
            for y_out in range(group):
                for part, step in enumerate((0, group, -group)):
                    reach = abs(step + y_in - y_out)
                    if 1 <= reach <= 4:
                        total[y_in * width + z_in, part * LANES + y_out * width + z_in] += SECOND[reach]
            for reach in range(1, 5):
                for z_out in ((z_in + reach) % width, (z_in - reach) % width):
                    total[y_in * width + z_in, y_in * width + z_out] += SECOND[reach]
    return jnp.asarray(np.concatenate([total, total], axis=0), jnp.bfloat16)


def periodic(distance, width):
    return ((distance + width // 2) & (width - 1)) - width // 2


def bell_of(offset):
    distance = offset.astype(jnp.float32)
    bell = jnp.exp(-0.5 * distance * distance / (projector_width * projector_width))
    return bell, distance / projector_width * bell


def tables_kernel(atoms, site_ref, stencil_ref, near_ref, far_ref, zy_ref, xbell_ref, xslope_ref, y_ref):
    width = xbell_ref.shape[0]
    kinds = 2 * atoms
    group = LANES // width

    def site_of(column, axis_number):
        atom = (column % kinds) // 2
        position = jnp.zeros(column.shape, jnp.int32)
        for number in range(atoms):
            position = jnp.where(atom == number, site_ref[number, axis_number], position)
        return position

    def factor(coordinate, column):
        bell, slope = bell_of(periodic(coordinate - site_of(column, 2), width))
        value = jnp.where(column % 2 == 0, bell, slope)
        high = value.astype(jnp.bfloat16).astype(jnp.float32)
        return jnp.where(column % LANES < LANES // 2, high, value - high)

    def groups_agree(point, column):
        return (point % LANES) // width == (column // kinds) % group

    shape = (2 * LANES, LANES)
    first = lax.broadcasted_iota(jnp.int32, shape, 0)
    last = lax.broadcasted_iota(jnp.int32, shape, 1)
    near_ref[:, :LANES] = stencil_ref[:, :LANES]
    far_ref[...] = stencil_ref[:, LANES:]
    inward = jnp.where(groups_agree(first, last), factor(first % width, last), 0.0)
    near_ref[:, LANES:] = inward.astype(jnp.bfloat16)
    outward = jnp.where(groups_agree(last, first), factor(last % width, first), 0.0)
    zy_ref[...] = outward.astype(jnp.bfloat16)

    shape = (width, ROWS, LANES)
    plane = lax.broadcasted_iota(jnp.int32, shape, 0)
    column = lax.broadcasted_iota(jnp.int32, shape, 2)
    bell, slope = bell_of(periodic(plane - site_of(column, 0), width))
    xbell_ref[...] = bell
    xslope_ref[...] = slope

    shape = (ROWS, LANES)
    column = lax.broadcasted_iota(jnp.int32, shape, 1)
    row = lax.broadcasted_iota(jnp.int32, shape, 0) * group + (column // kinds) % group
    bell, slope = bell_of(periodic(row - site_of(column, 1), width))
    scale = -1.0 / KINETIC
    even = column % 2 == 0
    y_ref[0] = bell
    y_ref[1] = slope
    y_ref[2] = bell * jnp.where(even, scale * radial_strength, scale * polar_strength)
    y_ref[3] = bell * jnp.where(even, scale * polar_strength, 0.0)
    y_ref[4] = slope * jnp.where(even, scale * polar_strength, 0.0)


def vector_kernel(blocks, host_ref, here_ref, *refs):
    out_ref = refs[blocks]
    owned = refs[0].shape[1]
    host = host_ref[0]
    place = lax.broadcasted_iota(jnp.int32, (1, owned), 1)
    present = jnp.zeros((1, owned), jnp.float32)
    previous, beside = present, present
    for number in range(blocks):
        position = place + lax.rem(here_ref[0] + number, blocks) * owned
        before, now = refs[number][0:1, :], refs[number][1:2, :]
        present = present + jnp.where(position == host, now, 0.0)
        previous = previous + jnp.where(position == host, before, 0.0)
        beside = beside + jnp.where((position == host - 1) | (position == host + 1), now, 0.0)
    present = jnp.sum(present)
    out_ref[0] = present
    out_ref[1] = 2.0 * present - jnp.sum(previous) + courant_square * (jnp.sum(beside) - 2.0 * present)
    out_ref[2] = host.astype(jnp.float32)


def run_copies(pairs, sems):
    copies = [
        pltpu.make_async_copy(source, target, sems.at[number]) for number, (source, target) in enumerate(pairs)
    ]
    for copy in copies:
        copy.start()
    for copy in copies:
        copy.wait()


def pack_kernel(parts, share, count, first, source_ref, potential_ref, out_ref, sems):
    pairs = []
    for owner in range(parts):
        pairs.append((potential_ref, out_ref.at[owner, 2 * count]))
        for part in range(2):
            source = source_ref.at[part, pl.ds(owner * share + first, count)]
            pairs.append((source, out_ref.at[owner, pl.ds(part * count, count)]))
    run_copies(pairs, sems)


def pack_pieces_kernel(parts, share, count, first, here_ref, source_ref, *refs):
    pairs = []
    for step in range(parts):
        owner = lax.rem(here_ref[0] + step, parts)
        for part in range(2):
            source = source_ref.at[part, pl.ds(owner * share + first, count)]
            pairs.append((source, refs[step].at[pl.ds(part * count, count)]))
    run_copies(pairs, refs[parts])


def unpack_kernel(parts, share, count, first, piece_ref, *refs):
    out_ref, sems = refs[-2:]
    pairs = []
    for owner in range(parts):
        for part in range(2):
            target = out_ref.at[part, pl.ds(owner * share + first, count)]
            pairs.append((piece_ref.at[owner, pl.ds(part * count, count)], target))
    run_copies(pairs, sems)


def unpack_pieces_kernel(parts, share, count, first, here_ref, *refs):
    out_ref, sems = refs[parts:]
    pairs = []
    for step in range(parts):
        owner = lax.rem(here_ref[0] + parts - step, parts)
        for part in range(2):
            target = out_ref.at[part, pl.ds(owner * share + first, count)]
            pairs.append((refs[step].at[pl.ds(part * count, count)], target))
    run_copies(pairs, sems)


def fold(values):
    while len(values) > 1:
        half = len(values) // 2
        values = [values[number] + values[number + half] for number in range(half)]
    return values[0]


def total_of_groups(value, kinds):
    for shift in (4, 2, 1):
        value = value + pltpu.roll(value, shift, 0)
    shift = LANES // 2
    while shift >= kinds:
        value = value + pltpu.roll(value, shift, 1)
        shift //= 2
    return value


def propagate_in_kernel(
    count, vector_value, field_ref, total_ref, potential_ref, tables, scratch, width, kinds
):
    near_ref, far_ref, zy_ref, xbell_ref, xslope_ref, y_ref = tables
    split_ref, first_ref, second_ref, partial_ref, drift_ref, spread_ref, diagonal_ref = scratch
    diagonal_ref[...] = (3.0 * SECOND[0] - 0.5 * vector_value * vector_value / KINETIC) - potential_ref[
        ...
    ] * (1.0 / KINETIC)
    block = ROWS
    slab = block * ROWS
    cell_rows = width * ROWS

    def split(planes):
        rows = planes.reshape(slab, LANES)
        high = rows.astype(jnp.bfloat16)
        low = (rows - high.astype(jnp.float32)).astype(jnp.bfloat16)
        return high, low

    def store_split(ref, number, start, planes):
        rows = pl.ds(number * cell_rows + start * ROWS, slab)
        high, low = split(planes)
        ref[rows, :LANES] = high
        ref[rows, LANES:] = low

    for number in range(2 * count):
        for start in range(0, width, block):
            store_split(split_ref, number, start, field_ref[number, start : start + block])

    def one_order(order, carry):
        inverse = jnp.where(order == 1, 1.0, jnp.where(order == 2, 0.5, jnp.where(order == 3, 1.0 / 3.0, 0.25)))
        step_scale = inverse * time_step
        kinetic = step_scale * KINETIC
        drift = step_scale * SLOPE * vector_value
        slopes = [drift * weight for weight in FIRST]
        outers = {}
        for orbital in range(count):
            rows = pl.ds(2 * orbital * cell_rows, 2 * cell_rows)
            first_ref[rows, :] = jnp.dot(split_ref[rows, :], near_ref[...], preferred_element_type=jnp.float32)
            for number in (2 * orbital, 2 * orbital + 1):
                bells = [jnp.zeros((ROWS, LANES), jnp.float32) for _ in range(2)]
                inclines = [jnp.zeros((ROWS, LANES), jnp.float32) for _ in range(2)]
                for plane in range(width):
                    inner = first_ref[pl.ds(number * cell_rows + plane * ROWS, ROWS), LANES:]
                    turn = plane % 2
                    bells[turn] = bells[turn] + inner * xbell_ref[plane]
                    inclines[turn] = inclines[turn] + inner * xslope_ref[plane]
                bell = bells[0] + bells[1]
                incline = inclines[0] + inclines[1]
                first = total_of_groups(bell * y_ref[0], kinds)
                second = total_of_groups(incline * y_ref[0], kinds)
                third = total_of_groups(bell * y_ref[1], kinds)
                outers[number] = (first * y_ref[2] + third * y_ref[4], second * y_ref[3])
        for orbital in range(count):
            rows = pl.ds(2 * orbital * cell_rows, 2 * cell_rows)
            second_ref[rows, :] = jnp.dot(split_ref[rows, :], far_ref[...], preferred_element_type=jnp.float32)
            for start in range(0, width, block):
                for number in (2 * orbital, 2 * orbital + 1):
                    near = {
                        plane: field_ref[number, plane % width] for plane in range(start - 4, start + block + 4)
                    }
                    for plane in range(start, start + block):
                        line = pl.ds(number * cell_rows + plane * ROWS, ROWS)
                        total = first_ref[line, :LANES]
                        total = total + pltpu.roll(second_ref[line, :LANES], ROWS - 1, 0)
                        total = total + pltpu.roll(second_ref[line, LANES:], 1, 0)
                        total = total + diagonal_ref[plane] * near[plane]
                        moved = None
                        for reach in range(1, 5):
                            ahead, behind = near[plane + reach], near[plane - reach]
                            total = total + SECOND[reach] * (ahead + behind)
                            term = slopes[reach - 1] * (ahead - behind)
                            moved = term if moved is None else moved + term
                        partial_ref[number, plane] = total
                        drift_ref[number, plane] = moved
        for orbital in range(count):
            real, imaginary = 2 * orbital, 2 * orbital + 1
            for start in range(0, width, block):
                xbell = xbell_ref[start : start + block]
                xslope = xslope_ref[start : start + block]
                for number in (real, imaginary):
                    spread = xbell * outers[number][0][None] + xslope * outers[number][1][None]
                    store_split(spread_ref, number, start, spread)
            rows = pl.ds(real * cell_rows, 2 * cell_rows)
            first_ref[rows, :LANES] = jnp.dot(
                spread_ref[rows, :], zy_ref[...], preferred_element_type=jnp.float32
            )
            for start in range(0, width, block):
                images = []
                for number in (real, imaginary):
                    rows = pl.ds(number * cell_rows + start * ROWS, slab)
                    images.append(
                        partial_ref[number, start : start + block]
                        + first_ref[rows, :LANES].reshape(block, ROWS, LANES)
                    )
                new = (
                    -kinetic * images[1] - drift_ref[real, start : start + block],
                    kinetic * images[0] - drift_ref[imaginary, start : start + block],
                )
                for number, value in zip((real, imaginary), new):
                    field_ref[number, start : start + block] = value
                    total_ref[number, start : start + block] += value
                    store_split(split_ref, number, start, value)
        return carry

    lax.fori_loop(1, ORDER + 1, one_order, 0)


def sums_in_kernel(count, total_ref, width):
    flow = jnp.zeros((ROWS, LANES), jnp.float32)
    density = jnp.zeros((ROWS, LANES), jnp.float32)
    for orbital in range(count):
        for plane in range(width):
            real = total_ref[2 * orbital, plane]
            imaginary = total_ref[2 * orbital + 1, plane]
            moved = None
            for reach in range(1, 5):
                ahead = total_ref[2 * orbital + 1, (plane + reach) % width]
                behind = total_ref[2 * orbital + 1, (plane - reach) % width]
                term = FIRST[reach - 1] * (ahead - behind)
                moved = term if moved is None else moved + term
            flow = flow + real * moved
            density = density + (real * real + imaginary * imaginary)
    return (2.0 * SLOPE) * flow, density


def first_kernel(parts, count, kinds, opening, scalar_ref, *refs):
    if opening:
        piece_ref, *tables, total_ref, out_ref, potential_ref, field_ref = refs[:11]
        scratch = refs[11:]
    else:
        here_ref, pieces, refs = refs[0], refs[1 : 1 + parts], refs[1 + parts :]
        potential_ref, *tables, sums_ref, total_ref, out_ref, field_ref = refs[:11]
        scratch = refs[11:]
    width = total_ref.shape[1]
    planes = width // parts
    for step in range(parts):
        if opening:
            piece, start = piece_ref.at[step], step * planes
        else:
            piece, start = pieces[step], lax.rem(here_ref[0] + parts - step, parts) * planes
        for index in range(planes):
            rows = pl.ds(index, ROWS, stride=planes)
            for orbital in range(count):
                for part in range(2):
                    value = piece[part * count + orbital, rows, :]
                    field_ref[2 * orbital + part, start + index] = value
                    total_ref[2 * orbital + part, start + index] = value
            if opening:
                potential_ref[start + index] = piece[2 * count, rows, :]
    propagate_in_kernel(
        count, scalar_ref[0], field_ref, total_ref, potential_ref, tables, scratch, width, kinds
    )
    flow, density = sums_in_kernel(count, total_ref, width)
    if not opening:
        flow, density = sums_ref[0] + flow, sums_ref[1] + density
    out_ref[0] = flow
    out_ref[1] = density


def second_kernel(parts, count, kinds, points, opening, copies, scalar_ref, *refs):
    if opening:
        here_ref, seen, refs = refs[0], refs[1 : 1 + parts], refs[1 + parts :]
    else:
        vector_ref, first_sums_ref, sums_ref, *refs = refs
    psi_ref, potential_ref, *tables = refs[:8]
    refs = refs[8:]
    if copies and opening:
        first_sums_ref = seen[0]
    if opening and not copies:
        pieces, vector_ref, refs = refs[:parts], refs[parts], refs[parts + 1 :]
    else:
        piece_ref, *refs = refs
    out_ref, field_ref, total_ref = refs[:3]
    scratch = refs[3:]
    width = total_ref.shape[1]
    planes = width // parts
    if opening:
        flow = jnp.sum(fold([ref[0] for ref in seen]))
        density = jnp.sum(fold([ref[1] for ref in seen]))
        current = (flow + scalar_ref[0] * density) * (1.0 / points)
        vector_value = scalar_ref[1] - source_weight * current
        if not copies:
            vector_ref[0] = vector_value
    else:
        vector_value = vector_ref[0]
    field_ref[...] = psi_ref[...]
    total_ref[...] = psi_ref[...]
    propagate_in_kernel(
        count, vector_value, field_ref, total_ref, potential_ref, tables, scratch, width, kinds
    )
    for step in range(parts):
        if copies:
            piece, start = piece_ref.at[step], step * planes
        else:
            piece, start = pieces[step], lax.rem(here_ref[0] + step, parts) * planes
        for index in range(planes):
            rows = pl.ds(index, ROWS, stride=planes)
            for orbital in range(count):
                for part in range(2):
                    piece[part * count + orbital, rows, :] = total_ref[2 * orbital + part, start + index]
    flow, density = sums_in_kernel(count, total_ref, width)
    if not opening:
        flow, density = sums_ref[0] + flow, sums_ref[1] + density
    if copies:
        row = lax.broadcasted_iota(jnp.int32, (ROWS, LANES), 0)
        own = first_sums_ref[0] + scalar_ref[0] * first_sums_ref[1]
        own = jnp.sum(own, axis=0, keepdims=True) * (1.0 / points)
        new = jnp.sum(flow + vector_value * density, axis=0, keepdims=True) * (1.0 / points)
        message = jnp.where(row == 0, own, jnp.where(row == 1, new, scalar_ref[2]))
        for copy in range(copies):
            out_ref[copy] = message
    else:
        out_ref[0] = flow
        out_ref[1] = density


def vmem():
    return pl.BlockSpec(memory_space=pltpu.VMEM)


def smem():
    return pl.BlockSpec(memory_space=pltpu.SMEM)


def anywhere():
    return pl.BlockSpec(memory_space=pl.ANY)


def hbm():
    return pl.BlockSpec(memory_space=pltpu.HBM)


def float_array(*shape):
    return jax.ShapeDtypeStruct(shape, jnp.float32)


def exchanged(value, axes):
    return lax.all_to_all(value, axes, split_axis=0, concat_axis=0, tiled=True)


def shifted(value, axis_name, count, shift):
    return lax.ppermute(value, axis_name, [((index + shift) % count, index) for index in range(count)])


def per_device(parts, blocks, orbitals, local_potential, atom_sites, host_point, fields):
    norb = orbitals.shape[2]
    planes, points = local_potential.shape
    width = planes * parts
    share = norb // parts
    last_count = 1 if share > 1 else 0
    main_count = share - last_count
    owned = fields.shape[1]
    atoms = atom_sites.shape[0]
    kinds = 2 * atoms
    held = ROWS * planes
    total_points = float(width**3 * norb)
    here = lax.axis_index("grid").astype(jnp.int32)[None]
    block = lax.axis_index("macro").astype(jnp.int32)
    params = pltpu.CompilerParams(vmem_limit_bytes=LIMIT)

    def rows_of(value):
        lead = value.shape[:-2]
        value = value.reshape(*lead, planes, ROWS, LANES)
        return jnp.swapaxes(value, -3, -2).reshape(*lead, held, LANES)

    def planes_of(value):
        lead = value.shape[:-2]
        value = value.reshape(*lead, ROWS, planes, LANES)
        return jnp.swapaxes(value, -3, -2)

    source = rows_of(orbitals[0])
    packed = pl.pallas_call(
        functools.partial(pack_kernel, parts, share, main_count, 0),
        out_shape=float_array(parts, 2 * main_count + 1, held, LANES),
        in_specs=[hbm(), hbm()],
        out_specs=anywhere(),
        scratch_shapes=[pltpu.SemaphoreType.DMA((parts * 3,))],
        compiler_params=params,
    )(source, rows_of(local_potential))
    main = exchanged(packed, "grid")
    fields, source, packed = lax.optimization_barrier((fields, source, packed))
    if last_count:
        last = pl.pallas_call(
            functools.partial(pack_pieces_kernel, parts, share, last_count, main_count),
            out_shape=[float_array(2 * last_count, held, LANES)] * parts,
            in_specs=[smem(), hbm()],
            out_specs=[anywhere()] * parts,
            scratch_shapes=[pltpu.SemaphoreType.DMA((parts * 2,))],
            compiler_params=params,
        )(here, source)
        last = [last[0]] + [shifted(last[step], "grid", parts, -step) for step in range(1, parts)]
    field_blocks = [fields] + [shifted(fields, "macro", blocks, step) for step in range(1, blocks)]

    tables = pl.pallas_call(
        functools.partial(tables_kernel, atoms),
        out_shape=[
            jax.ShapeDtypeStruct((2 * LANES, 2 * LANES), jnp.bfloat16),
            jax.ShapeDtypeStruct((2 * LANES, 2 * LANES), jnp.bfloat16),
            jax.ShapeDtypeStruct((2 * LANES, LANES), jnp.bfloat16),
            float_array(width, ROWS, LANES),
            float_array(width, ROWS, LANES),
            float_array(5, ROWS, LANES),
        ],
        in_specs=[smem(), vmem()],
        out_specs=[vmem()] * 6,
        compiler_params=params,
    )(atom_sites, stencil_weights(width))

    scalars = pl.pallas_call(
        functools.partial(vector_kernel, blocks),
        out_shape=float_array(3),
        in_specs=[smem(), smem()] + [vmem()] * blocks,
        out_specs=smem(),
        compiler_params=params,
    )(host_point, block[None], *field_blocks)

    def micro_call(kernel, count, inputs, scalar_inputs, outputs, scalar_outputs, cells):
        rows = 2 * count * width * ROWS
        cell = pltpu.VMEM((2 * count, width, ROWS, LANES), jnp.float32)
        return pl.pallas_call(
            kernel,
            out_shape=outputs,
            in_specs=[smem() if number < scalar_inputs else vmem() for number in range(len(inputs))],
            out_specs=[smem() if number in scalar_outputs else vmem() for number in range(len(outputs))],
            scratch_shapes=[cell] * cells
            + [
                pltpu.VMEM((rows, 2 * LANES), jnp.bfloat16),
                pltpu.VMEM((rows, 2 * LANES), jnp.float32),
                pltpu.VMEM((rows, 2 * LANES), jnp.float32),
                cell,
                cell,
                pltpu.VMEM((rows, 2 * LANES), jnp.bfloat16),
                pltpu.VMEM((width, ROWS, LANES), jnp.float32),
            ],
            compiler_params=params,
            cost_estimate=pl.CostEstimate(
                flops=count * 3 * 2 * 512 * 256 * 256 * ORDER, bytes_accessed=4 * 1024 * 1024, transcendentals=0
            ),
        )(*inputs)

    def cells_of(count):
        return float_array(2 * count, width, ROWS, LANES)

    sums_shape = float_array(2, ROWS, LANES)
    main_psi, sums, potential = micro_call(
        functools.partial(first_kernel, parts, main_count, kinds, True),
        main_count,
        [scalars, main, *tables],
        1,
        [cells_of(main_count), sums_shape, float_array(width, ROWS, LANES)],
        (),
        1,
    )
    if last_count:
        last_psi, sums = micro_call(
            functools.partial(first_kernel, parts, last_count, kinds, False),
            last_count,
            [scalars, here, *last, potential, *tables, sums],
            2,
            [cells_of(last_count), sums_shape],
            (),
            1,
        )
    seen = [sums] + [shifted(sums, "grid", parts, step) for step in range(1, parts)]

    everyone = blocks * parts
    pieces_shape = float_array(parts, 2 * main_count, held, LANES)
    messages_shape = float_array(everyone, ROWS, LANES)
    whole_shape = float_array(2, norb, held, LANES)
    if last_count:
        *pieces, vector_value, second_sums = micro_call(
            functools.partial(second_kernel, parts, last_count, kinds, total_points, True, 0),
            last_count,
            [scalars, here, *seen, last_psi, potential, *tables],
            2,
            [float_array(2 * last_count, held, LANES)] * parts + [float_array(1), sums_shape],
            (parts,),
            2,
        )
        pieces = [pieces[0]] + [shifted(pieces[step], "grid", parts, -step) for step in range(1, parts)]
        main_pieces, messages = micro_call(
            functools.partial(second_kernel, parts, main_count, kinds, total_points, False, everyone),
            main_count,
            [scalars, vector_value, sums, second_sums, main_psi, potential, *tables],
            2,
            [pieces_shape, messages_shape],
            (),
            2,
        )
    else:
        main_pieces, messages = micro_call(
            functools.partial(second_kernel, parts, main_count, kinds, total_points, True, everyone),
            main_count,
            [scalars, here, *seen, main_psi, potential, *tables],
            2,
            [pieces_shape, messages_shape],
            (),
            2,
        )
    returned = exchanged(main_pieces, "grid")
    result = []
    if last_count:
        result = pl.pallas_call(
            functools.partial(unpack_pieces_kernel, parts, share, last_count, main_count),
            out_shape=whole_shape,
            in_specs=[smem()] + [anywhere()] * parts,
            out_specs=hbm(),
            scratch_shapes=[pltpu.SemaphoreType.DMA((parts * 2,))],
            compiler_params=params,
        )(here, *pieces)
        result, messages = lax.optimization_barrier((result, messages))
        result = [result]
    result = pl.pallas_call(
        functools.partial(unpack_kernel, parts, share, main_count, 0),
        out_shape=whole_shape,
        in_specs=[anywhere()] + [hbm()] * len(result),
        out_specs=hbm(),
        scratch_shapes=[pltpu.SemaphoreType.DMA((parts * 2,))],
        input_output_aliases={1: 0} if result else {},
        compiler_params=params,
    )(returned, *result)
    orbitals_out = planes_of(result).reshape(2, norb, planes, points)

    messages = exchanged(messages, ("macro", "grid")).reshape(blocks, parts, ROWS, LANES)
    currents = jnp.sum(messages[:, :, :2], axis=(1, 3))
    hosts = messages[:, 0, 2, 0].astype(jnp.int32)
    length = blocks * owned
    start = block * owned
    positions = lax.broadcasted_iota(jnp.int32, (length,), 0)
    sources = jnp.sum(
        jnp.where(positions[None, None] == hosts[:, None, None], currents[:, :, None], 0.0), axis=0
    )
    turned = jnp.concatenate(field_blocks, axis=1)
    whole = lax.dynamic_slice_in_dim(
        jnp.concatenate([turned, turned], axis=1), length - start, length, axis=1
    )
    previous, present = whole[0], whole[1]
    for step in range(STEPS):
        rim = jnp.pad(present, 1)
        following = (
            2.0 * present
            - previous
            + courant_square * (rim[2:] - 2.0 * present + rim[:-2])
            - source_weight * sources[step]
        )
        previous, present = present, following
    fields_out = lax.dynamic_slice_in_dim(jnp.stack([previous, present]), start, owned, axis=1)
    return orbitals_out[None], fields_out


def solution(mesh):
    in_specs = (
        P("macro", None, None, "grid", None),
        P("grid", None),
        P(),
        P("macro"),
        P(None, "macro"),
    )
    out_specs = (P("macro", None, None, "grid", None), P(None, "macro"))
    return jax.shard_map(
        functools.partial(per_device, mesh.shape["grid"], mesh.shape["macro"]),
        mesh=mesh,
        in_specs=in_specs,
        out_specs=out_specs,
        check_vma=False,
    )
```

```python
import functools

import jax
import jax.numpy as jnp
import numpy as np
from jax import lax
from jax.experimental import pallas as pl
from jax.experimental.pallas import tpu as pltpu
from jax.sharding import PartitionSpec as P

ORDER = 4
STEPS = 2
spacing = 0.3206
time_step = 0.02
courant_square = 0.81
source_weight = 0.1
radial_strength = 0.3
polar_strength = -0.2
projector_width = 2.5

SECOND = (-14350.0, 8064.0, -1008.0, 128.0, -9.0)
FIRST = (672.0, -168.0, 32.0, -3.0)
KINETIC = 1.0 / (2.0 * 5040.0 * spacing * spacing)
SLOPE = 1.0 / (840.0 * spacing)

LANES = 128
ROWS = 8
LIMIT = 24 * 1024 * 1024


def stencil_weights(width):
    group = LANES // width
    total = np.zeros((LANES, 3 * LANES), np.float32)
    for y_in in range(group):
        for z_in in range(width):
            for y_out in range(group):
                for part, step in enumerate((0, group, -group)):
                    reach = abs(step + y_in - y_out)
                    if 1 <= reach <= 4:
                        total[y_in * width + z_in, part * LANES + y_out * width + z_in] += SECOND[reach]
            for reach in range(1, 5):
                for z_out in ((z_in + reach) % width, (z_in - reach) % width):
                    total[y_in * width + z_in, y_in * width + z_out] += SECOND[reach]
    return jnp.asarray(np.concatenate([total, total], axis=0), jnp.bfloat16)


def periodic(distance, width):
    return ((distance + width // 2) & (width - 1)) - width // 2


def bell_of(offset):
    distance = offset.astype(jnp.float32)
    bell = jnp.exp(-0.5 * distance * distance / (projector_width * projector_width))
    return bell, distance / projector_width * bell


def tables_kernel(atoms, site_ref, stencil_ref, near_ref, far_ref, zy_ref, xbell_ref, xslope_ref, y_ref):
    width = xbell_ref.shape[0]
    kinds = 2 * atoms
    group = LANES // width

    def site_of(column, axis_number):
        atom = (column % kinds) // 2
        position = jnp.zeros(column.shape, jnp.int32)
        for number in range(atoms):
            position = jnp.where(atom == number, site_ref[number, axis_number], position)
        return position

    def factor(coordinate, column):
        bell, slope = bell_of(periodic(coordinate - site_of(column, 2), width))
        value = jnp.where(column % 2 == 0, bell, slope)
        high = value.astype(jnp.bfloat16).astype(jnp.float32)
        return jnp.where(column % LANES < LANES // 2, high, value - high)

    def groups_agree(point, column):
        return (point % LANES) // width == (column // kinds) % group

    shape = (2 * LANES, LANES)
    first = lax.broadcasted_iota(jnp.int32, shape, 0)
    last = lax.broadcasted_iota(jnp.int32, shape, 1)
    near_ref[:, :LANES] = stencil_ref[:, :LANES]
    far_ref[...] = stencil_ref[:, LANES:]
    inward = jnp.where(groups_agree(first, last), factor(first % width, last), 0.0)
    near_ref[:, LANES:] = inward.astype(jnp.bfloat16)
    outward = jnp.where(groups_agree(last, first), factor(last % width, first), 0.0)
    zy_ref[...] = outward.astype(jnp.bfloat16)

    shape = (width, ROWS, LANES)
    plane = lax.broadcasted_iota(jnp.int32, shape, 0)
    column = lax.broadcasted_iota(jnp.int32, shape, 2)
    bell, slope = bell_of(periodic(plane - site_of(column, 0), width))
    xbell_ref[...] = bell
    xslope_ref[...] = slope

    shape = (ROWS, LANES)
    column = lax.broadcasted_iota(jnp.int32, shape, 1)
    row = lax.broadcasted_iota(jnp.int32, shape, 0) * group + (column // kinds) % group
    bell, slope = bell_of(periodic(row - site_of(column, 1), width))
    scale = -1.0 / KINETIC
    even = column % 2 == 0
    y_ref[0] = bell
    y_ref[1] = slope
    y_ref[2] = bell * jnp.where(even, scale * radial_strength, scale * polar_strength)
    y_ref[3] = bell * jnp.where(even, scale * polar_strength, 0.0)
    y_ref[4] = slope * jnp.where(even, scale * polar_strength, 0.0)


def vector_kernel(blocks, host_ref, here_ref, *refs):
    out_ref = refs[blocks]
    owned = refs[0].shape[1]
    host = host_ref[0]
    place = lax.broadcasted_iota(jnp.int32, (1, owned), 1)
    present = jnp.zeros((1, owned), jnp.float32)
    previous, beside = present, present
    for number in range(blocks):
        position = place + lax.rem(here_ref[0] + number, blocks) * owned
        before, now = refs[number][0:1, :], refs[number][1:2, :]
        present = present + jnp.where(position == host, now, 0.0)
        previous = previous + jnp.where(position == host, before, 0.0)
        beside = beside + jnp.where((position == host - 1) | (position == host + 1), now, 0.0)
    present = jnp.sum(present)
    out_ref[0] = present
    out_ref[1] = 2.0 * present - jnp.sum(previous) + courant_square * (jnp.sum(beside) - 2.0 * present)
    out_ref[2] = host.astype(jnp.float32)


def run_copies(pairs, sems):
    copies = [
        pltpu.make_async_copy(source, target, sems.at[number]) for number, (source, target) in enumerate(pairs)
    ]
    for copy in copies:
        copy.start()
    for copy in copies:
        copy.wait()


def pack_kernel(parts, share, count, first, source_ref, potential_ref, out_ref, sems):
    pairs = []
    for owner in range(parts):
        pairs.append((potential_ref, out_ref.at[owner, 2 * count]))
        for part in range(2):
            source = source_ref.at[part, pl.ds(owner * share + first, count)]
            pairs.append((source, out_ref.at[owner, pl.ds(part * count, count)]))
    run_copies(pairs, sems)


def pack_pieces_kernel(parts, share, count, first, here_ref, source_ref, *refs):
    pairs = []
    for step in range(parts):
        owner = lax.rem(here_ref[0] + step, parts)
        for part in range(2):
            source = source_ref.at[part, pl.ds(owner * share + first, count)]
            pairs.append((source, refs[step].at[pl.ds(part * count, count)]))
    run_copies(pairs, refs[parts])


def unpack_kernel(parts, share, count, first, piece_ref, *refs):
    out_ref, sems = refs[-2:]
    pairs = []
    for owner in range(parts):
        for part in range(2):
            target = out_ref.at[part, pl.ds(owner * share + first, count)]
            pairs.append((piece_ref.at[owner, pl.ds(part * count, count)], target))
    run_copies(pairs, sems)


def unpack_pieces_kernel(parts, share, count, first, here_ref, *refs):
    out_ref, sems = refs[-2:]
    pairs = []
    for step in range(parts):
        owner = lax.rem(here_ref[0] + parts - step, parts)
        for part in range(2):
            target = out_ref.at[part, pl.ds(owner * share + first, count)]
            pairs.append((refs[step].at[pl.ds(part * count, count)], target))
    run_copies(pairs, sems)


def fold(values):
    while len(values) > 1:
        half = len(values) // 2
        values = [values[number] + values[number + half] for number in range(half)]
    return values[0]


def total_of_groups(value, kinds):
    for shift in (4, 2, 1):
        value = value + pltpu.roll(value, shift, 0)
    shift = LANES // 2
    while shift >= kinds:
        value = value + pltpu.roll(value, shift, 1)
        shift //= 2
    return value


def propagate_in_kernel(
    count, vector_value, field_ref, total_ref, potential_ref, tables, scratch, width, kinds
):
    near_ref, far_ref, zy_ref, xbell_ref, xslope_ref, y_ref = tables
    split_ref, first_ref, second_ref, partial_ref, drift_ref, spread_ref, diagonal_ref = scratch
    diagonal_ref[...] = (3.0 * SECOND[0] - 0.5 * vector_value * vector_value / KINETIC) - potential_ref[
        ...
    ] * (1.0 / KINETIC)
    block = ROWS
    slab = block * ROWS
    cell_rows = width * ROWS

    def split(planes):
        rows = planes.reshape(slab, LANES)
        high = rows.astype(jnp.bfloat16)
        low = (rows - high.astype(jnp.float32)).astype(jnp.bfloat16)
        return high, low

    def store_split(ref, number, start, planes):
        rows = pl.ds(number * cell_rows + start * ROWS, slab)
        high, low = split(planes)
        ref[rows, :LANES] = high
        ref[rows, LANES:] = low

    for number in range(2 * count):
        for start in range(0, width, block):
            store_split(split_ref, number, start, field_ref[number, start : start + block])

    def one_order(order, carry):
        inverse = jnp.where(order == 1, 1.0, jnp.where(order == 2, 0.5, jnp.where(order == 3, 1.0 / 3.0, 0.25)))
        step_scale = inverse * time_step
        kinetic = step_scale * KINETIC
        drift = step_scale * SLOPE * vector_value
        slopes = [drift * weight for weight in FIRST]
        outers = {}
        for orbital in range(count):
            rows = pl.ds(2 * orbital * cell_rows, 2 * cell_rows)
            first_ref[rows, :] = jnp.dot(split_ref[rows, :], near_ref[...], preferred_element_type=jnp.float32)
            for number in (2 * orbital, 2 * orbital + 1):
                bells = [jnp.zeros((ROWS, LANES), jnp.float32) for _ in range(2)]
                inclines = [jnp.zeros((ROWS, LANES), jnp.float32) for _ in range(2)]
                for plane in range(width):
                    inner = first_ref[pl.ds(number * cell_rows + plane * ROWS, ROWS), LANES:]
                    turn = plane % 2
                    bells[turn] = bells[turn] + inner * xbell_ref[plane]
                    inclines[turn] = inclines[turn] + inner * xslope_ref[plane]
                bell = bells[0] + bells[1]
                incline = inclines[0] + inclines[1]
                first = total_of_groups(bell * y_ref[0], kinds)
                second = total_of_groups(incline * y_ref[0], kinds)
                third = total_of_groups(bell * y_ref[1], kinds)
                outers[number] = (first * y_ref[2] + third * y_ref[4], second * y_ref[3])
        for orbital in range(count):
            rows = pl.ds(2 * orbital * cell_rows, 2 * cell_rows)
            second_ref[rows, :] = jnp.dot(split_ref[rows, :], far_ref[...], preferred_element_type=jnp.float32)
            for start in range(0, width, block):
                for number in (2 * orbital, 2 * orbital + 1):
                    near = {
                        plane: field_ref[number, plane % width] for plane in range(start - 4, start + block + 4)
                    }
                    for plane in range(start, start + block):
                        line = pl.ds(number * cell_rows + plane * ROWS, ROWS)
                        total = first_ref[line, :LANES]
                        total = total + pltpu.roll(second_ref[line, :LANES], ROWS - 1, 0)
                        total = total + pltpu.roll(second_ref[line, LANES:], 1, 0)
                        total = total + diagonal_ref[plane] * near[plane]
                        moved = None
                        for reach in range(1, 5):
                            ahead, behind = near[plane + reach], near[plane - reach]
                            total = total + SECOND[reach] * (ahead + behind)
                            term = slopes[reach - 1] * (ahead - behind)
                            moved = term if moved is None else moved + term
                        partial_ref[number, plane] = total
                        drift_ref[number, plane] = moved
        for orbital in range(count):
            real, imaginary = 2 * orbital, 2 * orbital + 1
            for start in range(0, width, block):
                xbell = xbell_ref[start : start + block]
                xslope = xslope_ref[start : start + block]
                for number in (real, imaginary):
                    spread = xbell * outers[number][0][None] + xslope * outers[number][1][None]
                    store_split(spread_ref, number, start, spread)
            rows = pl.ds(real * cell_rows, 2 * cell_rows)
            first_ref[rows, :LANES] = jnp.dot(
                spread_ref[rows, :], zy_ref[...], preferred_element_type=jnp.float32
            )
            for start in range(0, width, block):
                images = []
                for number in (real, imaginary):
                    rows = pl.ds(number * cell_rows + start * ROWS, slab)
                    images.append(
                        partial_ref[number, start : start + block]
                        + first_ref[rows, :LANES].reshape(block, ROWS, LANES)
                    )
                new = (
                    -kinetic * images[1] - drift_ref[real, start : start + block],
                    kinetic * images[0] - drift_ref[imaginary, start : start + block],
                )
                for number, value in zip((real, imaginary), new):
                    field_ref[number, start : start + block] = value
                    total_ref[number, start : start + block] += value
                    store_split(split_ref, number, start, value)
        return carry

    lax.fori_loop(1, ORDER + 1, one_order, 0)


def sums_in_kernel(count, total_ref, width):
    flow = jnp.zeros((ROWS, LANES), jnp.float32)
    density = jnp.zeros((ROWS, LANES), jnp.float32)
    for orbital in range(count):
        for plane in range(width):
            real = total_ref[2 * orbital, plane]
            imaginary = total_ref[2 * orbital + 1, plane]
            moved = None
            for reach in range(1, 5):
                ahead = total_ref[2 * orbital + 1, (plane + reach) % width]
                behind = total_ref[2 * orbital + 1, (plane - reach) % width]
                term = FIRST[reach - 1] * (ahead - behind)
                moved = term if moved is None else moved + term
            flow = flow + real * moved
            density = density + (real * real + imaginary * imaginary)
    return (2.0 * SLOPE) * flow, density


def first_kernel(parts, count, kinds, opening, scalar_ref, *refs):
    if opening:
        piece_ref, *tables, total_ref, out_ref, potential_ref, field_ref = refs[:11]
        scratch = refs[11:]
    else:
        here_ref, pieces, refs = refs[0], refs[1 : 1 + parts], refs[1 + parts :]
        potential_ref, *tables, sums_ref, total_ref, out_ref, field_ref = refs[:11]
        scratch = refs[11:]
    width = total_ref.shape[1]
    planes = width // parts
    for step in range(parts):
        if opening:
            piece, start = piece_ref.at[step], step * planes
        else:
            piece, start = pieces[step], lax.rem(here_ref[0] + parts - step, parts) * planes
        for index in range(planes):
            rows = pl.ds(index, ROWS, stride=planes)
            for orbital in range(count):
                for part in range(2):
                    value = piece[part * count + orbital, rows, :]
                    field_ref[2 * orbital + part, start + index] = value
                    total_ref[2 * orbital + part, start + index] = value
            if opening:
                potential_ref[start + index] = piece[2 * count, rows, :]
    propagate_in_kernel(
        count, scalar_ref[0], field_ref, total_ref, potential_ref, tables, scratch, width, kinds
    )
    flow, density = sums_in_kernel(count, total_ref, width)
    if not opening:
        flow, density = sums_ref[0] + flow, sums_ref[1] + density
    out_ref[0] = flow
    out_ref[1] = density


def second_kernel(parts, count, kinds, points, opening, permuted, copies, scalar_ref, *refs):
    if permuted:
        here_ref, *refs = refs
    if opening:
        seen, refs = refs[:parts], refs[parts:]
        first_sums_ref = seen[0]
    else:
        vector_ref, first_sums_ref, sums_ref, *refs = refs
    psi_ref, potential_ref, *tables = refs[:8]
    refs = refs[8:]
    if permuted:
        pieces, refs = refs[:parts], refs[parts:]
    else:
        piece_ref, *refs = refs
    if opening and not copies:
        vector_ref, *refs = refs
    out_ref, field_ref, total_ref = refs[:3]
    scratch = refs[3:]
    width = total_ref.shape[1]
    planes = width // parts
    if opening:
        flow = jnp.sum(fold([ref[0] for ref in seen]))
        density = jnp.sum(fold([ref[1] for ref in seen]))
        current = (flow + scalar_ref[0] * density) * (1.0 / points)
        vector_value = scalar_ref[1] - source_weight * current
        if not copies:
            vector_ref[0] = vector_value
    else:
        vector_value = vector_ref[0]
    field_ref[...] = psi_ref[...]
    total_ref[...] = psi_ref[...]
    propagate_in_kernel(
        count, vector_value, field_ref, total_ref, potential_ref, tables, scratch, width, kinds
    )
    for step in range(parts):
        if permuted:
            piece, start = pieces[step], lax.rem(here_ref[0] + step, parts) * planes
        else:
            piece, start = piece_ref.at[step], step * planes
        for index in range(planes):
            rows = pl.ds(index, ROWS, stride=planes)
            for orbital in range(count):
                for part in range(2):
                    piece[part * count + orbital, rows, :] = total_ref[2 * orbital + part, start + index]
    flow, density = sums_in_kernel(count, total_ref, width)
    if not opening:
        flow, density = sums_ref[0] + flow, sums_ref[1] + density
    if copies:
        row = lax.broadcasted_iota(jnp.int32, (ROWS, LANES), 0)
        own = first_sums_ref[0] + scalar_ref[0] * first_sums_ref[1]
        own = jnp.sum(own, axis=0, keepdims=True) * (1.0 / points)
        new = jnp.sum(flow + vector_value * density, axis=0, keepdims=True) * (1.0 / points)
        message = jnp.where(row == 0, own, jnp.where(row == 1, new, scalar_ref[2]))
        for copy in range(copies):
            out_ref[copy] = message
    else:
        out_ref[0] = flow
        out_ref[1] = density


def vmem():
    return pl.BlockSpec(memory_space=pltpu.VMEM)


def smem():
    return pl.BlockSpec(memory_space=pltpu.SMEM)


def anywhere():
    return pl.BlockSpec(memory_space=pl.ANY)


def hbm():
    return pl.BlockSpec(memory_space=pltpu.HBM)


def float_array(*shape):
    return jax.ShapeDtypeStruct(shape, jnp.float32)


def exchanged(value, axes):
    return lax.all_to_all(value, axes, split_axis=0, concat_axis=0, tiled=True)


def shifted(value, axis_name, count, shift):
    return lax.ppermute(value, axis_name, [((index + shift) % count, index) for index in range(count)])


def per_device(parts, blocks, orbitals, local_potential, atom_sites, host_point, fields):
    norb = orbitals.shape[2]
    planes, points = local_potential.shape
    width = planes * parts
    share = norb // parts
    last_count = share // 2
    main_count = share - last_count
    owned = fields.shape[1]
    atoms = atom_sites.shape[0]
    kinds = 2 * atoms
    held = ROWS * planes
    total_points = float(width**3 * norb)
    here = lax.axis_index("grid").astype(jnp.int32)[None]
    block = lax.axis_index("macro").astype(jnp.int32)
    params = pltpu.CompilerParams(vmem_limit_bytes=LIMIT)

    def rows_of(value):
        lead = value.shape[:-2]
        value = value.reshape(*lead, planes, ROWS, LANES)
        return jnp.swapaxes(value, -3, -2).reshape(*lead, held, LANES)

    def planes_of(value):
        lead = value.shape[:-2]
        value = value.reshape(*lead, ROWS, planes, LANES)
        return jnp.swapaxes(value, -3, -2)

    source = rows_of(orbitals[0])
    packed = pl.pallas_call(
        functools.partial(pack_kernel, parts, share, main_count, 0),
        out_shape=float_array(parts, 2 * main_count + 1, held, LANES),
        in_specs=[hbm(), hbm()],
        out_specs=anywhere(),
        scratch_shapes=[pltpu.SemaphoreType.DMA((parts * 3,))],
        compiler_params=params,
    )(source, rows_of(local_potential))
    main = exchanged(packed, "grid")
    fields, source, packed = lax.optimization_barrier((fields, source, packed))
    if last_count:
        last = pl.pallas_call(
            functools.partial(pack_pieces_kernel, parts, share, last_count, main_count),
            out_shape=[float_array(2 * last_count, held, LANES)] * parts,
            in_specs=[smem(), hbm()],
            out_specs=[anywhere()] * parts,
            scratch_shapes=[pltpu.SemaphoreType.DMA((parts * 2,))],
            compiler_params=params,
        )(here, source)
        last = [last[0]] + [shifted(last[step], "grid", parts, -step) for step in range(1, parts)]
    field_blocks = [fields] + [shifted(fields, "macro", blocks, step) for step in range(1, blocks)]

    tables = pl.pallas_call(
        functools.partial(tables_kernel, atoms),
        out_shape=[
            jax.ShapeDtypeStruct((2 * LANES, 2 * LANES), jnp.bfloat16),
            jax.ShapeDtypeStruct((2 * LANES, 2 * LANES), jnp.bfloat16),
            jax.ShapeDtypeStruct((2 * LANES, LANES), jnp.bfloat16),
            float_array(width, ROWS, LANES),
            float_array(width, ROWS, LANES),
            float_array(5, ROWS, LANES),
        ],
        in_specs=[smem(), vmem()],
        out_specs=[vmem()] * 6,
        compiler_params=params,
    )(atom_sites, stencil_weights(width))

    scalars = pl.pallas_call(
        functools.partial(vector_kernel, blocks),
        out_shape=float_array(3),
        in_specs=[smem(), smem()] + [vmem()] * blocks,
        out_specs=smem(),
        compiler_params=params,
    )(host_point, block[None], *field_blocks)

    def micro_call(kernel, count, inputs, scalar_inputs, outputs, scalar_outputs, cells):
        rows = 2 * count * width * ROWS
        cell = pltpu.VMEM((2 * count, width, ROWS, LANES), jnp.float32)
        return pl.pallas_call(
            kernel,
            out_shape=outputs,
            in_specs=[smem() if number < scalar_inputs else vmem() for number in range(len(inputs))],
            out_specs=[smem() if number in scalar_outputs else vmem() for number in range(len(outputs))],
            scratch_shapes=[cell] * cells
            + [
                pltpu.VMEM((rows, 2 * LANES), jnp.bfloat16),
                pltpu.VMEM((rows, 2 * LANES), jnp.float32),
                pltpu.VMEM((rows, 2 * LANES), jnp.float32),
                cell,
                cell,
                pltpu.VMEM((rows, 2 * LANES), jnp.bfloat16),
                pltpu.VMEM((width, ROWS, LANES), jnp.float32),
            ],
            compiler_params=params,
            cost_estimate=pl.CostEstimate(
                flops=count * 3 * 2 * 512 * 256 * 256 * ORDER, bytes_accessed=4 * 1024 * 1024, transcendentals=0
            ),
        )(*inputs)

    def cells_of(count):
        return float_array(2 * count, width, ROWS, LANES)

    sums_shape = float_array(2, ROWS, LANES)
    main_psi, sums, potential = micro_call(
        functools.partial(first_kernel, parts, main_count, kinds, True),
        main_count,
        [scalars, main, *tables],
        1,
        [cells_of(main_count), sums_shape, float_array(width, ROWS, LANES)],
        (),
        1,
    )
    if last_count:
        last_psi, sums = micro_call(
            functools.partial(first_kernel, parts, last_count, kinds, False),
            last_count,
            [scalars, here, *last, potential, *tables, sums],
            2,
            [cells_of(last_count), sums_shape],
            (),
            1,
        )
    seen = [sums] + [shifted(sums, "grid", parts, step) for step in range(1, parts)]

    everyone = blocks * parts
    pieces_shape = float_array(parts, 2 * main_count, held, LANES)
    messages_shape = float_array(everyone, ROWS, LANES)
    whole_shape = float_array(2, norb, held, LANES)
    main_pieces, *rest = micro_call(
        functools.partial(
            second_kernel, parts, main_count, kinds, total_points, True, False, 0 if last_count else everyone
        ),
        main_count,
        [scalars, *seen, main_psi, potential, *tables],
        1,
        [pieces_shape] + ([float_array(1), sums_shape] if last_count else [messages_shape]),
        (1,) if last_count else (),
        2,
    )
    returned = exchanged(main_pieces, "grid")
    messages = rest[-1]
    if last_count:
        vector_value, second_sums = rest
        *pieces, messages = micro_call(
            functools.partial(second_kernel, parts, last_count, kinds, total_points, False, True, everyone),
            last_count,
            [scalars, here, vector_value, sums, second_sums, last_psi, potential, *tables],
            3,
            [float_array(2 * last_count, held, LANES)] * parts + [messages_shape],
            (),
            2,
        )
        pieces = [pieces[0]] + [shifted(pieces[step], "grid", parts, -step) for step in range(1, parts)]
    result = pl.pallas_call(
        functools.partial(unpack_kernel, parts, share, main_count, 0),
        out_shape=whole_shape,
        in_specs=[anywhere()],
        out_specs=hbm(),
        scratch_shapes=[pltpu.SemaphoreType.DMA((parts * 2,))],
        compiler_params=params,
    )(returned)
    result, messages = lax.optimization_barrier((result, messages))
    messages = exchanged(messages, ("macro", "grid")).reshape(blocks, parts, ROWS, LANES)
    if last_count:
        result = pl.pallas_call(
            functools.partial(unpack_pieces_kernel, parts, share, last_count, main_count),
            out_shape=whole_shape,
            in_specs=[smem()] + [anywhere()] * parts + [hbm()],
            out_specs=hbm(),
            scratch_shapes=[pltpu.SemaphoreType.DMA((parts * 2,))],
            input_output_aliases={1 + parts: 0},
            compiler_params=params,
        )(here, *pieces, result)
    orbitals_out = planes_of(result).reshape(2, norb, planes, points)

    currents = jnp.sum(messages[:, :, :2], axis=(1, 3))
    hosts = messages[:, 0, 2, 0].astype(jnp.int32)
    length = blocks * owned
    start = block * owned
    positions = lax.broadcasted_iota(jnp.int32, (length,), 0)
    sources = jnp.sum(
        jnp.where(positions[None, None] == hosts[:, None, None], currents[:, :, None], 0.0), axis=0
    )
    turned = jnp.concatenate(field_blocks, axis=1)
    whole = lax.dynamic_slice_in_dim(
        jnp.concatenate([turned, turned], axis=1), length - start, length, axis=1
    )
    previous, present = whole[0], whole[1]
    for step in range(STEPS):
        rim = jnp.pad(present, 1)
        following = (
            2.0 * present
            - previous
            + courant_square * (rim[2:] - 2.0 * present + rim[:-2])
            - source_weight * sources[step]
        )
        previous, present = present, following
    fields_out = lax.dynamic_slice_in_dim(jnp.stack([previous, present]), start, owned, axis=1)
    return orbitals_out[None], fields_out


def solution(mesh):
    in_specs = (
        P("macro", None, None, "grid", None),
        P("grid", None),
        P(),
        P("macro"),
        P(None, "macro"),
    )
    out_specs = (P("macro", None, None, "grid", None), P(None, "macro"))
    return jax.shard_map(
        functools.partial(per_device, mesh.shape["grid"], mesh.shape["macro"]),
        mesh=mesh,
        in_specs=in_specs,
        out_specs=out_specs,
        check_vma=False,
    )
```

```python
import functools

import jax
import jax.numpy as jnp
import numpy as np
from jax import lax
from jax.experimental import pallas as pl
from jax.experimental.pallas import tpu as pltpu
from jax.sharding import PartitionSpec as P

ORDER = 4
STEPS = 2
spacing = 0.3206
time_step = 0.02
courant_square = 0.81
source_weight = 0.1
radial_strength = 0.3
polar_strength = -0.2
projector_width = 2.5

SECOND = (-14350.0, 8064.0, -1008.0, 128.0, -9.0)
FIRST = (672.0, -168.0, 32.0, -3.0)
KINETIC = 1.0 / (2.0 * 5040.0 * spacing * spacing)
SLOPE = 1.0 / (840.0 * spacing)

LANES = 128
ROWS = 8
LIMIT = 24 * 1024 * 1024
WHOLE = 60 * 1024 * 1024


def stencil_weights(width):
    group = LANES // width
    total = np.zeros((LANES, 3 * LANES), np.float32)
    for y_in in range(group):
        for z_in in range(width):
            for y_out in range(group):
                for part, step in enumerate((0, group, -group)):
                    reach = abs(step + y_in - y_out)
                    if 1 <= reach <= 4:
                        total[y_in * width + z_in, part * LANES + y_out * width + z_in] += SECOND[reach]
            for reach in range(1, 5):
                for z_out in ((z_in + reach) % width, (z_in - reach) % width):
                    total[y_in * width + z_in, y_in * width + z_out] += SECOND[reach]
    return jnp.asarray(np.concatenate([total, total], axis=0), jnp.bfloat16)


def periodic(distance, width):
    return ((distance + width // 2) & (width - 1)) - width // 2


def bell_of(offset):
    distance = offset.astype(jnp.float32)
    bell = jnp.exp(-0.5 * distance * distance / (projector_width * projector_width))
    return bell, distance / projector_width * bell


def tables_kernel(atoms, site_ref, stencil_ref, near_ref, far_ref, zy_ref, xbell_ref, xslope_ref, y_ref):
    width = xbell_ref.shape[0]
    kinds = 2 * atoms
    group = LANES // width

    def site_of(column, axis_number):
        atom = (column % kinds) // 2
        position = jnp.zeros(column.shape, jnp.int32)
        for number in range(atoms):
            position = jnp.where(atom == number, site_ref[number, axis_number], position)
        return position

    def factor(coordinate, column):
        bell, slope = bell_of(periodic(coordinate - site_of(column, 2), width))
        value = jnp.where(column % 2 == 0, bell, slope)
        high = value.astype(jnp.bfloat16).astype(jnp.float32)
        return jnp.where(column % LANES < LANES // 2, high, value - high)

    def groups_agree(point, column):
        return (point % LANES) // width == (column // kinds) % group

    shape = (2 * LANES, LANES)
    first = lax.broadcasted_iota(jnp.int32, shape, 0)
    last = lax.broadcasted_iota(jnp.int32, shape, 1)
    near_ref[:, :LANES] = stencil_ref[:, :LANES]
    far_ref[...] = stencil_ref[:, LANES:]
    inward = jnp.where(groups_agree(first, last), factor(first % width, last), 0.0)
    near_ref[:, LANES:] = inward.astype(jnp.bfloat16)
    outward = jnp.where(groups_agree(last, first), factor(last % width, first), 0.0)
    zy_ref[...] = outward.astype(jnp.bfloat16)

    shape = (width, ROWS, LANES)
    plane = lax.broadcasted_iota(jnp.int32, shape, 0)
    column = lax.broadcasted_iota(jnp.int32, shape, 2)
    bell, slope = bell_of(periodic(plane - site_of(column, 0), width))
    xbell_ref[...] = bell
    xslope_ref[...] = slope

    shape = (ROWS, LANES)
    column = lax.broadcasted_iota(jnp.int32, shape, 1)
    row = lax.broadcasted_iota(jnp.int32, shape, 0) * group + (column // kinds) % group
    bell, slope = bell_of(periodic(row - site_of(column, 1), width))
    scale = -1.0 / KINETIC
    even = column % 2 == 0
    y_ref[0] = bell
    y_ref[1] = slope
    y_ref[2] = bell * jnp.where(even, scale * radial_strength, scale * polar_strength)
    y_ref[3] = bell * jnp.where(even, scale * polar_strength, 0.0)
    y_ref[4] = slope * jnp.where(even, scale * polar_strength, 0.0)


def vector_kernel(blocks, host_ref, here_ref, *refs):
    out_ref = refs[blocks]
    owned = refs[0].shape[1]
    host = host_ref[0]
    place = lax.broadcasted_iota(jnp.int32, (1, owned), 1)
    present = jnp.zeros((1, owned), jnp.float32)
    previous, beside = present, present
    for number in range(blocks):
        position = place + lax.rem(here_ref[0] + number, blocks) * owned
        before, now = refs[number][0:1, :], refs[number][1:2, :]
        present = present + jnp.where(position == host, now, 0.0)
        previous = previous + jnp.where(position == host, before, 0.0)
        beside = beside + jnp.where((position == host - 1) | (position == host + 1), now, 0.0)
    present = jnp.sum(present)
    out_ref[0] = present
    out_ref[1] = 2.0 * present - jnp.sum(previous) + courant_square * (jnp.sum(beside) - 2.0 * present)
    out_ref[2] = host.astype(jnp.float32)


def run_copies(pairs, sems):
    copies = [
        pltpu.make_async_copy(source, target, sems.at[number]) for number, (source, target) in enumerate(pairs)
    ]
    for copy in copies:
        copy.start()
    for copy in copies:
        copy.wait()


def pack_kernel(parts, share, count, first, source_ref, potential_ref, out_ref, sems):
    pairs = []
    for owner in range(parts):
        pairs.append((potential_ref, out_ref.at[owner, 2 * count]))
        for part in range(2):
            source = source_ref.at[part, pl.ds(owner * share + first, count)]
            pairs.append((source, out_ref.at[owner, pl.ds(part * count, count)]))
    run_copies(pairs, sems)


def pack_pieces_kernel(parts, share, count, first, here_ref, source_ref, *refs):
    pairs = []
    for step in range(parts):
        owner = lax.rem(here_ref[0] + step, parts)
        for part in range(2):
            source = source_ref.at[part, pl.ds(owner * share + first, count)]
            pairs.append((source, refs[step].at[pl.ds(part * count, count)]))
    run_copies(pairs, refs[parts])


def unpack_kernel(parts, share, count, first, piece_ref, *refs):
    out_ref, sems = refs[-2:]
    pairs = []
    for owner in range(parts):
        for part in range(2):
            target = out_ref.at[part, pl.ds(owner * share + first, count)]
            pairs.append((piece_ref.at[owner, pl.ds(part * count, count)], target))
    run_copies(pairs, sems)


def fold(values):
    while len(values) > 1:
        half = len(values) // 2
        values = [values[number] + values[number + half] for number in range(half)]
    return values[0]


def total_of_groups(value, kinds):
    for shift in (4, 2, 1):
        value = value + pltpu.roll(value, shift, 0)
    shift = LANES // 2
    while shift >= kinds:
        value = value + pltpu.roll(value, shift, 1)
        shift //= 2
    return value


def propagate_in_kernel(
    count, vector_value, field_ref, total_ref, potential_ref, tables, scratch, width, kinds
):
    near_ref, far_ref, zy_ref, xbell_ref, xslope_ref, y_ref = tables
    split_ref, first_ref, second_ref, partial_ref, drift_ref, spread_ref, diagonal_ref = scratch
    diagonal_ref[...] = (3.0 * SECOND[0] - 0.5 * vector_value * vector_value / KINETIC) - potential_ref[
        ...
    ] * (1.0 / KINETIC)
    block = ROWS
    slab = block * ROWS
    cell_rows = width * ROWS

    def split(planes):
        rows = planes.reshape(slab, LANES)
        high = rows.astype(jnp.bfloat16)
        low = (rows - high.astype(jnp.float32)).astype(jnp.bfloat16)
        return high, low

    def store_split(ref, number, start, planes):
        rows = pl.ds(number * cell_rows + start * ROWS, slab)
        high, low = split(planes)
        ref[rows, :LANES] = high
        ref[rows, LANES:] = low

    for number in range(2 * count):
        for start in range(0, width, block):
            store_split(split_ref, number, start, field_ref[number, start : start + block])

    def one_order(order, carry):
        inverse = jnp.where(order == 1, 1.0, jnp.where(order == 2, 0.5, jnp.where(order == 3, 1.0 / 3.0, 0.25)))
        step_scale = inverse * time_step
        kinetic = step_scale * KINETIC
        drift = step_scale * SLOPE * vector_value
        slopes = [drift * weight for weight in FIRST]
        outers = {}
        for orbital in range(count):
            rows = pl.ds(2 * orbital * cell_rows, 2 * cell_rows)
            first_ref[rows, :] = jnp.dot(split_ref[rows, :], near_ref[...], preferred_element_type=jnp.float32)
            for number in (2 * orbital, 2 * orbital + 1):
                bells = [jnp.zeros((ROWS, LANES), jnp.float32) for _ in range(2)]
                inclines = [jnp.zeros((ROWS, LANES), jnp.float32) for _ in range(2)]
                for plane in range(width):
                    inner = first_ref[pl.ds(number * cell_rows + plane * ROWS, ROWS), LANES:]
                    turn = plane % 2
                    bells[turn] = bells[turn] + inner * xbell_ref[plane]
                    inclines[turn] = inclines[turn] + inner * xslope_ref[plane]
                bell = bells[0] + bells[1]
                incline = inclines[0] + inclines[1]
                first = total_of_groups(bell * y_ref[0], kinds)
                second = total_of_groups(incline * y_ref[0], kinds)
                third = total_of_groups(bell * y_ref[1], kinds)
                outers[number] = (first * y_ref[2] + third * y_ref[4], second * y_ref[3])
        for orbital in range(count):
            rows = pl.ds(2 * orbital * cell_rows, 2 * cell_rows)
            second_ref[rows, :] = jnp.dot(split_ref[rows, :], far_ref[...], preferred_element_type=jnp.float32)
            for start in range(0, width, block):
                for number in (2 * orbital, 2 * orbital + 1):
                    near = {
                        plane: field_ref[number, plane % width] for plane in range(start - 4, start + block + 4)
                    }
                    for plane in range(start, start + block):
                        line = pl.ds(number * cell_rows + plane * ROWS, ROWS)
                        total = first_ref[line, :LANES]
                        total = total + pltpu.roll(second_ref[line, :LANES], ROWS - 1, 0)
                        total = total + pltpu.roll(second_ref[line, LANES:], 1, 0)
                        total = total + diagonal_ref[plane] * near[plane]
                        moved = None
                        for reach in range(1, 5):
                            ahead, behind = near[plane + reach], near[plane - reach]
                            total = total + SECOND[reach] * (ahead + behind)
                            term = slopes[reach - 1] * (ahead - behind)
                            moved = term if moved is None else moved + term
                        partial_ref[number, plane] = total
                        drift_ref[number, plane] = moved
        for orbital in range(count):
            real, imaginary = 2 * orbital, 2 * orbital + 1
            for start in range(0, width, block):
                xbell = xbell_ref[start : start + block]
                xslope = xslope_ref[start : start + block]
                for number in (real, imaginary):
                    spread = xbell * outers[number][0][None] + xslope * outers[number][1][None]
                    store_split(spread_ref, number, start, spread)
            rows = pl.ds(real * cell_rows, 2 * cell_rows)
            first_ref[rows, :LANES] = jnp.dot(
                spread_ref[rows, :], zy_ref[...], preferred_element_type=jnp.float32
            )
            for start in range(0, width, block):
                images = []
                for number in (real, imaginary):
                    rows = pl.ds(number * cell_rows + start * ROWS, slab)
                    images.append(
                        partial_ref[number, start : start + block]
                        + first_ref[rows, :LANES].reshape(block, ROWS, LANES)
                    )
                new = (
                    -kinetic * images[1] - drift_ref[real, start : start + block],
                    kinetic * images[0] - drift_ref[imaginary, start : start + block],
                )
                for number, value in zip((real, imaginary), new):
                    field_ref[number, start : start + block] = value
                    total_ref[number, start : start + block] += value
                    store_split(split_ref, number, start, value)
        return carry

    lax.fori_loop(1, ORDER + 1, one_order, 0)


def sums_in_kernel(count, total_ref, width):
    flow = jnp.zeros((ROWS, LANES), jnp.float32)
    density = jnp.zeros((ROWS, LANES), jnp.float32)
    for orbital in range(count):
        for plane in range(width):
            real = total_ref[2 * orbital, plane]
            imaginary = total_ref[2 * orbital + 1, plane]
            moved = None
            for reach in range(1, 5):
                ahead = total_ref[2 * orbital + 1, (plane + reach) % width]
                behind = total_ref[2 * orbital + 1, (plane - reach) % width]
                term = FIRST[reach - 1] * (ahead - behind)
                moved = term if moved is None else moved + term
            flow = flow + real * moved
            density = density + (real * real + imaginary * imaginary)
    return (2.0 * SLOPE) * flow, density


def first_kernel(parts, count, kinds, opening, scalar_ref, *refs):
    if opening:
        piece_ref, *tables, total_ref, out_ref, potential_ref, field_ref = refs[:11]
        scratch = refs[11:]
    else:
        here_ref, pieces, refs = refs[0], refs[1 : 1 + parts], refs[1 + parts :]
        potential_ref, *tables, sums_ref, total_ref, out_ref, field_ref = refs[:11]
        scratch = refs[11:]
    width = total_ref.shape[1]
    planes = width // parts
    for step in range(parts):
        if opening:
            piece, start = piece_ref.at[step], step * planes
        else:
            piece, start = pieces[step], lax.rem(here_ref[0] + parts - step, parts) * planes
        for index in range(planes):
            rows = pl.ds(index, ROWS, stride=planes)
            for orbital in range(count):
                for part in range(2):
                    value = piece[part * count + orbital, rows, :]
                    field_ref[2 * orbital + part, start + index] = value
                    total_ref[2 * orbital + part, start + index] = value
            if opening:
                potential_ref[start + index] = piece[2 * count, rows, :]
    propagate_in_kernel(
        count, scalar_ref[0], field_ref, total_ref, potential_ref, tables, scratch, width, kinds
    )
    flow, density = sums_in_kernel(count, total_ref, width)
    if not opening:
        flow, density = sums_ref[0] + flow, sums_ref[1] + density
    out_ref[0] = flow
    out_ref[1] = density


def second_kernel(parts, count, kinds, points, opening, closing, scalar_ref, *refs):
    if opening:
        seen, refs = refs[:parts], refs[parts:]
        first_sums_ref = seen[0]
    else:
        vector_ref, first_sums_ref, sums_ref, *refs = refs
    psi_ref, potential_ref, *tables = refs[:8]
    refs = refs[8:]
    piece_ref, *refs = refs
    if opening and not closing:
        vector_ref, *refs = refs
    out_ref, field_ref, total_ref = refs[:3]
    scratch = refs[3:]
    width = total_ref.shape[1]
    planes = width // parts
    if opening:
        flow = jnp.sum(fold([ref[0] for ref in seen]))
        density = jnp.sum(fold([ref[1] for ref in seen]))
        current = (flow + scalar_ref[0] * density) * (1.0 / points)
        vector_value = scalar_ref[1] - source_weight * current
        if not closing:
            vector_ref[0] = vector_value
    else:
        vector_value = vector_ref[0]
    field_ref[...] = psi_ref[...]
    total_ref[...] = psi_ref[...]
    propagate_in_kernel(
        count, vector_value, field_ref, total_ref, potential_ref, tables, scratch, width, kinds
    )
    for step in range(parts):
        piece, start = piece_ref.at[step], step * planes
        for index in range(planes):
            rows = pl.ds(index, ROWS, stride=planes)
            for orbital in range(count):
                for part in range(2):
                    piece[part * count + orbital, rows, :] = total_ref[2 * orbital + part, start + index]
    flow, density = sums_in_kernel(count, total_ref, width)
    if not opening:
        flow, density = sums_ref[0] + flow, sums_ref[1] + density
    if closing:
        row = lax.broadcasted_iota(jnp.int32, (ROWS, LANES), 0)
        own = first_sums_ref[0] + scalar_ref[0] * first_sums_ref[1]
        own = jnp.sum(own, axis=0, keepdims=True) * (1.0 / points)
        new = jnp.sum(flow + vector_value * density, axis=0, keepdims=True) * (1.0 / points)
        host = scalar_ref[2] * (1.0 / parts)
        out_ref[...] = jnp.where(row == 0, own, jnp.where(row == 1, new, host))
    else:
        out_ref[0] = flow
        out_ref[1] = density


def fields_kernel(blocks, owned, here_ref, window_ref, *refs):
    messages, out_ref = refs[:blocks], refs[blocks]
    edge = (LANES - owned) // 2
    length = blocks * owned
    position = lax.broadcasted_iota(jnp.int32, (1, LANES), 1) + (here_ref[0] * owned - edge)
    inside = (position >= 0) & (position < length)
    previous = jnp.where(inside, window_ref[0:1, :], 0.0)
    present = jnp.where(inside, window_ref[1:2, :], 0.0)
    place = position.astype(jnp.float32)
    for step in range(STEPS):
        source = jnp.zeros((1, LANES), jnp.float32)
        for message in messages:
            current = jnp.sum(message[step : step + 1, :])
            source = source + jnp.where(place == message[2:3, :], current, 0.0)
        beside = pltpu.roll(present, 1, 1) + pltpu.roll(present, LANES - 1, 1)
        following = (
            2.0 * present - previous + courant_square * (beside - 2.0 * present) - source_weight * source
        )
        previous, present = present, jnp.where(inside, following, 0.0)
    out_ref[0:1, :] = pltpu.roll(previous, LANES - edge, 1)[:, :owned]
    out_ref[1:2, :] = pltpu.roll(present, LANES - edge, 1)[:, :owned]


def vmem():
    return pl.BlockSpec(memory_space=pltpu.VMEM)


def smem():
    return pl.BlockSpec(memory_space=pltpu.SMEM)


def anywhere():
    return pl.BlockSpec(memory_space=pl.ANY)


def hbm():
    return pl.BlockSpec(memory_space=pltpu.HBM)


def float_array(*shape):
    return jax.ShapeDtypeStruct(shape, jnp.float32)


def exchanged(value, axes):
    return lax.all_to_all(value, axes, split_axis=0, concat_axis=0, tiled=True)


def shifted(value, axis_name, count, shift):
    return lax.ppermute(value, axis_name, [((index + shift) % count, index) for index in range(count)])


def per_device(parts, blocks, orbitals, local_potential, atom_sites, host_point, fields):
    norb = orbitals.shape[2]
    planes, points = local_potential.shape
    width = planes * parts
    share = norb // parts
    last_count = share // 2
    main_count = share - last_count
    owned = fields.shape[1]
    atoms = atom_sites.shape[0]
    kinds = 2 * atoms
    held = ROWS * planes
    total_points = float(width**3 * norb)
    here = lax.axis_index("grid").astype(jnp.int32)[None]
    block = lax.axis_index("macro").astype(jnp.int32)
    params = pltpu.CompilerParams(vmem_limit_bytes=LIMIT)
    whole_params = pltpu.CompilerParams(vmem_limit_bytes=WHOLE)

    def rows_of(value):
        lead = value.shape[:-2]
        value = value.reshape(*lead, planes, ROWS, LANES)
        return jnp.swapaxes(value, -3, -2).reshape(*lead, held, LANES)

    def planes_of(value):
        lead = value.shape[:-2]
        value = value.reshape(*lead, ROWS, planes, LANES)
        return jnp.swapaxes(value, -3, -2)

    source = rows_of(orbitals[0])
    packed = pl.pallas_call(
        functools.partial(pack_kernel, parts, share, main_count, 0),
        out_shape=float_array(parts, 2 * main_count + 1, held, LANES),
        in_specs=[hbm(), hbm()],
        out_specs=anywhere(),
        scratch_shapes=[pltpu.SemaphoreType.DMA((parts * 3,))],
        compiler_params=whole_params,
    )(source, rows_of(local_potential))
    main = exchanged(packed, "grid")
    fields, packed = lax.optimization_barrier((fields, packed))
    field_blocks = [fields] + [shifted(fields, "macro", blocks, step) for step in range(1, blocks)]

    tables = pl.pallas_call(
        functools.partial(tables_kernel, atoms),
        out_shape=[
            jax.ShapeDtypeStruct((2 * LANES, 2 * LANES), jnp.bfloat16),
            jax.ShapeDtypeStruct((2 * LANES, 2 * LANES), jnp.bfloat16),
            jax.ShapeDtypeStruct((2 * LANES, LANES), jnp.bfloat16),
            float_array(width, ROWS, LANES),
            float_array(width, ROWS, LANES),
            float_array(5, ROWS, LANES),
        ],
        in_specs=[smem(), vmem()],
        out_specs=[vmem()] * 6,
        compiler_params=params,
    )(atom_sites, stencil_weights(width))

    scalars = pl.pallas_call(
        functools.partial(vector_kernel, blocks),
        out_shape=float_array(3),
        in_specs=[smem(), smem()] + [vmem()] * blocks,
        out_specs=smem(),
        compiler_params=params,
    )(host_point, block[None], *field_blocks)

    source, scalars = lax.optimization_barrier((source, scalars))
    if last_count:
        last = pl.pallas_call(
            functools.partial(pack_pieces_kernel, parts, share, last_count, main_count),
            out_shape=[float_array(2 * last_count, held, LANES)] * parts,
            in_specs=[smem(), hbm()],
            out_specs=[anywhere()] * parts,
            scratch_shapes=[pltpu.SemaphoreType.DMA((parts * 2,))],
            compiler_params=whole_params,
        )(here, source)
        last = [last[0]] + [shifted(last[step], "grid", parts, -step) for step in range(1, parts)]
    edge = (LANES - owned) // 2
    window = jnp.concatenate(
        [field_blocks[-1][:, owned - edge :], field_blocks[0], field_blocks[1 % blocks][:, :edge]], axis=1
    )

    def micro_call(kernel, count, inputs, scalar_inputs, outputs, scalar_outputs, cells):
        rows = 2 * count * width * ROWS
        cell = pltpu.VMEM((2 * count, width, ROWS, LANES), jnp.float32)
        return pl.pallas_call(
            kernel,
            out_shape=outputs,
            in_specs=[smem() if number < scalar_inputs else vmem() for number in range(len(inputs))],
            out_specs=[smem() if number in scalar_outputs else vmem() for number in range(len(outputs))],
            scratch_shapes=[cell] * cells
            + [
                pltpu.VMEM((rows, 2 * LANES), jnp.bfloat16),
                pltpu.VMEM((rows, 2 * LANES), jnp.float32),
                pltpu.VMEM((rows, 2 * LANES), jnp.float32),
                cell,
                cell,
                pltpu.VMEM((rows, 2 * LANES), jnp.bfloat16),
                pltpu.VMEM((width, ROWS, LANES), jnp.float32),
            ],
            compiler_params=params,
            cost_estimate=pl.CostEstimate(
                flops=count * 3 * 2 * 512 * 256 * 256 * ORDER, bytes_accessed=4 * 1024 * 1024, transcendentals=0
            ),
        )(*inputs)

    def cells_of(count):
        return float_array(2 * count, width, ROWS, LANES)

    sums_shape = float_array(2, ROWS, LANES)
    main_psi, sums, potential = micro_call(
        functools.partial(first_kernel, parts, main_count, kinds, True),
        main_count,
        [scalars, main, *tables],
        1,
        [cells_of(main_count), sums_shape, float_array(width, ROWS, LANES)],
        (),
        1,
    )
    if last_count:
        last_psi, sums = micro_call(
            functools.partial(first_kernel, parts, last_count, kinds, False),
            last_count,
            [scalars, here, *last, potential, *tables, sums],
            2,
            [cells_of(last_count), sums_shape],
            (),
            1,
        )
    seen = [sums] + [shifted(sums, "grid", parts, step) for step in range(1, parts)]

    whole_shape = float_array(2, norb, held, LANES)
    message_shape = float_array(ROWS, LANES)
    result = []

    def give_back(pieces, count, first):
        return pl.pallas_call(
            functools.partial(unpack_kernel, parts, share, count, first),
            out_shape=whole_shape,
            in_specs=[anywhere()] + [hbm()] * len(result),
            out_specs=hbm(),
            scratch_shapes=[pltpu.SemaphoreType.DMA((parts * 2,))],
            input_output_aliases={1: 0} if result else {},
            compiler_params=params,
        )(exchanged(pieces, "grid"), *result)

    main_pieces, *rest = micro_call(
        functools.partial(second_kernel, parts, main_count, kinds, total_points, True, not last_count),
        main_count,
        [scalars, *seen, main_psi, potential, *tables],
        1,
        [float_array(parts, 2 * main_count, held, LANES)]
        + ([float_array(1), sums_shape] if last_count else [message_shape]),
        (1,) if last_count else (),
        2,
    )
    result = [give_back(main_pieces, main_count, 0)]
    message = rest[-1]
    if last_count:
        vector_value, second_sums = rest
        last_pieces, message = micro_call(
            functools.partial(second_kernel, parts, last_count, kinds, total_points, False, True),
            last_count,
            [scalars, vector_value, sums, second_sums, last_psi, potential, *tables],
            2,
            [float_array(parts, 2 * last_count, held, LANES), message_shape],
            (),
            2,
        )
        first_result, message = lax.optimization_barrier((result[0], message))
        result = [first_result]
        result = [give_back(last_pieces, last_count, main_count)]
    result = result[0]
    orbitals_out = planes_of(result).reshape(2, norb, planes, points)

    message = fold([message] + [shifted(message, "grid", parts, step) for step in range(1, parts)])
    messages = [message] + [shifted(message, "macro", blocks, step) for step in range(1, blocks)]
    fields_out = pl.pallas_call(
        functools.partial(fields_kernel, blocks, owned),
        out_shape=float_array(2, owned),
        in_specs=[smem()] + [vmem()] * (1 + blocks),
        out_specs=vmem(),
        compiler_params=params,
    )(block[None], window, *messages)
    return orbitals_out[None], fields_out


def solution(mesh):
    in_specs = (
        P("macro", None, None, "grid", None),
        P("grid", None),
        P(),
        P("macro"),
        P(None, "macro"),
    )
    out_specs = (P("macro", None, None, "grid", None), P(None, "macro"))
    return jax.shard_map(
        functools.partial(per_device, mesh.shape["grid"], mesh.shape["macro"]),
        mesh=mesh,
        in_specs=in_specs,
        out_specs=out_specs,
        check_vma=False,
    )
```

```python
import functools

import jax
import jax.numpy as jnp
import numpy as np
from jax import lax
from jax.experimental import pallas as pl
from jax.experimental.pallas import tpu as pltpu
from jax.sharding import PartitionSpec as P

ORDER = 4
STEPS = 2
spacing = 0.3206
time_step = 0.02
courant_square = 0.81
source_weight = 0.1
radial_strength = 0.3
polar_strength = -0.2
projector_width = 2.5

SECOND = (-14350.0, 8064.0, -1008.0, 128.0, -9.0)
FIRST = (672.0, -168.0, 32.0, -3.0)
KINETIC = 1.0 / (2.0 * 5040.0 * spacing * spacing)
SLOPE = 1.0 / (840.0 * spacing)

LANES = 128
ROWS = 8
LIMIT = 24 * 1024 * 1024
WHOLE = 60 * 1024 * 1024


def stencil_weights(width):
    group = LANES // width
    total = np.zeros((LANES, 3 * LANES), np.float32)
    for y_in in range(group):
        for z_in in range(width):
            for y_out in range(group):
                for part, step in enumerate((0, group, -group)):
                    reach = abs(step + y_in - y_out)
                    if 1 <= reach <= 4:
                        total[y_in * width + z_in, part * LANES + y_out * width + z_in] += SECOND[reach]
            for reach in range(1, 5):
                for z_out in ((z_in + reach) % width, (z_in - reach) % width):
                    total[y_in * width + z_in, y_in * width + z_out] += SECOND[reach]
    return jnp.asarray(np.concatenate([total, total], axis=0), jnp.bfloat16)


def periodic(distance, width):
    return ((distance + width // 2) & (width - 1)) - width // 2


def bell_of(offset):
    distance = offset.astype(jnp.float32)
    bell = jnp.exp(-0.5 * distance * distance / (projector_width * projector_width))
    return bell, distance / projector_width * bell


def tables_kernel(atoms, site_ref, stencil_ref, near_ref, far_ref, zy_ref, xbell_ref, xslope_ref, y_ref):
    width = xbell_ref.shape[0]
    kinds = 2 * atoms
    group = LANES // width

    def site_of(column, axis_number):
        atom = (column % kinds) // 2
        position = jnp.zeros(column.shape, jnp.int32)
        for number in range(atoms):
            position = jnp.where(atom == number, site_ref[number, axis_number], position)
        return position

    def factor(coordinate, column):
        bell, slope = bell_of(periodic(coordinate - site_of(column, 2), width))
        value = jnp.where(column % 2 == 0, bell, slope)
        high = value.astype(jnp.bfloat16).astype(jnp.float32)
        return jnp.where(column % LANES < LANES // 2, high, value - high)

    def groups_agree(point, column):
        return (point % LANES) // width == (column // kinds) % group

    shape = (2 * LANES, LANES)
    first = lax.broadcasted_iota(jnp.int32, shape, 0)
    last = lax.broadcasted_iota(jnp.int32, shape, 1)
    near_ref[:, :LANES] = stencil_ref[:, :LANES]
    far_ref[...] = stencil_ref[:, LANES:]
    inward = jnp.where(groups_agree(first, last), factor(first % width, last), 0.0)
    near_ref[:, LANES:] = inward.astype(jnp.bfloat16)
    outward = jnp.where(groups_agree(last, first), factor(last % width, first), 0.0)
    zy_ref[...] = outward.astype(jnp.bfloat16)

    shape = (width, ROWS, LANES)
    plane = lax.broadcasted_iota(jnp.int32, shape, 0)
    column = lax.broadcasted_iota(jnp.int32, shape, 2)
    bell, slope = bell_of(periodic(plane - site_of(column, 0), width))
    xbell_ref[...] = bell
    xslope_ref[...] = slope

    shape = (ROWS, LANES)
    column = lax.broadcasted_iota(jnp.int32, shape, 1)
    row = lax.broadcasted_iota(jnp.int32, shape, 0) * group + (column // kinds) % group
    bell, slope = bell_of(periodic(row - site_of(column, 1), width))
    scale = -1.0 / KINETIC
    even = column % 2 == 0
    y_ref[0] = bell
    y_ref[1] = slope
    y_ref[2] = bell * jnp.where(even, scale * radial_strength, scale * polar_strength)
    y_ref[3] = bell * jnp.where(even, scale * polar_strength, 0.0)
    y_ref[4] = slope * jnp.where(even, scale * polar_strength, 0.0)


def vector_kernel(blocks, host_ref, here_ref, *refs):
    out_ref = refs[blocks]
    owned = refs[0].shape[1]
    host = host_ref[0]
    place = lax.broadcasted_iota(jnp.int32, (1, owned), 1)
    present = jnp.zeros((1, owned), jnp.float32)
    previous, beside = present, present
    for number in range(blocks):
        position = place + lax.rem(here_ref[0] + number, blocks) * owned
        before, now = refs[number][0:1, :], refs[number][1:2, :]
        present = present + jnp.where(position == host, now, 0.0)
        previous = previous + jnp.where(position == host, before, 0.0)
        beside = beside + jnp.where((position == host - 1) | (position == host + 1), now, 0.0)
    present = jnp.sum(present)
    out_ref[0] = present
    out_ref[1] = 2.0 * present - jnp.sum(previous) + courant_square * (jnp.sum(beside) - 2.0 * present)
    out_ref[2] = host.astype(jnp.float32)


def run_copies(pairs, sems):
    copies = [
        pltpu.make_async_copy(source, target, sems.at[number]) for number, (source, target) in enumerate(pairs)
    ]
    for copy in copies:
        copy.start()
    for copy in copies:
        copy.wait()


def pack_kernel(parts, share, count, first, source_ref, potential_ref, out_ref, sems):
    pairs = []
    for owner in range(parts):
        pairs.append((potential_ref, out_ref.at[owner, 2 * count]))
        for part in range(2):
            source = source_ref.at[part, pl.ds(owner * share + first, count)]
            pairs.append((source, out_ref.at[owner, pl.ds(part * count, count)]))
    run_copies(pairs, sems)


def pack_pieces_kernel(parts, share, count, first, here_ref, source_ref, *refs):
    pairs = []
    for step in range(parts):
        owner = lax.rem(here_ref[0] + step, parts)
        for part in range(2):
            source = source_ref.at[part, pl.ds(owner * share + first, count)]
            pairs.append((source, refs[step].at[pl.ds(part * count, count)]))
    run_copies(pairs, refs[parts])


def unpack_kernel(parts, share, count, first, piece_ref, *refs):
    out_ref, sems = refs[-2:]
    pairs = []
    for owner in range(parts):
        for part in range(2):
            target = out_ref.at[part, pl.ds(owner * share + first, count)]
            pairs.append((piece_ref.at[owner, pl.ds(part * count, count)], target))
    run_copies(pairs, sems)


def fold(values):
    while len(values) > 1:
        half = len(values) // 2
        values = [values[number] + values[number + half] for number in range(half)]
    return values[0]


def total_of_groups(value, kinds):
    for shift in (4, 2, 1):
        value = value + pltpu.roll(value, shift, 0)
    shift = LANES // 2
    while shift >= kinds:
        value = value + pltpu.roll(value, shift, 1)
        shift //= 2
    return value


def propagate_in_kernel(
    count, vector_value, field_ref, total_ref, potential_ref, tables, scratch, width, kinds
):
    near_ref, far_ref, zy_ref, xbell_ref, xslope_ref, y_ref = tables
    split_ref, first_ref, second_ref, partial_ref, drift_ref, spread_ref, diagonal_ref = scratch
    diagonal_ref[...] = (3.0 * SECOND[0] - 0.5 * vector_value * vector_value / KINETIC) - potential_ref[
        ...
    ] * (1.0 / KINETIC)
    block = ROWS
    slab = block * ROWS
    cell_rows = width * ROWS

    def split(planes):
        rows = planes.reshape(slab, LANES)
        high = rows.astype(jnp.bfloat16)
        low = (rows - high.astype(jnp.float32)).astype(jnp.bfloat16)
        return high, low

    def store_split(ref, number, start, planes):
        rows = pl.ds(number * cell_rows + start * ROWS, slab)
        high, low = split(planes)
        ref[rows, :LANES] = high
        ref[rows, LANES:] = low

    for number in range(2 * count):
        for start in range(0, width, block):
            store_split(split_ref, number, start, field_ref[number, start : start + block])

    def one_order(order, carry):
        inverse = jnp.where(order == 1, 1.0, jnp.where(order == 2, 0.5, jnp.where(order == 3, 1.0 / 3.0, 0.25)))
        step_scale = inverse * time_step
        kinetic = step_scale * KINETIC
        drift = step_scale * SLOPE * vector_value
        slopes = [drift * weight for weight in FIRST]
        outers = {}
        for orbital in range(count):
            rows = pl.ds(2 * orbital * cell_rows, 2 * cell_rows)
            first_ref[rows, :] = jnp.dot(split_ref[rows, :], near_ref[...], preferred_element_type=jnp.float32)
            for number in (2 * orbital, 2 * orbital + 1):
                bells = [jnp.zeros((ROWS, LANES), jnp.float32) for _ in range(2)]
                inclines = [jnp.zeros((ROWS, LANES), jnp.float32) for _ in range(2)]
                for plane in range(width):
                    inner = first_ref[pl.ds(number * cell_rows + plane * ROWS, ROWS), LANES:]
                    turn = plane % 2
                    bells[turn] = bells[turn] + inner * xbell_ref[plane]
                    inclines[turn] = inclines[turn] + inner * xslope_ref[plane]
                bell = bells[0] + bells[1]
                incline = inclines[0] + inclines[1]
                first = total_of_groups(bell * y_ref[0], kinds)
                second = total_of_groups(incline * y_ref[0], kinds)
                third = total_of_groups(bell * y_ref[1], kinds)
                outers[number] = (first * y_ref[2] + third * y_ref[4], second * y_ref[3])
        for orbital in range(count):
            rows = pl.ds(2 * orbital * cell_rows, 2 * cell_rows)
            second_ref[rows, :] = jnp.dot(split_ref[rows, :], far_ref[...], preferred_element_type=jnp.float32)
            for start in range(0, width, block):
                for number in (2 * orbital, 2 * orbital + 1):
                    near = {
                        plane: field_ref[number, plane % width] for plane in range(start - 4, start + block + 4)
                    }
                    for plane in range(start, start + block):
                        line = pl.ds(number * cell_rows + plane * ROWS, ROWS)
                        total = first_ref[line, :LANES]
                        total = total + pltpu.roll(second_ref[line, :LANES], ROWS - 1, 0)
                        total = total + pltpu.roll(second_ref[line, LANES:], 1, 0)
                        total = total + diagonal_ref[plane] * near[plane]
                        moved = None
                        for reach in range(1, 5):
                            ahead, behind = near[plane + reach], near[plane - reach]
                            total = total + SECOND[reach] * (ahead + behind)
                            term = slopes[reach - 1] * (ahead - behind)
                            moved = term if moved is None else moved + term
                        partial_ref[number, plane] = total
                        drift_ref[number, plane] = moved
        for orbital in range(count):
            real, imaginary = 2 * orbital, 2 * orbital + 1
            for start in range(0, width, block):
                xbell = xbell_ref[start : start + block]
                xslope = xslope_ref[start : start + block]
                for number in (real, imaginary):
                    spread = xbell * outers[number][0][None] + xslope * outers[number][1][None]
                    store_split(spread_ref, number, start, spread)
            rows = pl.ds(real * cell_rows, 2 * cell_rows)
            first_ref[rows, :LANES] = jnp.dot(
                spread_ref[rows, :], zy_ref[...], preferred_element_type=jnp.float32
            )
            for start in range(0, width, block):
                images = []
                for number in (real, imaginary):
                    rows = pl.ds(number * cell_rows + start * ROWS, slab)
                    images.append(
                        partial_ref[number, start : start + block]
                        + first_ref[rows, :LANES].reshape(block, ROWS, LANES)
                    )
                new = (
                    -kinetic * images[1] - drift_ref[real, start : start + block],
                    kinetic * images[0] - drift_ref[imaginary, start : start + block],
                )
                for number, value in zip((real, imaginary), new):
                    field_ref[number, start : start + block] = value
                    total_ref[number, start : start + block] += value
                    store_split(split_ref, number, start, value)
        return carry

    lax.fori_loop(1, ORDER + 1, one_order, 0)


def sums_in_kernel(count, total_ref, width):
    flow = jnp.zeros((ROWS, LANES), jnp.float32)
    density = jnp.zeros((ROWS, LANES), jnp.float32)
    for orbital in range(count):
        for plane in range(width):
            real = total_ref[2 * orbital, plane]
            imaginary = total_ref[2 * orbital + 1, plane]
            moved = None
            for reach in range(1, 5):
                ahead = total_ref[2 * orbital + 1, (plane + reach) % width]
                behind = total_ref[2 * orbital + 1, (plane - reach) % width]
                term = FIRST[reach - 1] * (ahead - behind)
                moved = term if moved is None else moved + term
            flow = flow + real * moved
            density = density + (real * real + imaginary * imaginary)
    return (2.0 * SLOPE) * flow, density


def first_kernel(parts, count, kinds, opening, scalar_ref, *refs):
    if opening:
        piece_ref, *tables, total_ref, out_ref, potential_ref, field_ref = refs[:11]
        scratch = refs[11:]
    else:
        here_ref, pieces, refs = refs[0], refs[1 : 1 + parts], refs[1 + parts :]
        potential_ref, *tables, sums_ref, total_ref, out_ref, field_ref = refs[:11]
        scratch = refs[11:]
    width = total_ref.shape[1]
    planes = width // parts
    for step in range(parts):
        if opening:
            piece, start = piece_ref.at[step], step * planes
        else:
            piece, start = pieces[step], lax.rem(here_ref[0] + parts - step, parts) * planes
        for index in range(planes):
            rows = pl.ds(index, ROWS, stride=planes)
            for orbital in range(count):
                for part in range(2):
                    value = piece[part * count + orbital, rows, :]
                    field_ref[2 * orbital + part, start + index] = value
                    total_ref[2 * orbital + part, start + index] = value
            if opening:
                potential_ref[start + index] = piece[2 * count, rows, :]
    propagate_in_kernel(
        count, scalar_ref[0], field_ref, total_ref, potential_ref, tables, scratch, width, kinds
    )
    flow, density = sums_in_kernel(count, total_ref, width)
    if not opening:
        flow, density = sums_ref[0] + flow, sums_ref[1] + density
    out_ref[0] = flow
    out_ref[1] = density


def second_kernel(parts, count, kinds, points, opening, closing, scalar_ref, *refs):
    if opening:
        seen, refs = refs[:parts], refs[parts:]
        first_sums_ref = seen[0]
    else:
        vector_ref, first_sums_ref, sums_ref, *refs = refs
    psi_ref, potential_ref, *tables = refs[:8]
    refs = refs[8:]
    piece_ref, *refs = refs
    if opening and not closing:
        vector_ref, *refs = refs
    out_ref, field_ref, total_ref = refs[:3]
    scratch = refs[3:]
    width = total_ref.shape[1]
    planes = width // parts
    if opening:
        flow = jnp.sum(fold([ref[0] for ref in seen]))
        density = jnp.sum(fold([ref[1] for ref in seen]))
        current = (flow + scalar_ref[0] * density) * (1.0 / points)
        vector_value = scalar_ref[1] - source_weight * current
        if not closing:
            vector_ref[0] = vector_value
    else:
        vector_value = vector_ref[0]
    field_ref[...] = psi_ref[...]
    total_ref[...] = psi_ref[...]
    propagate_in_kernel(
        count, vector_value, field_ref, total_ref, potential_ref, tables, scratch, width, kinds
    )
    for step in range(parts):
        piece, start = piece_ref.at[step], step * planes
        for index in range(planes):
            rows = pl.ds(index, ROWS, stride=planes)
            for orbital in range(count):
                for part in range(2):
                    piece[part * count + orbital, rows, :] = total_ref[2 * orbital + part, start + index]
    flow, density = sums_in_kernel(count, total_ref, width)
    if not opening:
        flow, density = sums_ref[0] + flow, sums_ref[1] + density
    if closing:
        row = lax.broadcasted_iota(jnp.int32, (ROWS, LANES), 0)
        own = first_sums_ref[0] + scalar_ref[0] * first_sums_ref[1]
        own = jnp.sum(own, axis=0, keepdims=True) * (1.0 / points)
        new = jnp.sum(flow + vector_value * density, axis=0, keepdims=True) * (1.0 / points)
        host = scalar_ref[2] * (1.0 / parts)
        out_ref[...] = jnp.where(row == 0, own, jnp.where(row == 1, new, host))
    else:
        out_ref[0] = flow
        out_ref[1] = density


def fields_kernel(blocks, owned, here_ref, window_ref, *refs):
    messages, out_ref = refs[:blocks], refs[blocks]
    edge = (LANES - owned) // 2
    length = blocks * owned
    position = lax.broadcasted_iota(jnp.int32, (1, LANES), 1) + (here_ref[0] * owned - edge)
    inside = (position >= 0) & (position < length)
    previous = jnp.where(inside, window_ref[0:1, :], 0.0)
    present = jnp.where(inside, window_ref[1:2, :], 0.0)
    place = position.astype(jnp.float32)
    for step in range(STEPS):
        source = jnp.zeros((1, LANES), jnp.float32)
        for message in messages:
            current = jnp.sum(message[step : step + 1, :])
            source = source + jnp.where(place == message[2:3, :], current, 0.0)
        beside = pltpu.roll(present, 1, 1) + pltpu.roll(present, LANES - 1, 1)
        following = (
            2.0 * present - previous + courant_square * (beside - 2.0 * present) - source_weight * source
        )
        previous, present = present, jnp.where(inside, following, 0.0)
    out_ref[0:1, :] = pltpu.roll(previous, LANES - edge, 1)[:, :owned]
    out_ref[1:2, :] = pltpu.roll(present, LANES - edge, 1)[:, :owned]


def vmem():
    return pl.BlockSpec(memory_space=pltpu.VMEM)


def smem():
    return pl.BlockSpec(memory_space=pltpu.SMEM)


def anywhere():
    return pl.BlockSpec(memory_space=pl.ANY)


def hbm():
    return pl.BlockSpec(memory_space=pltpu.HBM)


def float_array(*shape):
    return jax.ShapeDtypeStruct(shape, jnp.float32)


def exchanged(value, axes):
    return lax.all_to_all(value, axes, split_axis=0, concat_axis=0, tiled=True)


def shifted(value, axis_name, count, shift):
    return lax.ppermute(value, axis_name, [((index + shift) % count, index) for index in range(count)])


def per_device(parts, blocks, orbitals, local_potential, atom_sites, host_point, fields):
    norb = orbitals.shape[2]
    planes, points = local_potential.shape
    width = planes * parts
    share = norb // parts
    last_count = share // 2
    main_count = share - last_count
    owned = fields.shape[1]
    atoms = atom_sites.shape[0]
    kinds = 2 * atoms
    held = ROWS * planes
    total_points = float(width**3 * norb)
    here = lax.axis_index("grid").astype(jnp.int32)[None]
    block = lax.axis_index("macro").astype(jnp.int32)
    params = pltpu.CompilerParams(vmem_limit_bytes=LIMIT)
    whole_params = pltpu.CompilerParams(vmem_limit_bytes=WHOLE)

    def rows_of(value):
        lead = value.shape[:-2]
        value = value.reshape(*lead, planes, ROWS, LANES)
        return jnp.swapaxes(value, -3, -2).reshape(*lead, held, LANES)

    def planes_of(value):
        lead = value.shape[:-2]
        value = value.reshape(*lead, ROWS, planes, LANES)
        return jnp.swapaxes(value, -3, -2)

    source = rows_of(orbitals[0])
    packed = pl.pallas_call(
        functools.partial(pack_kernel, parts, share, main_count, 0),
        out_shape=float_array(parts, 2 * main_count + 1, held, LANES),
        in_specs=[hbm(), hbm()],
        out_specs=vmem(),
        scratch_shapes=[pltpu.SemaphoreType.DMA((parts * 3,))],
        compiler_params=whole_params,
    )(source, rows_of(local_potential))
    main = exchanged(packed, "grid")
    fields, packed = lax.optimization_barrier((fields, packed))
    field_blocks = [fields] + [shifted(fields, "macro", blocks, step) for step in range(1, blocks)]

    tables = pl.pallas_call(
        functools.partial(tables_kernel, atoms),
        out_shape=[
            jax.ShapeDtypeStruct((2 * LANES, 2 * LANES), jnp.bfloat16),
            jax.ShapeDtypeStruct((2 * LANES, 2 * LANES), jnp.bfloat16),
            jax.ShapeDtypeStruct((2 * LANES, LANES), jnp.bfloat16),
            float_array(width, ROWS, LANES),
            float_array(width, ROWS, LANES),
            float_array(5, ROWS, LANES),
        ],
        in_specs=[smem(), vmem()],
        out_specs=[vmem()] * 6,
        compiler_params=params,
    )(atom_sites, stencil_weights(width))

    scalars = pl.pallas_call(
        functools.partial(vector_kernel, blocks),
        out_shape=float_array(3),
        in_specs=[smem(), smem()] + [vmem()] * blocks,
        out_specs=smem(),
        compiler_params=params,
    )(host_point, block[None], *field_blocks)

    source, scalars = lax.optimization_barrier((source, scalars))
    if last_count:
        last = pl.pallas_call(
            functools.partial(pack_pieces_kernel, parts, share, last_count, main_count),
            out_shape=[float_array(2 * last_count, held, LANES)] * parts,
            in_specs=[smem(), hbm()],
            out_specs=[vmem()] * parts,
            scratch_shapes=[pltpu.SemaphoreType.DMA((parts * 2,))],
            compiler_params=whole_params,
        )(here, source)
        last = [last[0]] + [shifted(last[step], "grid", parts, -step) for step in range(1, parts)]
    edge = (LANES - owned) // 2
    window = jnp.concatenate(
        [field_blocks[-1][:, owned - edge :], field_blocks[0], field_blocks[1 % blocks][:, :edge]], axis=1
    )

    def micro_call(kernel, count, inputs, scalar_inputs, outputs, scalar_outputs, cells):
        rows = 2 * count * width * ROWS
        cell = pltpu.VMEM((2 * count, width, ROWS, LANES), jnp.float32)
        return pl.pallas_call(
            kernel,
            out_shape=outputs,
            in_specs=[smem() if number < scalar_inputs else vmem() for number in range(len(inputs))],
            out_specs=[smem() if number in scalar_outputs else vmem() for number in range(len(outputs))],
            scratch_shapes=[cell] * cells
            + [
                pltpu.VMEM((rows, 2 * LANES), jnp.bfloat16),
                pltpu.VMEM((rows, 2 * LANES), jnp.float32),
                pltpu.VMEM((rows, 2 * LANES), jnp.float32),
                cell,
                cell,
                pltpu.VMEM((rows, 2 * LANES), jnp.bfloat16),
                pltpu.VMEM((width, ROWS, LANES), jnp.float32),
            ],
            compiler_params=params,
            cost_estimate=pl.CostEstimate(
                flops=count * 3 * 2 * 512 * 256 * 256 * ORDER, bytes_accessed=4 * 1024 * 1024, transcendentals=0
            ),
        )(*inputs)

    def cells_of(count):
        return float_array(2 * count, width, ROWS, LANES)

    sums_shape = float_array(2, ROWS, LANES)
    main_psi, sums, potential = micro_call(
        functools.partial(first_kernel, parts, main_count, kinds, True),
        main_count,
        [scalars, main, *tables],
        1,
        [cells_of(main_count), sums_shape, float_array(width, ROWS, LANES)],
        (),
        1,
    )
    if last_count:
        last_psi, sums = micro_call(
            functools.partial(first_kernel, parts, last_count, kinds, False),
            last_count,
            [scalars, here, *last, potential, *tables, sums],
            2,
            [cells_of(last_count), sums_shape],
            (),
            1,
        )
    seen = [sums] + [shifted(sums, "grid", parts, step) for step in range(1, parts)]

    whole_shape = float_array(2, norb, held, LANES)
    message_shape = float_array(ROWS, LANES)
    result = []

    def give_back(pieces, count, first):
        return pl.pallas_call(
            functools.partial(unpack_kernel, parts, share, count, first),
            out_shape=whole_shape,
            in_specs=[anywhere()] + [hbm()] * len(result),
            out_specs=hbm(),
            scratch_shapes=[pltpu.SemaphoreType.DMA((parts * 2,))],
            input_output_aliases={1: 0} if result else {},
            compiler_params=params,
        )(exchanged(pieces, "grid"), *result)

    main_pieces, *rest = micro_call(
        functools.partial(second_kernel, parts, main_count, kinds, total_points, True, not last_count),
        main_count,
        [scalars, *seen, main_psi, potential, *tables],
        1,
        [float_array(parts, 2 * main_count, held, LANES)]
        + ([float_array(1), sums_shape] if last_count else [message_shape]),
        (1,) if last_count else (),
        2,
    )
    result = [give_back(main_pieces, main_count, 0)]
    message = rest[-1]
    if last_count:
        vector_value, second_sums = rest
        last_pieces, message = micro_call(
            functools.partial(second_kernel, parts, last_count, kinds, total_points, False, True),
            last_count,
            [scalars, vector_value, sums, second_sums, last_psi, potential, *tables],
            2,
            [float_array(parts, 2 * last_count, held, LANES), message_shape],
            (),
            2,
        )
        first_result, message = lax.optimization_barrier((result[0], message))
        result = [first_result]
        result = [give_back(last_pieces, last_count, main_count)]
    result = result[0]
    orbitals_out = planes_of(result).reshape(2, norb, planes, points)

    message = fold([message] + [shifted(message, "grid", parts, step) for step in range(1, parts)])
    messages = [message] + [shifted(message, "macro", blocks, step) for step in range(1, blocks)]
    fields_out = pl.pallas_call(
        functools.partial(fields_kernel, blocks, owned),
        out_shape=float_array(2, owned),
        in_specs=[smem()] + [vmem()] * (1 + blocks),
        out_specs=vmem(),
        compiler_params=params,
    )(block[None], window, *messages)
    return orbitals_out[None], fields_out


def solution(mesh):
    in_specs = (
        P("macro", None, None, "grid", None),
        P("grid", None),
        P(),
        P("macro"),
        P(None, "macro"),
    )
    out_specs = (P("macro", None, None, "grid", None), P(None, "macro"))
    return jax.shard_map(
        functools.partial(per_device, mesh.shape["grid"], mesh.shape["macro"]),
        mesh=mesh,
        in_specs=in_specs,
        out_specs=out_specs,
        check_vma=False,
    )
```

```python
import functools

import jax
import jax.numpy as jnp
import numpy as np
from jax import lax
from jax.experimental import pallas as pl
from jax.experimental.pallas import tpu as pltpu
from jax.sharding import PartitionSpec as P

ORDER = 4
STEPS = 2
spacing = 0.3206
time_step = 0.02
courant_square = 0.81
source_weight = 0.1
radial_strength = 0.3
polar_strength = -0.2
projector_width = 2.5

SECOND = (-14350.0, 8064.0, -1008.0, 128.0, -9.0)
FIRST = (672.0, -168.0, 32.0, -3.0)
KINETIC = 1.0 / (2.0 * 5040.0 * spacing * spacing)
SLOPE = 1.0 / (840.0 * spacing)

LANES = 128
ROWS = 8
LIMIT = 24 * 1024 * 1024
WHOLE = 60 * 1024 * 1024


def stencil_weights(width):
    group = LANES // width
    total = np.zeros((LANES, 3 * LANES), np.float32)
    for y_in in range(group):
        for z_in in range(width):
            for y_out in range(group):
                for part, step in enumerate((0, group, -group)):
                    reach = abs(step + y_in - y_out)
                    if 1 <= reach <= 4:
                        total[y_in * width + z_in, part * LANES + y_out * width + z_in] += SECOND[reach]
            for reach in range(1, 5):
                for z_out in ((z_in + reach) % width, (z_in - reach) % width):
                    total[y_in * width + z_in, y_in * width + z_out] += SECOND[reach]
    return jnp.asarray(np.concatenate([total, total], axis=0), jnp.bfloat16)


def periodic(distance, width):
    return ((distance + width // 2) & (width - 1)) - width // 2


def bell_of(offset):
    distance = offset.astype(jnp.float32)
    bell = jnp.exp(-0.5 * distance * distance / (projector_width * projector_width))
    return bell, distance / projector_width * bell


def tables_kernel(atoms, site_ref, stencil_ref, near_ref, far_ref, zy_ref, xbell_ref, xslope_ref, y_ref):
    width = xbell_ref.shape[0]
    kinds = 2 * atoms
    group = LANES // width

    def site_of(column, axis_number):
        atom = (column % kinds) // 2
        position = jnp.zeros(column.shape, jnp.int32)
        for number in range(atoms):
            position = jnp.where(atom == number, site_ref[number, axis_number], position)
        return position

    def factor(coordinate, column):
        bell, slope = bell_of(periodic(coordinate - site_of(column, 2), width))
        value = jnp.where(column % 2 == 0, bell, slope)
        high = value.astype(jnp.bfloat16).astype(jnp.float32)
        return jnp.where(column % LANES < LANES // 2, high, value - high)

    def groups_agree(point, column):
        return (point % LANES) // width == (column // kinds) % group

    shape = (2 * LANES, LANES)
    first = lax.broadcasted_iota(jnp.int32, shape, 0)
    last = lax.broadcasted_iota(jnp.int32, shape, 1)
    near_ref[:, :LANES] = stencil_ref[:, :LANES]
    far_ref[...] = stencil_ref[:, LANES:]
    inward = jnp.where(groups_agree(first, last), factor(first % width, last), 0.0)
    near_ref[:, LANES:] = inward.astype(jnp.bfloat16)
    outward = jnp.where(groups_agree(last, first), factor(last % width, first), 0.0)
    zy_ref[...] = outward.astype(jnp.bfloat16)

    shape = (width, ROWS, LANES)
    plane = lax.broadcasted_iota(jnp.int32, shape, 0)
    column = lax.broadcasted_iota(jnp.int32, shape, 2)
    bell, slope = bell_of(periodic(plane - site_of(column, 0), width))
    xbell_ref[...] = bell
    xslope_ref[...] = slope

    shape = (ROWS, LANES)
    column = lax.broadcasted_iota(jnp.int32, shape, 1)
    row = lax.broadcasted_iota(jnp.int32, shape, 0) * group + (column // kinds) % group
    bell, slope = bell_of(periodic(row - site_of(column, 1), width))
    scale = -1.0 / KINETIC
    even = column % 2 == 0
    y_ref[0] = bell
    y_ref[1] = slope
    y_ref[2] = bell * jnp.where(even, scale * radial_strength, scale * polar_strength)
    y_ref[3] = bell * jnp.where(even, scale * polar_strength, 0.0)
    y_ref[4] = slope * jnp.where(even, scale * polar_strength, 0.0)


def vector_kernel(blocks, host_ref, here_ref, *refs):
    out_ref = refs[blocks]
    owned = refs[0].shape[1]
    host = host_ref[0]
    place = lax.broadcasted_iota(jnp.int32, (1, owned), 1)
    present = jnp.zeros((1, owned), jnp.float32)
    previous, beside = present, present
    for number in range(blocks):
        position = place + lax.rem(here_ref[0] + number, blocks) * owned
        before, now = refs[number][0:1, :], refs[number][1:2, :]
        present = present + jnp.where(position == host, now, 0.0)
        previous = previous + jnp.where(position == host, before, 0.0)
        beside = beside + jnp.where((position == host - 1) | (position == host + 1), now, 0.0)
    present = jnp.sum(present)
    out_ref[0] = present
    out_ref[1] = 2.0 * present - jnp.sum(previous) + courant_square * (jnp.sum(beside) - 2.0 * present)
    out_ref[2] = host.astype(jnp.float32)


def run_copies(pairs, sems):
    copies = [
        pltpu.make_async_copy(source, target, sems.at[number]) for number, (source, target) in enumerate(pairs)
    ]
    for copy in copies:
        copy.start()
    for copy in copies:
        copy.wait()


def pack_kernel(parts, share, count, first, source_ref, potential_ref, out_ref, sems):
    pairs = []
    for owner in range(parts):
        pairs.append((potential_ref, out_ref.at[owner, 2 * count]))
        for part in range(2):
            source = source_ref.at[part, pl.ds(owner * share + first, count)]
            pairs.append((source, out_ref.at[owner, pl.ds(part * count, count)]))
    run_copies(pairs, sems)


def pack_pieces_kernel(parts, share, count, first, here_ref, source_ref, *refs):
    pairs = []
    for step in range(parts):
        owner = lax.rem(here_ref[0] + step, parts)
        for part in range(2):
            source = source_ref.at[part, pl.ds(owner * share + first, count)]
            pairs.append((source, refs[step].at[pl.ds(part * count, count)]))
    run_copies(pairs, refs[parts])


def unpack_kernel(parts, share, count, first, piece_ref, *refs):
    out_ref, sems = refs[-2:]
    pairs = []
    for owner in range(parts):
        for part in range(2):
            target = out_ref.at[part, pl.ds(owner * share + first, count)]
            pairs.append((piece_ref.at[owner, pl.ds(part * count, count)], target))
    run_copies(pairs, sems)


def fold(values):
    while len(values) > 1:
        half = len(values) // 2
        values = [values[number] + values[number + half] for number in range(half)]
    return values[0]


def total_of_groups(value, kinds):
    for shift in (4, 2, 1):
        value = value + pltpu.roll(value, shift, 0)
    shift = LANES // 2
    while shift >= kinds:
        value = value + pltpu.roll(value, shift, 1)
        shift //= 2
    return value


def propagate_in_kernel(
    count, vector_value, field_ref, total_ref, potential_ref, tables, scratch, width, kinds
):
    near_ref, far_ref, zy_ref, xbell_ref, xslope_ref, y_ref = tables
    split_ref, first_ref, second_ref, partial_ref, drift_ref, spread_ref, diagonal_ref = scratch
    diagonal_ref[...] = (3.0 * SECOND[0] - 0.5 * vector_value * vector_value / KINETIC) - potential_ref[
        ...
    ] * (1.0 / KINETIC)
    block = ROWS
    slab = block * ROWS
    cell_rows = width * ROWS

    def split(planes):
        rows = planes.reshape(slab, LANES)
        high = rows.astype(jnp.bfloat16)
        low = (rows - high.astype(jnp.float32)).astype(jnp.bfloat16)
        return high, low

    def store_split(ref, number, start, planes):
        rows = pl.ds(number * cell_rows + start * ROWS, slab)
        high, low = split(planes)
        ref[rows, :LANES] = high
        ref[rows, LANES:] = low

    for number in range(2 * count):
        for start in range(0, width, block):
            store_split(split_ref, number, start, field_ref[number, start : start + block])

    def one_order(order, carry):
        inverse = jnp.where(order == 1, 1.0, jnp.where(order == 2, 0.5, jnp.where(order == 3, 1.0 / 3.0, 0.25)))
        step_scale = inverse * time_step
        kinetic = step_scale * KINETIC
        drift = step_scale * SLOPE * vector_value
        slopes = [drift * weight for weight in FIRST]
        outers = {}
        for orbital in range(count):
            rows = pl.ds(2 * orbital * cell_rows, 2 * cell_rows)
            first_ref[rows, :] = jnp.dot(split_ref[rows, :], near_ref[...], preferred_element_type=jnp.float32)
            for number in (2 * orbital, 2 * orbital + 1):
                bells = [jnp.zeros((ROWS, LANES), jnp.float32) for _ in range(2)]
                inclines = [jnp.zeros((ROWS, LANES), jnp.float32) for _ in range(2)]
                for plane in range(width):
                    inner = first_ref[pl.ds(number * cell_rows + plane * ROWS, ROWS), LANES:]
                    turn = plane % 2
                    bells[turn] = bells[turn] + inner * xbell_ref[plane]
                    inclines[turn] = inclines[turn] + inner * xslope_ref[plane]
                bell = bells[0] + bells[1]
                incline = inclines[0] + inclines[1]
                first = total_of_groups(bell * y_ref[0], kinds)
                second = total_of_groups(incline * y_ref[0], kinds)
                third = total_of_groups(bell * y_ref[1], kinds)
                outers[number] = (first * y_ref[2] + third * y_ref[4], second * y_ref[3])
        for orbital in range(count):
            rows = pl.ds(2 * orbital * cell_rows, 2 * cell_rows)
            second_ref[rows, :] = jnp.dot(split_ref[rows, :], far_ref[...], preferred_element_type=jnp.float32)
            for start in range(0, width, block):
                for number in (2 * orbital, 2 * orbital + 1):
                    near = {
                        plane: field_ref[number, plane % width] for plane in range(start - 4, start + block + 4)
                    }
                    for plane in range(start, start + block):
                        line = pl.ds(number * cell_rows + plane * ROWS, ROWS)
                        total = first_ref[line, :LANES]
                        total = total + pltpu.roll(second_ref[line, :LANES], ROWS - 1, 0)
                        total = total + pltpu.roll(second_ref[line, LANES:], 1, 0)
                        total = total + diagonal_ref[plane] * near[plane]
                        moved = None
                        for reach in range(1, 5):
                            ahead, behind = near[plane + reach], near[plane - reach]
                            total = total + SECOND[reach] * (ahead + behind)
                            term = slopes[reach - 1] * (ahead - behind)
                            moved = term if moved is None else moved + term
                        partial_ref[number, plane] = total
                        drift_ref[number, plane] = moved
        for orbital in range(count):
            real, imaginary = 2 * orbital, 2 * orbital + 1
            for start in range(0, width, block):
                xbell = xbell_ref[start : start + block]
                xslope = xslope_ref[start : start + block]
                for number in (real, imaginary):
                    spread = xbell * outers[number][0][None] + xslope * outers[number][1][None]
                    store_split(spread_ref, number, start, spread)
            rows = pl.ds(real * cell_rows, 2 * cell_rows)
            first_ref[rows, :LANES] = jnp.dot(
                spread_ref[rows, :], zy_ref[...], preferred_element_type=jnp.float32
            )
            for start in range(0, width, block):
                images = []
                for number in (real, imaginary):
                    rows = pl.ds(number * cell_rows + start * ROWS, slab)
                    images.append(
                        partial_ref[number, start : start + block]
                        + first_ref[rows, :LANES].reshape(block, ROWS, LANES)
                    )
                new = (
                    -kinetic * images[1] - drift_ref[real, start : start + block],
                    kinetic * images[0] - drift_ref[imaginary, start : start + block],
                )
                for number, value in zip((real, imaginary), new):
                    field_ref[number, start : start + block] = value
                    total_ref[number, start : start + block] += value
                    store_split(split_ref, number, start, value)
        return carry

    lax.fori_loop(1, ORDER + 1, one_order, 0)


def sums_in_kernel(count, total_ref, width):
    flow = jnp.zeros((ROWS, LANES), jnp.float32)
    density = jnp.zeros((ROWS, LANES), jnp.float32)
    for orbital in range(count):
        for plane in range(width):
            real = total_ref[2 * orbital, plane]
            imaginary = total_ref[2 * orbital + 1, plane]
            moved = None
            for reach in range(1, 5):
                ahead = total_ref[2 * orbital + 1, (plane + reach) % width]
                behind = total_ref[2 * orbital + 1, (plane - reach) % width]
                term = FIRST[reach - 1] * (ahead - behind)
                moved = term if moved is None else moved + term
            flow = flow + real * moved
            density = density + (real * real + imaginary * imaginary)
    return (2.0 * SLOPE) * flow, density


def first_kernel(parts, count, kinds, opening, scalar_ref, *refs):
    if opening:
        piece_ref, *tables, total_ref, out_ref, potential_ref, field_ref = refs[:11]
        scratch = refs[11:]
    else:
        here_ref, pieces, refs = refs[0], refs[1 : 1 + parts], refs[1 + parts :]
        potential_ref, *tables, sums_ref, total_ref, out_ref, field_ref = refs[:11]
        scratch = refs[11:]
    width = total_ref.shape[1]
    planes = width // parts
    for step in range(parts):
        if opening:
            piece, start = piece_ref.at[step], step * planes
        else:
            piece, start = pieces[step], lax.rem(here_ref[0] + parts - step, parts) * planes
        for index in range(planes):
            rows = pl.ds(index, ROWS, stride=planes)
            for orbital in range(count):
                for part in range(2):
                    value = piece[part * count + orbital, rows, :]
                    field_ref[2 * orbital + part, start + index] = value
                    total_ref[2 * orbital + part, start + index] = value
            if opening:
                potential_ref[start + index] = piece[2 * count, rows, :]
    propagate_in_kernel(
        count, scalar_ref[0], field_ref, total_ref, potential_ref, tables, scratch, width, kinds
    )
    flow, density = sums_in_kernel(count, total_ref, width)
    if not opening:
        flow, density = sums_ref[0] + flow, sums_ref[1] + density
    out_ref[0] = flow
    out_ref[1] = density


def second_kernel(parts, count, kinds, points, opening, closing, scalar_ref, *refs):
    if opening:
        seen, refs = refs[:parts], refs[parts:]
        first_sums_ref = seen[0]
    else:
        vector_ref, first_sums_ref, sums_ref, *refs = refs
    psi_ref, potential_ref, *tables = refs[:8]
    refs = refs[8:]
    piece_ref, *refs = refs
    if opening and not closing:
        vector_ref, *refs = refs
    out_ref, field_ref, total_ref = refs[:3]
    scratch = refs[3:]
    width = total_ref.shape[1]
    planes = width // parts
    if opening:
        flow = jnp.sum(fold([ref[0] for ref in seen]))
        density = jnp.sum(fold([ref[1] for ref in seen]))
        current = (flow + scalar_ref[0] * density) * (1.0 / points)
        vector_value = scalar_ref[1] - source_weight * current
        if not closing:
            vector_ref[0] = vector_value
    else:
        vector_value = vector_ref[0]
    field_ref[...] = psi_ref[...]
    total_ref[...] = psi_ref[...]
    propagate_in_kernel(
        count, vector_value, field_ref, total_ref, potential_ref, tables, scratch, width, kinds
    )
    for step in range(parts):
        piece, start = piece_ref.at[step], step * planes
        for index in range(planes):
            rows = pl.ds(index, ROWS, stride=planes)
            for orbital in range(count):
                for part in range(2):
                    piece[part * count + orbital, rows, :] = total_ref[2 * orbital + part, start + index]
    flow, density = sums_in_kernel(count, total_ref, width)
    if not opening:
        flow, density = sums_ref[0] + flow, sums_ref[1] + density
    if closing:
        row = lax.broadcasted_iota(jnp.int32, (ROWS, LANES), 0)
        own = first_sums_ref[0] + scalar_ref[0] * first_sums_ref[1]
        own = jnp.sum(own, axis=0, keepdims=True) * (1.0 / points)
        new = jnp.sum(flow + vector_value * density, axis=0, keepdims=True) * (1.0 / points)
        host = scalar_ref[2] * (1.0 / parts)
        out_ref[...] = jnp.where(row == 0, own, jnp.where(row == 1, new, host))
    else:
        out_ref[0] = flow
        out_ref[1] = density


def fields_kernel(blocks, owned, here_ref, window_ref, *refs):
    messages, out_ref = refs[:blocks], refs[blocks]
    edge = (LANES - owned) // 2
    length = blocks * owned
    position = lax.broadcasted_iota(jnp.int32, (1, LANES), 1) + (here_ref[0] * owned - edge)
    inside = (position >= 0) & (position < length)
    previous = jnp.where(inside, window_ref[0:1, :], 0.0)
    present = jnp.where(inside, window_ref[1:2, :], 0.0)
    place = position.astype(jnp.float32)
    for step in range(STEPS):
        source = jnp.zeros((1, LANES), jnp.float32)
        for message in messages:
            current = jnp.sum(message[step : step + 1, :])
            source = source + jnp.where(place == message[2:3, :], current, 0.0)
        beside = pltpu.roll(present, 1, 1) + pltpu.roll(present, LANES - 1, 1)
        following = (
            2.0 * present - previous + courant_square * (beside - 2.0 * present) - source_weight * source
        )
        previous, present = present, jnp.where(inside, following, 0.0)
    out_ref[0:1, :] = pltpu.roll(previous, LANES - edge, 1)[:, :owned]
    out_ref[1:2, :] = pltpu.roll(present, LANES - edge, 1)[:, :owned]


def vmem():
    return pl.BlockSpec(memory_space=pltpu.VMEM)


def smem():
    return pl.BlockSpec(memory_space=pltpu.SMEM)


def anywhere():
    return pl.BlockSpec(memory_space=pl.ANY)


def hbm():
    return pl.BlockSpec(memory_space=pltpu.HBM)


def float_array(*shape):
    return jax.ShapeDtypeStruct(shape, jnp.float32)


def exchanged(value, axes):
    return lax.all_to_all(value, axes, split_axis=0, concat_axis=0, tiled=True)


def shifted(value, axis_name, count, shift):
    return lax.ppermute(value, axis_name, [((index + shift) % count, index) for index in range(count)])


def per_device(parts, blocks, orbitals, local_potential, atom_sites, host_point, fields):
    norb = orbitals.shape[2]
    planes, points = local_potential.shape
    width = planes * parts
    share = norb // parts
    last_count = share // 2
    main_count = share - last_count
    owned = fields.shape[1]
    atoms = atom_sites.shape[0]
    kinds = 2 * atoms
    held = ROWS * planes
    total_points = float(width**3 * norb)
    here = lax.axis_index("grid").astype(jnp.int32)[None]
    block = lax.axis_index("macro").astype(jnp.int32)
    params = pltpu.CompilerParams(vmem_limit_bytes=LIMIT)
    whole_params = pltpu.CompilerParams(vmem_limit_bytes=WHOLE)

    def rows_of(value):
        lead = value.shape[:-2]
        value = value.reshape(*lead, planes, ROWS, LANES)
        return jnp.swapaxes(value, -3, -2).reshape(*lead, held, LANES)

    def planes_of(value):
        lead = value.shape[:-2]
        value = value.reshape(*lead, ROWS, planes, LANES)
        return jnp.swapaxes(value, -3, -2)

    source = rows_of(orbitals[0])
    packed = pl.pallas_call(
        functools.partial(pack_kernel, parts, share, main_count, 0),
        out_shape=float_array(parts, 2 * main_count + 1, held, LANES),
        in_specs=[hbm(), hbm()],
        out_specs=vmem(),
        scratch_shapes=[pltpu.SemaphoreType.DMA((parts * 3,))],
        compiler_params=whole_params,
    )(source, rows_of(local_potential))
    main = exchanged(packed, "grid")
    fields, packed = lax.optimization_barrier((fields, packed))
    field_blocks = [fields] + [shifted(fields, "macro", blocks, step) for step in range(1, blocks)]

    tables = pl.pallas_call(
        functools.partial(tables_kernel, atoms),
        out_shape=[
            jax.ShapeDtypeStruct((2 * LANES, 2 * LANES), jnp.bfloat16),
            jax.ShapeDtypeStruct((2 * LANES, 2 * LANES), jnp.bfloat16),
            jax.ShapeDtypeStruct((2 * LANES, LANES), jnp.bfloat16),
            float_array(width, ROWS, LANES),
            float_array(width, ROWS, LANES),
            float_array(5, ROWS, LANES),
        ],
        in_specs=[smem(), vmem()],
        out_specs=[vmem()] * 6,
        compiler_params=params,
    )(atom_sites, stencil_weights(width))

    scalars = pl.pallas_call(
        functools.partial(vector_kernel, blocks),
        out_shape=float_array(3),
        in_specs=[smem(), smem()] + [vmem()] * blocks,
        out_specs=smem(),
        compiler_params=params,
    )(host_point, block[None], *field_blocks)

    source, scalars = lax.optimization_barrier((source, scalars))
    if last_count:
        last = pl.pallas_call(
            functools.partial(pack_pieces_kernel, parts, share, last_count, main_count),
            out_shape=[float_array(2 * last_count, held, LANES)] * parts,
            in_specs=[smem(), hbm()],
            out_specs=[vmem()] * parts,
            scratch_shapes=[pltpu.SemaphoreType.DMA((parts * 2,))],
            compiler_params=whole_params,
        )(here, source)
        last = [last[0]] + [shifted(last[step], "grid", parts, -step) for step in range(1, parts)]
    edge = (LANES - owned) // 2
    window = jnp.concatenate(
        [field_blocks[-1][:, owned - edge :], field_blocks[0], field_blocks[1 % blocks][:, :edge]], axis=1
    )

    def micro_call(kernel, count, inputs, scalar_inputs, outputs, scalar_outputs, cells):
        rows = 2 * count * width * ROWS
        cell = pltpu.VMEM((2 * count, width, ROWS, LANES), jnp.float32)
        return pl.pallas_call(
            kernel,
            out_shape=outputs,
            in_specs=[smem() if number < scalar_inputs else vmem() for number in range(len(inputs))],
            out_specs=[smem() if number in scalar_outputs else vmem() for number in range(len(outputs))],
            scratch_shapes=[cell] * cells
            + [
                pltpu.VMEM((rows, 2 * LANES), jnp.bfloat16),
                pltpu.VMEM((rows, 2 * LANES), jnp.float32),
                pltpu.VMEM((rows, 2 * LANES), jnp.float32),
                cell,
                cell,
                pltpu.VMEM((rows, 2 * LANES), jnp.bfloat16),
                pltpu.VMEM((width, ROWS, LANES), jnp.float32),
            ],
            compiler_params=params,
            cost_estimate=pl.CostEstimate(
                flops=count * 3 * 2 * 512 * 256 * 256 * ORDER, bytes_accessed=4 * 1024 * 1024, transcendentals=0
            ),
        )(*inputs)

    def cells_of(count):
        return float_array(2 * count, width, ROWS, LANES)

    sums_shape = float_array(2, ROWS, LANES)
    main_psi, sums, potential = micro_call(
        functools.partial(first_kernel, parts, main_count, kinds, True),
        main_count,
        [scalars, main, *tables],
        1,
        [cells_of(main_count), sums_shape, float_array(width, ROWS, LANES)],
        (),
        1,
    )
    if last_count:
        last_psi, sums = micro_call(
            functools.partial(first_kernel, parts, last_count, kinds, False),
            last_count,
            [scalars, here, *last, potential, *tables, sums],
            2,
            [cells_of(last_count), sums_shape],
            (),
            1,
        )
    seen = [sums] + [shifted(sums, "grid", parts, step) for step in range(1, parts)]

    whole_shape = float_array(2, norb, held, LANES)
    message_shape = float_array(ROWS, LANES)
    result = []

    def give_back(pieces, count, first):
        return pl.pallas_call(
            functools.partial(unpack_kernel, parts, share, count, first),
            out_shape=whole_shape,
            in_specs=[anywhere()] + [hbm()] * len(result),
            out_specs=hbm(),
            scratch_shapes=[pltpu.SemaphoreType.DMA((parts * 2,))],
            input_output_aliases={1: 0} if result else {},
            compiler_params=params,
        )(exchanged(pieces, "grid"), *result)

    main_pieces, *rest = micro_call(
        functools.partial(second_kernel, parts, main_count, kinds, total_points, True, not last_count),
        main_count,
        [scalars, *seen, main_psi, potential, *tables],
        1,
        [float_array(parts, 2 * main_count, held, LANES)]
        + ([float_array(1), sums_shape] if last_count else [message_shape]),
        (1,) if last_count else (),
        2,
    )
    result = [give_back(main_pieces, main_count, 0)]
    message = rest[-1]
    if last_count:
        vector_value, second_sums = rest
        last_pieces, message = micro_call(
            functools.partial(second_kernel, parts, last_count, kinds, total_points, False, True),
            last_count,
            [scalars, vector_value, sums, second_sums, last_psi, potential, *tables],
            2,
            [float_array(parts, 2 * last_count, held, LANES), message_shape],
            (),
            2,
        )
    message = fold([message] + [shifted(message, "grid", parts, step) for step in range(1, parts)])
    if last_count:
        last_pieces, message = lax.optimization_barrier((last_pieces, message))
        result = [give_back(last_pieces, last_count, main_count)]
    result = result[0]
    orbitals_out = planes_of(result).reshape(2, norb, planes, points)

    messages = [message] + [shifted(message, "macro", blocks, step) for step in range(1, blocks)]
    fields_out = pl.pallas_call(
        functools.partial(fields_kernel, blocks, owned),
        out_shape=float_array(2, owned),
        in_specs=[smem()] + [vmem()] * (1 + blocks),
        out_specs=vmem(),
        compiler_params=params,
    )(block[None], window, *messages)
    return orbitals_out[None], fields_out


def solution(mesh):
    in_specs = (
        P("macro", None, None, "grid", None),
        P("grid", None),
        P(),
        P("macro"),
        P(None, "macro"),
    )
    out_specs = (P("macro", None, None, "grid", None), P(None, "macro"))
    return jax.shard_map(
        functools.partial(per_device, mesh.shape["grid"], mesh.shape["macro"]),
        mesh=mesh,
        in_specs=in_specs,
        out_specs=out_specs,
        check_vma=False,
    )
```

```python
import functools

import jax
import jax.numpy as jnp
import numpy as np
from jax import lax
from jax.experimental import pallas as pl
from jax.experimental.pallas import tpu as pltpu
from jax.sharding import PartitionSpec as P

ORDER = 4
STEPS = 2
spacing = 0.3206
time_step = 0.02
courant_square = 0.81
source_weight = 0.1
radial_strength = 0.3
polar_strength = -0.2
projector_width = 2.5

SECOND = (-14350.0, 8064.0, -1008.0, 128.0, -9.0)
FIRST = (672.0, -168.0, 32.0, -3.0)
KINETIC = 1.0 / (2.0 * 5040.0 * spacing * spacing)
SLOPE = 1.0 / (840.0 * spacing)

LANES = 128
ROWS = 8
LIMIT = 24 * 1024 * 1024
WHOLE = 60 * 1024 * 1024


def stencil_weights(width):
    group = LANES // width
    total = np.zeros((LANES, 3 * LANES), np.float32)
    for y_in in range(group):
        for z_in in range(width):
            for y_out in range(group):
                for part, step in enumerate((0, group, -group)):
                    reach = abs(step + y_in - y_out)
                    if 1 <= reach <= 4:
                        total[y_in * width + z_in, part * LANES + y_out * width + z_in] += SECOND[reach]
            for reach in range(1, 5):
                for z_out in ((z_in + reach) % width, (z_in - reach) % width):
                    total[y_in * width + z_in, y_in * width + z_out] += SECOND[reach]
    return jnp.asarray(np.concatenate([total, total], axis=0), jnp.bfloat16)


def periodic(distance, width):
    return ((distance + width // 2) & (width - 1)) - width // 2


def bell_of(offset):
    distance = offset.astype(jnp.float32)
    bell = jnp.exp(-0.5 * distance * distance / (projector_width * projector_width))
    return bell, distance / projector_width * bell


def tables_kernel(atoms, site_ref, stencil_ref, near_ref, far_ref, zy_ref, xbell_ref, xslope_ref, y_ref):
    width = xbell_ref.shape[0]
    kinds = 2 * atoms
    group = LANES // width

    def site_of(column, axis_number):
        atom = (column % kinds) // 2
        position = jnp.zeros(column.shape, jnp.int32)
        for number in range(atoms):
            position = jnp.where(atom == number, site_ref[number, axis_number], position)
        return position

    def factor(coordinate, column):
        bell, slope = bell_of(periodic(coordinate - site_of(column, 2), width))
        value = jnp.where(column % 2 == 0, bell, slope)
        high = value.astype(jnp.bfloat16).astype(jnp.float32)
        return jnp.where(column % LANES < LANES // 2, high, value - high)

    def groups_agree(point, column):
        return (point % LANES) // width == (column // kinds) % group

    shape = (2 * LANES, LANES)
    first = lax.broadcasted_iota(jnp.int32, shape, 0)
    last = lax.broadcasted_iota(jnp.int32, shape, 1)
    near_ref[:, :LANES] = stencil_ref[:, :LANES]
    far_ref[...] = stencil_ref[:, LANES:]
    inward = jnp.where(groups_agree(first, last), factor(first % width, last), 0.0)
    near_ref[:, LANES:] = inward.astype(jnp.bfloat16)
    outward = jnp.where(groups_agree(last, first), factor(last % width, first), 0.0)
    zy_ref[...] = outward.astype(jnp.bfloat16)

    shape = (width, ROWS, LANES)
    plane = lax.broadcasted_iota(jnp.int32, shape, 0)
    column = lax.broadcasted_iota(jnp.int32, shape, 2)
    bell, slope = bell_of(periodic(plane - site_of(column, 0), width))
    xbell_ref[...] = bell
    xslope_ref[...] = slope

    shape = (ROWS, LANES)
    column = lax.broadcasted_iota(jnp.int32, shape, 1)
    row = lax.broadcasted_iota(jnp.int32, shape, 0) * group + (column // kinds) % group
    bell, slope = bell_of(periodic(row - site_of(column, 1), width))
    scale = -1.0 / KINETIC
    even = column % 2 == 0
    y_ref[0] = bell
    y_ref[1] = slope
    y_ref[2] = bell * jnp.where(even, scale * radial_strength, scale * polar_strength)
    y_ref[3] = bell * jnp.where(even, scale * polar_strength, 0.0)
    y_ref[4] = slope * jnp.where(even, scale * polar_strength, 0.0)


def vector_kernel(blocks, host_ref, here_ref, *refs):
    out_ref = refs[blocks]
    owned = refs[0].shape[1]
    host = host_ref[0]
    place = lax.broadcasted_iota(jnp.int32, (1, owned), 1)
    present = jnp.zeros((1, owned), jnp.float32)
    previous, beside = present, present
    for number in range(blocks):
        position = place + lax.rem(here_ref[0] + number, blocks) * owned
        before, now = refs[number][0:1, :], refs[number][1:2, :]
        present = present + jnp.where(position == host, now, 0.0)
        previous = previous + jnp.where(position == host, before, 0.0)
        beside = beside + jnp.where((position == host - 1) | (position == host + 1), now, 0.0)
    present = jnp.sum(present)
    out_ref[0] = present
    out_ref[1] = 2.0 * present - jnp.sum(previous) + courant_square * (jnp.sum(beside) - 2.0 * present)
    out_ref[2] = host.astype(jnp.float32)


def run_copies(pairs, sems):
    copies = [
        pltpu.make_async_copy(source, target, sems.at[number]) for number, (source, target) in enumerate(pairs)
    ]
    for copy in copies:
        copy.start()
    for copy in copies:
        copy.wait()


def pack_kernel(parts, share, count, first, source_ref, potential_ref, out_ref, sems):
    pairs = []
    for owner in range(parts):
        pairs.append((potential_ref, out_ref.at[owner, 2 * count]))
        for part in range(2):
            source = source_ref.at[part, pl.ds(owner * share + first, count)]
            pairs.append((source, out_ref.at[owner, pl.ds(part * count, count)]))
    run_copies(pairs, sems)


def pack_pieces_kernel(parts, share, count, first, here_ref, source_ref, *refs):
    pairs = []
    for step in range(parts):
        owner = lax.rem(here_ref[0] + step, parts)
        for part in range(2):
            source = source_ref.at[part, pl.ds(owner * share + first, count)]
            pairs.append((source, refs[step].at[pl.ds(part * count, count)]))
    run_copies(pairs, refs[parts])


def unpack_kernel(parts, share, count, first, piece_ref, *refs):
    out_ref, sems = refs[-2:]
    pairs = []
    for owner in range(parts):
        for part in range(2):
            target = out_ref.at[part, pl.ds(owner * share + first, count)]
            pairs.append((piece_ref.at[owner, pl.ds(part * count, count)], target))
    run_copies(pairs, sems)


def fold(values):
    while len(values) > 1:
        half = len(values) // 2
        values = [values[number] + values[number + half] for number in range(half)]
    return values[0]


def total_of_groups(value, kinds):
    for shift in (4, 2, 1):
        value = value + pltpu.roll(value, shift, 0)
    shift = LANES // 2
    while shift >= kinds:
        value = value + pltpu.roll(value, shift, 1)
        shift //= 2
    return value


def propagate_in_kernel(
    count, vector_value, source_ref, field_ref, total_ref, potential_ref, tables, scratch, width, kinds
):
    near_ref, far_ref, zy_ref, xbell_ref, xslope_ref, y_ref = tables
    split_ref, first_ref, second_ref, partial_ref, spread_ref, diagonal_ref = scratch
    diagonal_ref[...] = (3.0 * SECOND[0] - 0.5 * vector_value * vector_value / KINETIC) - potential_ref[
        ...
    ] * (1.0 / KINETIC)
    block = ROWS
    slab = block * ROWS
    cell_rows = width * ROWS

    def split(planes):
        rows = planes.reshape(slab, LANES)
        high = rows.astype(jnp.bfloat16)
        low = (rows - high.astype(jnp.float32)).astype(jnp.bfloat16)
        return high, low

    def store_split(ref, number, start, planes):
        rows = pl.ds(number * cell_rows + start * ROWS, slab)
        high, low = split(planes)
        ref[rows, :LANES] = high
        ref[rows, LANES:] = low

    for number in range(2 * count):
        for start in range(0, width, block):
            planes = source_ref[number, start : start + block]
            store_split(split_ref, number, start, planes)
            if source_ref is not field_ref:
                field_ref[number, start : start + block] = planes
                total_ref[number, start : start + block] = planes

    def one_order(order, carry):
        inverse = jnp.where(order == 1, 1.0, jnp.where(order == 2, 0.5, jnp.where(order == 3, 1.0 / 3.0, 0.25)))
        step_scale = inverse * time_step
        kinetic = step_scale * KINETIC
        drift = step_scale * SLOPE * vector_value
        slopes = [drift * weight for weight in FIRST]
        outers = {}
        for orbital in range(count):
            rows = pl.ds(2 * orbital * cell_rows, 2 * cell_rows)
            first_ref[rows, :] = jnp.dot(split_ref[rows, :], near_ref[...], preferred_element_type=jnp.float32)
            for number in (2 * orbital, 2 * orbital + 1):
                bells = [jnp.zeros((ROWS, LANES), jnp.float32) for _ in range(2)]
                inclines = [jnp.zeros((ROWS, LANES), jnp.float32) for _ in range(2)]
                for plane in range(width):
                    inner = first_ref[pl.ds(number * cell_rows + plane * ROWS, ROWS), LANES:]
                    turn = plane % 2
                    bells[turn] = bells[turn] + inner * xbell_ref[plane]
                    inclines[turn] = inclines[turn] + inner * xslope_ref[plane]
                bell = bells[0] + bells[1]
                incline = inclines[0] + inclines[1]
                first = total_of_groups(bell * y_ref[0], kinds)
                second = total_of_groups(incline * y_ref[0], kinds)
                third = total_of_groups(bell * y_ref[1], kinds)
                outers[number] = (kinetic * (first * y_ref[2] + third * y_ref[4]), kinetic * (second * y_ref[3]))
        for orbital in range(count):
            rows = pl.ds(2 * orbital * cell_rows, 2 * cell_rows)
            second_ref[rows, :] = jnp.dot(split_ref[rows, :], far_ref[...], preferred_element_type=jnp.float32)
            for start in range(0, width, block):
                near = [
                    {plane: field_ref[number, plane % width] for plane in range(start - 4, start + block + 4)}
                    for number in (2 * orbital, 2 * orbital + 1)
                ]
                for plane in range(start, start + block):
                    images, drifts = [], []
                    for part in range(2):
                        line = pl.ds((2 * orbital + part) * cell_rows + plane * ROWS, ROWS)
                        total = first_ref[line, :LANES]
                        total = total + pltpu.roll(second_ref[line, :LANES], ROWS - 1, 0)
                        total = total + pltpu.roll(second_ref[line, LANES:], 1, 0)
                        total = total + diagonal_ref[plane] * near[part][plane]
                        moved = None
                        for reach in range(1, 5):
                            ahead, behind = near[part][plane + reach], near[part][plane - reach]
                            total = total + SECOND[reach] * (ahead + behind)
                            term = slopes[reach - 1] * (ahead - behind)
                            moved = term if moved is None else moved + term
                        images.append(kinetic * total)
                        drifts.append(moved)
                    partial_ref[2 * orbital, plane] = -images[1] - drifts[0]
                    partial_ref[2 * orbital + 1, plane] = images[0] - drifts[1]
        for orbital in range(count):
            real, imaginary = 2 * orbital, 2 * orbital + 1
            for start in range(0, width, block):
                xbell = xbell_ref[start : start + block]
                xslope = xslope_ref[start : start + block]
                for number in (real, imaginary):
                    spread = xbell * outers[number][0][None] + xslope * outers[number][1][None]
                    store_split(spread_ref, number, start, spread)
            rows = pl.ds(real * cell_rows, 2 * cell_rows)
            first_ref[rows, :LANES] = jnp.dot(
                spread_ref[rows, :], zy_ref[...], preferred_element_type=jnp.float32
            )
            for start in range(0, width, block):
                spreads = [
                    first_ref[pl.ds(number * cell_rows + start * ROWS, slab), :LANES].reshape(block, ROWS, LANES)
                    for number in (real, imaginary)
                ]
                new = (
                    partial_ref[real, start : start + block] - spreads[1],
                    partial_ref[imaginary, start : start + block] + spreads[0],
                )
                for number, value in zip((real, imaginary), new):
                    field_ref[number, start : start + block] = value
                    total_ref[number, start : start + block] += value
                    store_split(split_ref, number, start, value)
        return carry

    lax.fori_loop(1, ORDER + 1, one_order, 0)


def sums_in_kernel(count, total_ref, width):
    flow = jnp.zeros((ROWS, LANES), jnp.float32)
    density = jnp.zeros((ROWS, LANES), jnp.float32)
    block = ROWS
    for orbital in range(count):
        for start in range(0, width, block):
            near = {
                plane: total_ref[2 * orbital + 1, plane % width] for plane in range(start - 4, start + block + 4)
            }
            for plane in range(start, start + block):
                real, imaginary = total_ref[2 * orbital, plane], near[plane]
                moved = None
                for reach in range(1, 5):
                    term = FIRST[reach - 1] * (near[plane + reach] - near[plane - reach])
                    moved = term if moved is None else moved + term
                flow = flow + real * moved
                density = density + (real * real + imaginary * imaginary)
    return (2.0 * SLOPE) * flow, density


def first_kernel(parts, count, kinds, opening, scalar_ref, *refs):
    if opening:
        piece_ref, *tables, total_ref, out_ref, potential_ref, field_ref = refs[:11]
        scratch = refs[11:]
    else:
        here_ref, pieces, refs = refs[0], refs[1 : 1 + parts], refs[1 + parts :]
        potential_ref, *tables, sums_ref, total_ref, out_ref, field_ref = refs[:11]
        scratch = refs[11:]
    width = total_ref.shape[1]
    planes = width // parts
    for step in range(parts):
        if opening:
            piece, start = piece_ref.at[step], step * planes
        else:
            piece, start = pieces[step], lax.rem(here_ref[0] + parts - step, parts) * planes
        for index in range(planes):
            rows = pl.ds(index, ROWS, stride=planes)
            for orbital in range(count):
                for part in range(2):
                    value = piece[part * count + orbital, rows, :]
                    field_ref[2 * orbital + part, start + index] = value
                    total_ref[2 * orbital + part, start + index] = value
            if opening:
                potential_ref[start + index] = piece[2 * count, rows, :]
    propagate_in_kernel(
        count, scalar_ref[0], field_ref, field_ref, total_ref, potential_ref, tables, scratch, width, kinds
    )
    flow, density = sums_in_kernel(count, total_ref, width)
    if not opening:
        flow, density = sums_ref[0] + flow, sums_ref[1] + density
    out_ref[0] = flow
    out_ref[1] = density


def second_kernel(parts, count, kinds, points, opening, closing, scalar_ref, *refs):
    if opening:
        seen, refs = refs[:parts], refs[parts:]
        first_sums_ref = seen[0]
    else:
        vector_ref, first_sums_ref, sums_ref, *refs = refs
    psi_ref, potential_ref, *tables = refs[:8]
    refs = refs[8:]
    piece_ref, *refs = refs
    if opening and not closing:
        vector_ref, *refs = refs
    out_ref, field_ref, total_ref = refs[:3]
    scratch = refs[3:]
    width = total_ref.shape[1]
    planes = width // parts
    if opening:
        flow = jnp.sum(fold([ref[0] for ref in seen]))
        density = jnp.sum(fold([ref[1] for ref in seen]))
        current = (flow + scalar_ref[0] * density) * (1.0 / points)
        vector_value = scalar_ref[1] - source_weight * current
        if not closing:
            vector_ref[0] = vector_value
    else:
        vector_value = vector_ref[0]
    propagate_in_kernel(
        count, vector_value, psi_ref, field_ref, total_ref, potential_ref, tables, scratch, width, kinds
    )
    for step in range(parts):
        piece, start = piece_ref.at[step], step * planes
        for index in range(planes):
            rows = pl.ds(index, ROWS, stride=planes)
            for orbital in range(count):
                for part in range(2):
                    piece[part * count + orbital, rows, :] = total_ref[2 * orbital + part, start + index]
    flow, density = sums_in_kernel(count, total_ref, width)
    if not opening:
        flow, density = sums_ref[0] + flow, sums_ref[1] + density
    if closing:
        row = lax.broadcasted_iota(jnp.int32, (ROWS, LANES), 0)
        own = first_sums_ref[0] + scalar_ref[0] * first_sums_ref[1]
        own = jnp.sum(own, axis=0, keepdims=True) * (1.0 / points)
        new = jnp.sum(flow + vector_value * density, axis=0, keepdims=True) * (1.0 / points)
        host = scalar_ref[2] * (1.0 / parts)
        out_ref[...] = jnp.where(row == 0, own, jnp.where(row == 1, new, host))
    else:
        out_ref[0] = flow
        out_ref[1] = density


def fields_kernel(blocks, owned, here_ref, window_ref, *refs):
    messages, out_ref = refs[:blocks], refs[blocks]
    edge = (LANES - owned) // 2
    length = blocks * owned
    position = lax.broadcasted_iota(jnp.int32, (1, LANES), 1) + (here_ref[0] * owned - edge)
    inside = (position >= 0) & (position < length)
    previous = jnp.where(inside, window_ref[0:1, :], 0.0)
    present = jnp.where(inside, window_ref[1:2, :], 0.0)
    place = position.astype(jnp.float32)
    for step in range(STEPS):
        source = jnp.zeros((1, LANES), jnp.float32)
        for message in messages:
            current = jnp.sum(message[step : step + 1, :])
            source = source + jnp.where(place == message[2:3, :], current, 0.0)
        beside = pltpu.roll(present, 1, 1) + pltpu.roll(present, LANES - 1, 1)
        following = (
            2.0 * present - previous + courant_square * (beside - 2.0 * present) - source_weight * source
        )
        previous, present = present, jnp.where(inside, following, 0.0)
    out_ref[0:1, :] = pltpu.roll(previous, LANES - edge, 1)[:, :owned]
    out_ref[1:2, :] = pltpu.roll(present, LANES - edge, 1)[:, :owned]


def vmem():
    return pl.BlockSpec(memory_space=pltpu.VMEM)


def smem():
    return pl.BlockSpec(memory_space=pltpu.SMEM)


def anywhere():
    return pl.BlockSpec(memory_space=pl.ANY)


def hbm():
    return pl.BlockSpec(memory_space=pltpu.HBM)


def float_array(*shape):
    return jax.ShapeDtypeStruct(shape, jnp.float32)


def exchanged(value, axes):
    return lax.all_to_all(value, axes, split_axis=0, concat_axis=0, tiled=True)


def shifted(value, axis_name, count, shift):
    return lax.ppermute(value, axis_name, [((index + shift) % count, index) for index in range(count)])


def per_device(parts, blocks, orbitals, local_potential, atom_sites, host_point, fields):
    norb = orbitals.shape[2]
    planes, points = local_potential.shape
    width = planes * parts
    share = norb // parts
    last_count = share // 2
    main_count = share - last_count
    owned = fields.shape[1]
    atoms = atom_sites.shape[0]
    kinds = 2 * atoms
    held = ROWS * planes
    total_points = float(width**3 * norb)
    here = lax.axis_index("grid").astype(jnp.int32)[None]
    block = lax.axis_index("macro").astype(jnp.int32)
    params = pltpu.CompilerParams(vmem_limit_bytes=LIMIT)
    whole_params = pltpu.CompilerParams(vmem_limit_bytes=WHOLE)

    def rows_of(value):
        lead = value.shape[:-2]
        value = value.reshape(*lead, planes, ROWS, LANES)
        return jnp.swapaxes(value, -3, -2).reshape(*lead, held, LANES)

    def planes_of(value):
        lead = value.shape[:-2]
        value = value.reshape(*lead, ROWS, planes, LANES)
        return jnp.swapaxes(value, -3, -2)

    source = rows_of(orbitals[0])
    packed = pl.pallas_call(
        functools.partial(pack_kernel, parts, share, main_count, 0),
        out_shape=float_array(parts, 2 * main_count + 1, held, LANES),
        in_specs=[hbm(), hbm()],
        out_specs=vmem(),
        scratch_shapes=[pltpu.SemaphoreType.DMA((parts * 3,))],
        compiler_params=whole_params,
    )(source, rows_of(local_potential))
    main = exchanged(packed, "grid")
    fields, packed = lax.optimization_barrier((fields, packed))
    field_blocks = [fields] + [shifted(fields, "macro", blocks, step) for step in range(1, blocks)]

    tables = pl.pallas_call(
        functools.partial(tables_kernel, atoms),
        out_shape=[
            jax.ShapeDtypeStruct((2 * LANES, 2 * LANES), jnp.bfloat16),
            jax.ShapeDtypeStruct((2 * LANES, 2 * LANES), jnp.bfloat16),
            jax.ShapeDtypeStruct((2 * LANES, LANES), jnp.bfloat16),
            float_array(width, ROWS, LANES),
            float_array(width, ROWS, LANES),
            float_array(5, ROWS, LANES),
        ],
        in_specs=[smem(), vmem()],
        out_specs=[vmem()] * 6,
        compiler_params=params,
    )(atom_sites, stencil_weights(width))

    scalars = pl.pallas_call(
        functools.partial(vector_kernel, blocks),
        out_shape=float_array(3),
        in_specs=[smem(), smem()] + [vmem()] * blocks,
        out_specs=smem(),
        compiler_params=params,
    )(host_point, block[None], *field_blocks)

    source, scalars = lax.optimization_barrier((source, scalars))
    if last_count:
        last = pl.pallas_call(
            functools.partial(pack_pieces_kernel, parts, share, last_count, main_count),
            out_shape=[float_array(2 * last_count, held, LANES)] * parts,
            in_specs=[smem(), hbm()],
            out_specs=[vmem()] * parts,
            scratch_shapes=[pltpu.SemaphoreType.DMA((parts * 2,))],
            compiler_params=whole_params,
        )(here, source)
        last = [last[0]] + [shifted(last[step], "grid", parts, -step) for step in range(1, parts)]
    edge = (LANES - owned) // 2
    window = jnp.concatenate(
        [field_blocks[-1][:, owned - edge :], field_blocks[0], field_blocks[1 % blocks][:, :edge]], axis=1
    )

    def micro_call(kernel, count, inputs, scalar_inputs, outputs, scalar_outputs, cells):
        rows = 2 * count * width * ROWS
        cell = pltpu.VMEM((2 * count, width, ROWS, LANES), jnp.float32)
        return pl.pallas_call(
            kernel,
            out_shape=outputs,
            in_specs=[smem() if number < scalar_inputs else vmem() for number in range(len(inputs))],
            out_specs=[smem() if number in scalar_outputs else vmem() for number in range(len(outputs))],
            scratch_shapes=[cell] * cells
            + [
                pltpu.VMEM((rows, 2 * LANES), jnp.bfloat16),
                pltpu.VMEM((rows, 2 * LANES), jnp.float32),
                pltpu.VMEM((rows, 2 * LANES), jnp.float32),
                cell,
                pltpu.VMEM((rows, 2 * LANES), jnp.bfloat16),
                pltpu.VMEM((width, ROWS, LANES), jnp.float32),
            ],
            compiler_params=params,
            cost_estimate=pl.CostEstimate(
                flops=count * 3 * 2 * 512 * 256 * 256 * ORDER, bytes_accessed=4 * 1024 * 1024, transcendentals=0
            ),
        )(*inputs)

    def cells_of(count):
        return float_array(2 * count, width, ROWS, LANES)

    sums_shape = float_array(2, ROWS, LANES)
    main_psi, sums, potential = micro_call(
        functools.partial(first_kernel, parts, main_count, kinds, True),
        main_count,
        [scalars, main, *tables],
        1,
        [cells_of(main_count), sums_shape, float_array(width, ROWS, LANES)],
        (),
        1,
    )
    if last_count:
        last_psi, sums = micro_call(
            functools.partial(first_kernel, parts, last_count, kinds, False),
            last_count,
            [scalars, here, *last, potential, *tables, sums],
            2,
            [cells_of(last_count), sums_shape],
            (),
            1,
        )
    seen = [sums] + [shifted(sums, "grid", parts, step) for step in range(1, parts)]

    whole_shape = float_array(2, norb, held, LANES)
    message_shape = float_array(ROWS, LANES)
    result = []

    def give_back(pieces, count, first):
        return pl.pallas_call(
            functools.partial(unpack_kernel, parts, share, count, first),
            out_shape=whole_shape,
            in_specs=[anywhere()] + [hbm()] * len(result),
            out_specs=hbm(),
            scratch_shapes=[pltpu.SemaphoreType.DMA((parts * 2,))],
            input_output_aliases={1: 0} if result else {},
            compiler_params=params,
        )(exchanged(pieces, "grid"), *result)

    main_pieces, *rest = micro_call(
        functools.partial(second_kernel, parts, main_count, kinds, total_points, True, not last_count),
        main_count,
        [scalars, *seen, main_psi, potential, *tables],
        1,
        [float_array(parts, 2 * main_count, held, LANES)]
        + ([float_array(1), sums_shape] if last_count else [message_shape]),
        (1,) if last_count else (),
        2,
    )
    result = [give_back(main_pieces, main_count, 0)]
    message = rest[-1]
    if last_count:
        vector_value, second_sums = rest
        last_pieces, message = micro_call(
            functools.partial(second_kernel, parts, last_count, kinds, total_points, False, True),
            last_count,
            [scalars, vector_value, sums, second_sums, last_psi, potential, *tables],
            2,
            [float_array(parts, 2 * last_count, held, LANES), message_shape],
            (),
            2,
        )
    message = fold([message] + [shifted(message, "grid", parts, step) for step in range(1, parts)])
    if last_count:
        last_pieces, message = lax.optimization_barrier((last_pieces, message))
        result = [give_back(last_pieces, last_count, main_count)]
    result = result[0]
    orbitals_out = planes_of(result).reshape(2, norb, planes, points)

    messages = [message] + [shifted(message, "macro", blocks, step) for step in range(1, blocks)]
    fields_out = pl.pallas_call(
        functools.partial(fields_kernel, blocks, owned),
        out_shape=float_array(2, owned),
        in_specs=[smem()] + [vmem()] * (1 + blocks),
        out_specs=vmem(),
        compiler_params=params,
    )(block[None], window, *messages)
    return orbitals_out[None], fields_out


def solution(mesh):
    in_specs = (
        P("macro", None, None, "grid", None),
        P("grid", None),
        P(),
        P("macro"),
        P(None, "macro"),
    )
    out_specs = (P("macro", None, None, "grid", None), P(None, "macro"))
    return jax.shard_map(
        functools.partial(per_device, mesh.shape["grid"], mesh.shape["macro"]),
        mesh=mesh,
        in_specs=in_specs,
        out_specs=out_specs,
        check_vma=False,
    )
```

```python
import functools

import jax
import jax.numpy as jnp
import numpy as np
from jax import lax
from jax.experimental import pallas as pl
from jax.experimental.pallas import tpu as pltpu
from jax.sharding import PartitionSpec as P

ORDER = 4
STEPS = 2
spacing = 0.3206
time_step = 0.02
courant_square = 0.81
source_weight = 0.1
radial_strength = 0.3
polar_strength = -0.2
projector_width = 2.5

SECOND = (-14350.0, 8064.0, -1008.0, 128.0, -9.0)
FIRST = (672.0, -168.0, 32.0, -3.0)
KINETIC = 1.0 / (2.0 * 5040.0 * spacing * spacing)
SLOPE = 1.0 / (840.0 * spacing)

LANES = 128
ROWS = 8
LIMIT = 24 * 1024 * 1024
WHOLE = 60 * 1024 * 1024


def stencil_weights(width):
    group = LANES // width
    total = np.zeros((LANES, 3 * LANES), np.float32)
    for y_in in range(group):
        for z_in in range(width):
            for y_out in range(group):
                for part, step in enumerate((0, group, -group)):
                    reach = abs(step + y_in - y_out)
                    if 1 <= reach <= 4:
                        total[y_in * width + z_in, part * LANES + y_out * width + z_in] += SECOND[reach]
            for reach in range(1, 5):
                for z_out in ((z_in + reach) % width, (z_in - reach) % width):
                    total[y_in * width + z_in, y_in * width + z_out] += SECOND[reach]
    return jnp.asarray(np.concatenate([total, total], axis=0), jnp.bfloat16)


def periodic(distance, width):
    return ((distance + width // 2) & (width - 1)) - width // 2


def bell_of(offset):
    distance = offset.astype(jnp.float32)
    bell = jnp.exp(-0.5 * distance * distance / (projector_width * projector_width))
    return bell, distance / projector_width * bell


def tables_kernel(atoms, site_ref, stencil_ref, yz_ref, zy_ref, xbell_ref, xslope_ref, y_ref):
    width = xbell_ref.shape[0]
    kinds = 2 * atoms
    group = LANES // width

    def site_of(column, axis_number):
        atom = (column % kinds) // 2
        position = jnp.zeros(column.shape, jnp.int32)
        for number in range(atoms):
            position = jnp.where(atom == number, site_ref[number, axis_number], position)
        return position

    def factor(coordinate, column):
        bell, slope = bell_of(periodic(coordinate - site_of(column, 2), width))
        value = jnp.where(column % 2 == 0, bell, slope)
        high = value.astype(jnp.bfloat16).astype(jnp.float32)
        return jnp.where(column % LANES < LANES // 2, high, value - high)

    def groups_agree(point, column):
        return (point % LANES) // width == (column // kinds) % group

    shape = (2 * LANES, LANES)
    first = lax.broadcasted_iota(jnp.int32, shape, 0)
    last = lax.broadcasted_iota(jnp.int32, shape, 1)
    yz_ref[:, : 3 * LANES] = stencil_ref[...]
    inward = jnp.where(groups_agree(first, last), factor(first % width, last), 0.0)
    yz_ref[:, 3 * LANES :] = inward.astype(jnp.bfloat16)
    outward = jnp.where(groups_agree(last, first), factor(last % width, first), 0.0)
    zy_ref[...] = outward.astype(jnp.bfloat16)

    shape = (width, ROWS, LANES)
    plane = lax.broadcasted_iota(jnp.int32, shape, 0)
    column = lax.broadcasted_iota(jnp.int32, shape, 2)
    bell, slope = bell_of(periodic(plane - site_of(column, 0), width))
    xbell_ref[...] = bell
    xslope_ref[...] = slope

    shape = (ROWS, LANES)
    column = lax.broadcasted_iota(jnp.int32, shape, 1)
    row = lax.broadcasted_iota(jnp.int32, shape, 0) * group + (column // kinds) % group
    bell, slope = bell_of(periodic(row - site_of(column, 1), width))
    scale = -1.0 / KINETIC
    even = column % 2 == 0
    y_ref[0] = bell
    y_ref[1] = slope
    y_ref[2] = bell * jnp.where(even, scale * radial_strength, scale * polar_strength)
    y_ref[3] = bell * jnp.where(even, scale * polar_strength, 0.0)
    y_ref[4] = slope * jnp.where(even, scale * polar_strength, 0.0)


def vector_kernel(blocks, host_ref, here_ref, *refs):
    out_ref = refs[blocks]
    owned = refs[0].shape[1]
    host = host_ref[0]
    place = lax.broadcasted_iota(jnp.int32, (1, owned), 1)
    present = jnp.zeros((1, owned), jnp.float32)
    previous, beside = present, present
    for number in range(blocks):
        position = place + lax.rem(here_ref[0] + number, blocks) * owned
        before, now = refs[number][0:1, :], refs[number][1:2, :]
        present = present + jnp.where(position == host, now, 0.0)
        previous = previous + jnp.where(position == host, before, 0.0)
        beside = beside + jnp.where((position == host - 1) | (position == host + 1), now, 0.0)
    present = jnp.sum(present)
    out_ref[0] = present
    out_ref[1] = 2.0 * present - jnp.sum(previous) + courant_square * (jnp.sum(beside) - 2.0 * present)
    out_ref[2] = host.astype(jnp.float32)


def run_copies(pairs, sems):
    copies = [
        pltpu.make_async_copy(source, target, sems.at[number]) for number, (source, target) in enumerate(pairs)
    ]
    for copy in copies:
        copy.start()
    for copy in copies:
        copy.wait()


def pack_kernel(parts, share, count, first, source_ref, potential_ref, out_ref, sems):
    pairs = []
    for owner in range(parts):
        pairs.append((potential_ref, out_ref.at[owner, 2 * count]))
        for part in range(2):
            source = source_ref.at[part, pl.ds(owner * share + first, count)]
            pairs.append((source, out_ref.at[owner, pl.ds(part * count, count)]))
    run_copies(pairs, sems)


def pack_pieces_kernel(parts, share, count, first, here_ref, source_ref, *refs):
    pairs = []
    for step in range(parts):
        owner = lax.rem(here_ref[0] + step, parts)
        for part in range(2):
            source = source_ref.at[part, pl.ds(owner * share + first, count)]
            pairs.append((source, refs[step].at[pl.ds(part * count, count)]))
    run_copies(pairs, refs[parts])


def unpack_kernel(parts, share, count, first, piece_ref, *refs):
    out_ref, sems = refs[-2:]
    pairs = []
    for owner in range(parts):
        for part in range(2):
            target = out_ref.at[part, pl.ds(owner * share + first, count)]
            pairs.append((piece_ref.at[owner, pl.ds(part * count, count)], target))
    run_copies(pairs, sems)


def fold(values):
    while len(values) > 1:
        half = len(values) // 2
        values = [values[number] + values[number + half] for number in range(half)]
    return values[0]


def total_of_groups(value, kinds):
    for shift in (4, 2, 1):
        value = value + pltpu.roll(value, shift, 0)
    shift = LANES // 2
    while shift >= kinds:
        value = value + pltpu.roll(value, shift, 1)
        shift //= 2
    return value


def propagate_in_kernel(
    count, vector_value, source_ref, field_ref, total_ref, potential_ref, tables, scratch, width, kinds
):
    yz_ref, zy_ref, xbell_ref, xslope_ref, y_ref = tables
    split_ref, product_ref, partial_ref, spread_ref, diagonal_ref = scratch
    diagonal_ref[...] = (3.0 * SECOND[0] - 0.5 * vector_value * vector_value / KINETIC) - potential_ref[
        ...
    ] * (1.0 / KINETIC)
    block = ROWS
    slab = block * ROWS
    cell_rows = width * ROWS

    def split(planes):
        rows = planes.reshape(slab, LANES)
        high = rows.astype(jnp.bfloat16)
        low = (rows - high.astype(jnp.float32)).astype(jnp.bfloat16)
        return high, low

    def store_split(ref, number, start, planes):
        rows = pl.ds(number * cell_rows + start * ROWS, slab)
        high, low = split(planes)
        ref[rows, :LANES] = high
        ref[rows, LANES:] = low

    for number in range(2 * count):
        for start in range(0, width, block):
            planes = source_ref[number, start : start + block]
            store_split(split_ref, number, start, planes)
            if source_ref is not field_ref:
                field_ref[number, start : start + block] = planes
                total_ref[number, start : start + block] = planes

    def one_order(order, carry):
        inverse = jnp.where(order == 1, 1.0, jnp.where(order == 2, 0.5, jnp.where(order == 3, 1.0 / 3.0, 0.25)))
        step_scale = inverse * time_step
        kinetic = step_scale * KINETIC
        drift = step_scale * SLOPE * vector_value
        slopes = [drift * weight for weight in FIRST]
        outers = {}
        for orbital in range(count):
            rows = pl.ds(2 * orbital * cell_rows, 2 * cell_rows)
            product_ref[rows, :] = jnp.dot(split_ref[rows, :], yz_ref[...], preferred_element_type=jnp.float32)
            for number in (2 * orbital, 2 * orbital + 1):
                bells = [jnp.zeros((ROWS, LANES), jnp.float32) for _ in range(2)]
                inclines = [jnp.zeros((ROWS, LANES), jnp.float32) for _ in range(2)]
                for plane in range(width):
                    inner = product_ref[pl.ds(number * cell_rows + plane * ROWS, ROWS), 3 * LANES :]
                    turn = plane % 2
                    bells[turn] = bells[turn] + inner * xbell_ref[plane]
                    inclines[turn] = inclines[turn] + inner * xslope_ref[plane]
                bell = bells[0] + bells[1]
                incline = inclines[0] + inclines[1]
                first = total_of_groups(bell * y_ref[0], kinds)
                second = total_of_groups(incline * y_ref[0], kinds)
                third = total_of_groups(bell * y_ref[1], kinds)
                outers[number] = (kinetic * (first * y_ref[2] + third * y_ref[4]), kinetic * (second * y_ref[3]))
        for orbital in range(count):
            for start in range(0, width, block):
                near = [
                    {plane: field_ref[number, plane % width] for plane in range(start - 4, start + block + 4)}
                    for number in (2 * orbital, 2 * orbital + 1)
                ]
                for plane in range(start, start + block):
                    images, drifts = [], []
                    for part in range(2):
                        line = pl.ds((2 * orbital + part) * cell_rows + plane * ROWS, ROWS)
                        total = product_ref[line, :LANES]
                        total = total + pltpu.roll(product_ref[line, LANES : 2 * LANES], ROWS - 1, 0)
                        total = total + pltpu.roll(product_ref[line, 2 * LANES : 3 * LANES], 1, 0)
                        total = total + diagonal_ref[plane] * near[part][plane]
                        moved = None
                        for reach in range(1, 5):
                            ahead, behind = near[part][plane + reach], near[part][plane - reach]
                            total = total + SECOND[reach] * (ahead + behind)
                            term = slopes[reach - 1] * (ahead - behind)
                            moved = term if moved is None else moved + term
                        images.append(kinetic * total)
                        drifts.append(moved)
                    partial_ref[2 * orbital, plane] = -images[1] - drifts[0]
                    partial_ref[2 * orbital + 1, plane] = images[0] - drifts[1]
        for orbital in range(count):
            real, imaginary = 2 * orbital, 2 * orbital + 1
            for start in range(0, width, block):
                xbell = xbell_ref[start : start + block]
                xslope = xslope_ref[start : start + block]
                for number in (real, imaginary):
                    spread = xbell * outers[number][0][None] + xslope * outers[number][1][None]
                    store_split(spread_ref, number, start, spread)
            rows = pl.ds(real * cell_rows, 2 * cell_rows)
            product_ref[rows, :LANES] = jnp.dot(
                spread_ref[rows, :], zy_ref[...], preferred_element_type=jnp.float32
            )
            for start in range(0, width, block):
                spreads = [
                    product_ref[pl.ds(number * cell_rows + start * ROWS, slab), :LANES].reshape(block, ROWS, LANES)
                    for number in (real, imaginary)
                ]
                new = (
                    partial_ref[real, start : start + block] - spreads[1],
                    partial_ref[imaginary, start : start + block] + spreads[0],
                )
                for number, value in zip((real, imaginary), new):
                    field_ref[number, start : start + block] = value
                    total_ref[number, start : start + block] += value
                    store_split(split_ref, number, start, value)
        return carry

    lax.fori_loop(1, ORDER + 1, one_order, 0)


def sums_in_kernel(count, total_ref, width):
    flow = jnp.zeros((ROWS, LANES), jnp.float32)
    density = jnp.zeros((ROWS, LANES), jnp.float32)
    block = ROWS
    for orbital in range(count):
        for start in range(0, width, block):
            near = {
                plane: total_ref[2 * orbital + 1, plane % width] for plane in range(start - 4, start + block + 4)
            }
            for plane in range(start, start + block):
                real, imaginary = total_ref[2 * orbital, plane], near[plane]
                moved = None
                for reach in range(1, 5):
                    term = FIRST[reach - 1] * (near[plane + reach] - near[plane - reach])
                    moved = term if moved is None else moved + term
                flow = flow + real * moved
                density = density + (real * real + imaginary * imaginary)
    return (2.0 * SLOPE) * flow, density


def first_kernel(parts, count, kinds, opening, scalar_ref, *refs):
    if opening:
        piece_ref, *tables, total_ref, out_ref, potential_ref, field_ref = refs[:10]
        scratch = refs[10:]
    else:
        here_ref, pieces, refs = refs[0], refs[1 : 1 + parts], refs[1 + parts :]
        potential_ref, *tables, sums_ref, total_ref, out_ref, field_ref = refs[:10]
        scratch = refs[10:]
    width = total_ref.shape[1]
    planes = width // parts
    for step in range(parts):
        if opening:
            piece, start = piece_ref.at[step], step * planes
        else:
            piece, start = pieces[step], lax.rem(here_ref[0] + parts - step, parts) * planes
        for index in range(planes):
            rows = pl.ds(index, ROWS, stride=planes)
            for orbital in range(count):
                for part in range(2):
                    value = piece[part * count + orbital, rows, :]
                    field_ref[2 * orbital + part, start + index] = value
                    total_ref[2 * orbital + part, start + index] = value
            if opening:
                potential_ref[start + index] = piece[2 * count, rows, :]
    propagate_in_kernel(
        count, scalar_ref[0], field_ref, field_ref, total_ref, potential_ref, tables, scratch, width, kinds
    )
    flow, density = sums_in_kernel(count, total_ref, width)
    if not opening:
        flow, density = sums_ref[0] + flow, sums_ref[1] + density
    out_ref[0] = flow
    out_ref[1] = density


def second_kernel(parts, count, kinds, points, opening, closing, scalar_ref, *refs):
    if opening:
        seen, refs = refs[:parts], refs[parts:]
        first_sums_ref = seen[0]
    else:
        vector_ref, first_sums_ref, sums_ref, *refs = refs
    psi_ref, potential_ref, *tables = refs[:7]
    refs = refs[7:]
    piece_ref, *refs = refs
    if opening and not closing:
        vector_ref, *refs = refs
    out_ref, field_ref, total_ref = refs[:3]
    scratch = refs[3:]
    width = total_ref.shape[1]
    planes = width // parts
    if opening:
        flow = jnp.sum(fold([ref[0] for ref in seen]))
        density = jnp.sum(fold([ref[1] for ref in seen]))
        current = (flow + scalar_ref[0] * density) * (1.0 / points)
        vector_value = scalar_ref[1] - source_weight * current
        if not closing:
            vector_ref[0] = vector_value
    else:
        vector_value = vector_ref[0]
    propagate_in_kernel(
        count, vector_value, psi_ref, field_ref, total_ref, potential_ref, tables, scratch, width, kinds
    )
    for step in range(parts):
        piece, start = piece_ref.at[step], step * planes
        for index in range(planes):
            rows = pl.ds(index, ROWS, stride=planes)
            for orbital in range(count):
                for part in range(2):
                    piece[part * count + orbital, rows, :] = total_ref[2 * orbital + part, start + index]
    flow, density = sums_in_kernel(count, total_ref, width)
    if not opening:
        flow, density = sums_ref[0] + flow, sums_ref[1] + density
    if closing:
        row = lax.broadcasted_iota(jnp.int32, (ROWS, LANES), 0)
        own = first_sums_ref[0] + scalar_ref[0] * first_sums_ref[1]
        own = jnp.sum(own, axis=0, keepdims=True) * (1.0 / points)
        new = jnp.sum(flow + vector_value * density, axis=0, keepdims=True) * (1.0 / points)
        host = scalar_ref[2] * (1.0 / parts)
        out_ref[...] = jnp.where(row == 0, own, jnp.where(row == 1, new, host))
    else:
        out_ref[0] = flow
        out_ref[1] = density


def fields_kernel(blocks, owned, here_ref, window_ref, *refs):
    messages, out_ref = refs[:blocks], refs[blocks]
    edge = (LANES - owned) // 2
    length = blocks * owned
    position = lax.broadcasted_iota(jnp.int32, (1, LANES), 1) + (here_ref[0] * owned - edge)
    inside = (position >= 0) & (position < length)
    previous = jnp.where(inside, window_ref[0:1, :], 0.0)
    present = jnp.where(inside, window_ref[1:2, :], 0.0)
    place = position.astype(jnp.float32)
    for step in range(STEPS):
        source = jnp.zeros((1, LANES), jnp.float32)
        for message in messages:
            current = jnp.sum(message[step : step + 1, :])
            source = source + jnp.where(place == message[2:3, :], current, 0.0)
        beside = pltpu.roll(present, 1, 1) + pltpu.roll(present, LANES - 1, 1)
        following = (
            2.0 * present - previous + courant_square * (beside - 2.0 * present) - source_weight * source
        )
        previous, present = present, jnp.where(inside, following, 0.0)
    out_ref[0:1, :] = pltpu.roll(previous, LANES - edge, 1)[:, :owned]
    out_ref[1:2, :] = pltpu.roll(present, LANES - edge, 1)[:, :owned]


def vmem():
    return pl.BlockSpec(memory_space=pltpu.VMEM)


def smem():
    return pl.BlockSpec(memory_space=pltpu.SMEM)


def anywhere():
    return pl.BlockSpec(memory_space=pl.ANY)


def hbm():
    return pl.BlockSpec(memory_space=pltpu.HBM)


def float_array(*shape):
    return jax.ShapeDtypeStruct(shape, jnp.float32)


def exchanged(value, axes):
    return lax.all_to_all(value, axes, split_axis=0, concat_axis=0, tiled=True)


def shifted(value, axis_name, count, shift):
    return lax.ppermute(value, axis_name, [((index + shift) % count, index) for index in range(count)])


def per_device(parts, blocks, orbitals, local_potential, atom_sites, host_point, fields):
    norb = orbitals.shape[2]
    planes, points = local_potential.shape
    width = planes * parts
    share = norb // parts
    last_count = share // 2
    main_count = share - last_count
    owned = fields.shape[1]
    atoms = atom_sites.shape[0]
    kinds = 2 * atoms
    held = ROWS * planes
    total_points = float(width**3 * norb)
    here = lax.axis_index("grid").astype(jnp.int32)[None]
    block = lax.axis_index("macro").astype(jnp.int32)
    params = pltpu.CompilerParams(vmem_limit_bytes=LIMIT)
    whole_params = pltpu.CompilerParams(vmem_limit_bytes=WHOLE)

    def rows_of(value):
        lead = value.shape[:-2]
        value = value.reshape(*lead, planes, ROWS, LANES)
        return jnp.swapaxes(value, -3, -2).reshape(*lead, held, LANES)

    def planes_of(value):
        lead = value.shape[:-2]
        value = value.reshape(*lead, ROWS, planes, LANES)
        return jnp.swapaxes(value, -3, -2)

    source = rows_of(orbitals[0])
    packed = pl.pallas_call(
        functools.partial(pack_kernel, parts, share, main_count, 0),
        out_shape=float_array(parts, 2 * main_count + 1, held, LANES),
        in_specs=[hbm(), hbm()],
        out_specs=vmem(),
        scratch_shapes=[pltpu.SemaphoreType.DMA((parts * 3,))],
        compiler_params=whole_params,
    )(source, rows_of(local_potential))
    main = exchanged(packed, "grid")
    fields, packed = lax.optimization_barrier((fields, packed))
    field_blocks = [fields] + [shifted(fields, "macro", blocks, step) for step in range(1, blocks)]

    tables = pl.pallas_call(
        functools.partial(tables_kernel, atoms),
        out_shape=[
            jax.ShapeDtypeStruct((2 * LANES, 4 * LANES), jnp.bfloat16),
            jax.ShapeDtypeStruct((2 * LANES, LANES), jnp.bfloat16),
            float_array(width, ROWS, LANES),
            float_array(width, ROWS, LANES),
            float_array(5, ROWS, LANES),
        ],
        in_specs=[smem(), vmem()],
        out_specs=[vmem()] * 5,
        compiler_params=params,
    )(atom_sites, stencil_weights(width))

    scalars = pl.pallas_call(
        functools.partial(vector_kernel, blocks),
        out_shape=float_array(3),
        in_specs=[smem(), smem()] + [vmem()] * blocks,
        out_specs=smem(),
        compiler_params=params,
    )(host_point, block[None], *field_blocks)

    source, scalars = lax.optimization_barrier((source, scalars))
    if last_count:
        last = pl.pallas_call(
            functools.partial(pack_pieces_kernel, parts, share, last_count, main_count),
            out_shape=[float_array(2 * last_count, held, LANES)] * parts,
            in_specs=[smem(), hbm()],
            out_specs=[vmem()] * parts,
            scratch_shapes=[pltpu.SemaphoreType.DMA((parts * 2,))],
            compiler_params=whole_params,
        )(here, source)
        last = [last[0]] + [shifted(last[step], "grid", parts, -step) for step in range(1, parts)]
    edge = (LANES - owned) // 2
    window = jnp.concatenate(
        [field_blocks[-1][:, owned - edge :], field_blocks[0], field_blocks[1 % blocks][:, :edge]], axis=1
    )

    def micro_call(kernel, count, inputs, scalar_inputs, outputs, scalar_outputs, cells):
        rows = 2 * count * width * ROWS
        cell = pltpu.VMEM((2 * count, width, ROWS, LANES), jnp.float32)
        return pl.pallas_call(
            kernel,
            out_shape=outputs,
            in_specs=[smem() if number < scalar_inputs else vmem() for number in range(len(inputs))],
            out_specs=[smem() if number in scalar_outputs else vmem() for number in range(len(outputs))],
            scratch_shapes=[cell] * cells
            + [
                pltpu.VMEM((rows, 2 * LANES), jnp.bfloat16),
                pltpu.VMEM((rows, 4 * LANES), jnp.float32),
                cell,
                pltpu.VMEM((rows, 2 * LANES), jnp.bfloat16),
                pltpu.VMEM((width, ROWS, LANES), jnp.float32),
            ],
            compiler_params=params,
            cost_estimate=pl.CostEstimate(
                flops=count * 3 * 2 * 512 * 256 * 256 * ORDER, bytes_accessed=4 * 1024 * 1024, transcendentals=0
            ),
        )(*inputs)

    def cells_of(count):
        return float_array(2 * count, width, ROWS, LANES)

    sums_shape = float_array(2, ROWS, LANES)
    main_psi, sums, potential = micro_call(
        functools.partial(first_kernel, parts, main_count, kinds, True),
        main_count,
        [scalars, main, *tables],
        1,
        [cells_of(main_count), sums_shape, float_array(width, ROWS, LANES)],
        (),
        1,
    )
    if last_count:
        last_psi, sums = micro_call(
            functools.partial(first_kernel, parts, last_count, kinds, False),
            last_count,
            [scalars, here, *last, potential, *tables, sums],
            2,
            [cells_of(last_count), sums_shape],
            (),
            1,
        )
    seen = [sums] + [shifted(sums, "grid", parts, step) for step in range(1, parts)]

    whole_shape = float_array(2, norb, held, LANES)
    message_shape = float_array(ROWS, LANES)
    result = []

    def give_back(pieces, count, first):
        return pl.pallas_call(
            functools.partial(unpack_kernel, parts, share, count, first),
            out_shape=whole_shape,
            in_specs=[anywhere()] + [hbm()] * len(result),
            out_specs=hbm(),
            scratch_shapes=[pltpu.SemaphoreType.DMA((parts * 2,))],
            input_output_aliases={1: 0} if result else {},
            compiler_params=params,
        )(exchanged(pieces, "grid"), *result)

    main_pieces, *rest = micro_call(
        functools.partial(second_kernel, parts, main_count, kinds, total_points, True, not last_count),
        main_count,
        [scalars, *seen, main_psi, potential, *tables],
        1,
        [float_array(parts, 2 * main_count, held, LANES)]
        + ([float_array(1), sums_shape] if last_count else [message_shape]),
        (1,) if last_count else (),
        2,
    )
    result = [give_back(main_pieces, main_count, 0)]
    message = rest[-1]
    if last_count:
        vector_value, second_sums = rest
        last_pieces, message = micro_call(
            functools.partial(second_kernel, parts, last_count, kinds, total_points, False, True),
            last_count,
            [scalars, vector_value, sums, second_sums, last_psi, potential, *tables],
            2,
            [float_array(parts, 2 * last_count, held, LANES), message_shape],
            (),
            2,
        )
    message = fold([message] + [shifted(message, "grid", parts, step) for step in range(1, parts)])
    if last_count:
        last_pieces, message = lax.optimization_barrier((last_pieces, message))
        result = [give_back(last_pieces, last_count, main_count)]
    result = result[0]
    orbitals_out = planes_of(result).reshape(2, norb, planes, points)

    messages = [message] + [shifted(message, "macro", blocks, step) for step in range(1, blocks)]
    fields_out = pl.pallas_call(
        functools.partial(fields_kernel, blocks, owned),
        out_shape=float_array(2, owned),
        in_specs=[smem()] + [vmem()] * (1 + blocks),
        out_specs=vmem(),
        compiler_params=params,
    )(block[None], window, *messages)
    return orbitals_out[None], fields_out


def solution(mesh):
    in_specs = (
        P("macro", None, None, "grid", None),
        P("grid", None),
        P(),
        P("macro"),
        P(None, "macro"),
    )
    out_specs = (P("macro", None, None, "grid", None), P(None, "macro"))
    return jax.shard_map(
        functools.partial(per_device, mesh.shape["grid"], mesh.shape["macro"]),
        mesh=mesh,
        in_specs=in_specs,
        out_specs=out_specs,
        check_vma=False,
    )
```

```python
import functools

import jax
import jax.numpy as jnp
import numpy as np
from jax import lax
from jax.experimental import pallas as pl
from jax.experimental.pallas import tpu as pltpu
from jax.sharding import PartitionSpec as P

ORDER = 4
STEPS = 2
spacing = 0.3206
time_step = 0.02
courant_square = 0.81
source_weight = 0.1
radial_strength = 0.3
polar_strength = -0.2
projector_width = 2.5

SECOND = (-14350.0, 8064.0, -1008.0, 128.0, -9.0)
FIRST = (672.0, -168.0, 32.0, -3.0)
KINETIC = 1.0 / (2.0 * 5040.0 * spacing * spacing)
SLOPE = 1.0 / (840.0 * spacing)

LANES = 128
ROWS = 8
LIMIT = 24 * 1024 * 1024
WHOLE = 60 * 1024 * 1024


def stencil_weights(width):
    group = LANES // width
    total = np.zeros((LANES, 3 * LANES), np.float32)
    for y_in in range(group):
        for z_in in range(width):
            for y_out in range(group):
                for part, step in enumerate((0, group, -group)):
                    reach = abs(step + y_in - y_out)
                    if 1 <= reach <= 4:
                        total[y_in * width + z_in, part * LANES + y_out * width + z_in] += SECOND[reach]
            for reach in range(1, 5):
                for z_out in ((z_in + reach) % width, (z_in - reach) % width):
                    total[y_in * width + z_in, y_in * width + z_out] += SECOND[reach]
    return jnp.asarray(np.concatenate([total, total], axis=0), jnp.bfloat16)


def periodic(distance, width):
    return ((distance + width // 2) & (width - 1)) - width // 2


def bell_of(offset):
    distance = offset.astype(jnp.float32)
    bell = jnp.exp(-0.5 * distance * distance / (projector_width * projector_width))
    return bell, distance / projector_width * bell


def tables_kernel(atoms, site_ref, stencil_ref, yz_ref, zy_ref, xbell_ref, xslope_ref, y_ref):
    width = xbell_ref.shape[0]
    kinds = 2 * atoms
    group = LANES // width

    def site_of(column, axis_number):
        atom = (column % kinds) // 2
        position = jnp.zeros(column.shape, jnp.int32)
        for number in range(atoms):
            position = jnp.where(atom == number, site_ref[number, axis_number], position)
        return position

    def factor(coordinate, column):
        bell, slope = bell_of(periodic(coordinate - site_of(column, 2), width))
        value = jnp.where(column % 2 == 0, bell, slope)
        high = value.astype(jnp.bfloat16).astype(jnp.float32)
        return jnp.where(column % LANES < LANES // 2, high, value - high)

    def groups_agree(point, column):
        return (point % LANES) // width == (column // kinds) % group

    shape = (2 * LANES, LANES)
    first = lax.broadcasted_iota(jnp.int32, shape, 0)
    last = lax.broadcasted_iota(jnp.int32, shape, 1)
    yz_ref[:, : 3 * LANES] = stencil_ref[...]
    inward = jnp.where(groups_agree(first, last), factor(first % width, last), 0.0)
    yz_ref[:, 3 * LANES :] = inward.astype(jnp.bfloat16)
    outward = jnp.where(groups_agree(last, first), factor(last % width, first), 0.0)
    zy_ref[...] = outward.astype(jnp.bfloat16)

    shape = (width, ROWS, LANES)
    plane = lax.broadcasted_iota(jnp.int32, shape, 0)
    column = lax.broadcasted_iota(jnp.int32, shape, 2)
    bell, slope = bell_of(periodic(plane - site_of(column, 0), width))
    xbell_ref[...] = bell
    xslope_ref[...] = slope

    shape = (ROWS, LANES)
    column = lax.broadcasted_iota(jnp.int32, shape, 1)
    row = lax.broadcasted_iota(jnp.int32, shape, 0) * group + (column // kinds) % group
    bell, slope = bell_of(periodic(row - site_of(column, 1), width))
    scale = -1.0 / KINETIC
    even = column % 2 == 0
    y_ref[0] = bell
    y_ref[1] = slope
    y_ref[2] = bell * jnp.where(even, scale * radial_strength, scale * polar_strength)
    y_ref[3] = bell * jnp.where(even, scale * polar_strength, 0.0)
    y_ref[4] = slope * jnp.where(even, scale * polar_strength, 0.0)


def vector_kernel(blocks, host_ref, here_ref, *refs):
    out_ref = refs[blocks]
    owned = refs[0].shape[1]
    host = host_ref[0]
    place = lax.broadcasted_iota(jnp.int32, (1, owned), 1)
    present = jnp.zeros((1, owned), jnp.float32)
    previous, beside = present, present
    for number in range(blocks):
        position = place + lax.rem(here_ref[0] + number, blocks) * owned
        before, now = refs[number][0:1, :], refs[number][1:2, :]
        present = present + jnp.where(position == host, now, 0.0)
        previous = previous + jnp.where(position == host, before, 0.0)
        beside = beside + jnp.where((position == host - 1) | (position == host + 1), now, 0.0)
    present = jnp.sum(present)
    out_ref[0] = present
    out_ref[1] = 2.0 * present - jnp.sum(previous) + courant_square * (jnp.sum(beside) - 2.0 * present)
    out_ref[2] = host.astype(jnp.float32)


def run_copies(pairs, sems):
    copies = [
        pltpu.make_async_copy(source, target, sems.at[number]) for number, (source, target) in enumerate(pairs)
    ]
    for copy in copies:
        copy.start()
    for copy in copies:
        copy.wait()


def pack_kernel(parts, share, count, first, source_ref, potential_ref, out_ref, sems):
    pairs = []
    for owner in range(parts):
        pairs.append((potential_ref, out_ref.at[owner, 2 * count]))
        for part in range(2):
            source = source_ref.at[part, pl.ds(owner * share + first, count)]
            pairs.append((source, out_ref.at[owner, pl.ds(part * count, count)]))
    run_copies(pairs, sems)


def pack_pieces_kernel(parts, share, count, first, here_ref, source_ref, *refs):
    pairs = []
    for step in range(parts):
        owner = lax.rem(here_ref[0] + step, parts)
        for part in range(2):
            source = source_ref.at[part, pl.ds(owner * share + first, count)]
            pairs.append((source, refs[step].at[pl.ds(part * count, count)]))
    run_copies(pairs, refs[parts])


def unpack_kernel(parts, share, count, first, piece_ref, *refs):
    out_ref, sems = refs[-2:]
    pairs = []
    for owner in range(parts):
        for part in range(2):
            target = out_ref.at[part, pl.ds(owner * share + first, count)]
            pairs.append((piece_ref.at[owner, pl.ds(part * count, count)], target))
    run_copies(pairs, sems)


def fold(values):
    while len(values) > 1:
        half = len(values) // 2
        values = [values[number] + values[number + half] for number in range(half)]
    return values[0]


def total_of_groups(value, kinds):
    for shift in (4, 2, 1):
        value = value + pltpu.roll(value, shift, 0)
    shift = LANES // 2
    while shift >= kinds:
        value = value + pltpu.roll(value, shift, 1)
        shift //= 2
    return value


def propagate_in_kernel(
    count, vector_value, source_ref, field_ref, total_ref, potential_ref, tables, scratch, width, kinds
):
    yz_ref, zy_ref, xbell_ref, xslope_ref, y_ref = tables
    split_ref, product_ref, partial_ref, spread_ref, diagonal_ref = scratch
    diagonal_ref[...] = (3.0 * SECOND[0] - 0.5 * vector_value * vector_value / KINETIC) - potential_ref[
        ...
    ] * (1.0 / KINETIC)
    block = ROWS
    slab = block * ROWS
    cell_rows = width * ROWS

    def split(planes):
        rows = planes.reshape(slab, LANES)
        high = rows.astype(jnp.bfloat16)
        low = (rows - high.astype(jnp.float32)).astype(jnp.bfloat16)
        return high, low

    def store_split(ref, number, start, planes):
        rows = pl.ds(number * cell_rows + start * ROWS, slab)
        high, low = split(planes)
        ref[rows, :LANES] = high
        ref[rows, LANES:] = low

    for number in range(2 * count):
        for start in range(0, width, block):
            planes = source_ref[number, start : start + block]
            store_split(split_ref, number, start, planes)
            if source_ref is not field_ref:
                field_ref[number, start : start + block] = planes
                total_ref[number, start : start + block] = planes

    def one_order(order):
        step_scale = time_step / order
        kinetic = step_scale * KINETIC
        drift = step_scale * SLOPE * vector_value
        slopes = [drift * weight for weight in FIRST]
        outers = {}
        for orbital in range(count):
            rows = pl.ds(2 * orbital * cell_rows, 2 * cell_rows)
            product_ref[rows, :] = jnp.dot(split_ref[rows, :], yz_ref[...], preferred_element_type=jnp.float32)
            for number in (2 * orbital, 2 * orbital + 1):
                bells = [jnp.zeros((ROWS, LANES), jnp.float32) for _ in range(2)]
                inclines = [jnp.zeros((ROWS, LANES), jnp.float32) for _ in range(2)]
                for plane in range(width):
                    inner = product_ref[pl.ds(number * cell_rows + plane * ROWS, ROWS), 3 * LANES :]
                    turn = plane % 2
                    bells[turn] = bells[turn] + inner * xbell_ref[plane]
                    inclines[turn] = inclines[turn] + inner * xslope_ref[plane]
                bell = bells[0] + bells[1]
                incline = inclines[0] + inclines[1]
                first = total_of_groups(bell * y_ref[0], kinds)
                second = total_of_groups(incline * y_ref[0], kinds)
                third = total_of_groups(bell * y_ref[1], kinds)
                outers[number] = (kinetic * (first * y_ref[2] + third * y_ref[4]), kinetic * (second * y_ref[3]))
        for orbital in range(count):
            for start in range(0, width, block):
                near = [
                    {plane: field_ref[number, plane % width] for plane in range(start - 4, start + block + 4)}
                    for number in (2 * orbital, 2 * orbital + 1)
                ]
                for plane in range(start, start + block):
                    images, drifts = [], []
                    for part in range(2):
                        line = pl.ds((2 * orbital + part) * cell_rows + plane * ROWS, ROWS)
                        total = product_ref[line, :LANES]
                        total = total + pltpu.roll(product_ref[line, LANES : 2 * LANES], ROWS - 1, 0)
                        total = total + pltpu.roll(product_ref[line, 2 * LANES : 3 * LANES], 1, 0)
                        total = total + diagonal_ref[plane] * near[part][plane]
                        moved = None
                        for reach in range(1, 5):
                            ahead, behind = near[part][plane + reach], near[part][plane - reach]
                            total = total + SECOND[reach] * (ahead + behind)
                            term = slopes[reach - 1] * (ahead - behind)
                            moved = term if moved is None else moved + term
                        images.append(kinetic * total)
                        drifts.append(moved)
                    partial_ref[2 * orbital, plane] = -images[1] - drifts[0]
                    partial_ref[2 * orbital + 1, plane] = images[0] - drifts[1]
        for orbital in range(count):
            real, imaginary = 2 * orbital, 2 * orbital + 1
            for start in range(0, width, block):
                xbell = xbell_ref[start : start + block]
                xslope = xslope_ref[start : start + block]
                for number in (real, imaginary):
                    spread = xbell * outers[number][0][None] + xslope * outers[number][1][None]
                    store_split(spread_ref, number, start, spread)
            rows = pl.ds(real * cell_rows, 2 * cell_rows)
            product_ref[rows, :LANES] = jnp.dot(
                spread_ref[rows, :], zy_ref[...], preferred_element_type=jnp.float32
            )
            for start in range(0, width, block):
                spreads = [
                    product_ref[pl.ds(number * cell_rows + start * ROWS, slab), :LANES].reshape(block, ROWS, LANES)
                    for number in (real, imaginary)
                ]
                new = (
                    partial_ref[real, start : start + block] - spreads[1],
                    partial_ref[imaginary, start : start + block] + spreads[0],
                )
                for number, value in zip((real, imaginary), new):
                    total_ref[number, start : start + block] += value
                    if order < ORDER:
                        field_ref[number, start : start + block] = value
                        store_split(split_ref, number, start, value)

    for order in range(1, ORDER + 1):
        one_order(order)


def sums_in_kernel(count, total_ref, width):
    flow = jnp.zeros((ROWS, LANES), jnp.float32)
    density = jnp.zeros((ROWS, LANES), jnp.float32)
    block = ROWS
    for orbital in range(count):
        for start in range(0, width, block):
            near = {
                plane: total_ref[2 * orbital + 1, plane % width] for plane in range(start - 4, start + block + 4)
            }
            for plane in range(start, start + block):
                real, imaginary = total_ref[2 * orbital, plane], near[plane]
                moved = None
                for reach in range(1, 5):
                    term = FIRST[reach - 1] * (near[plane + reach] - near[plane - reach])
                    moved = term if moved is None else moved + term
                flow = flow + real * moved
                density = density + (real * real + imaginary * imaginary)
    return (2.0 * SLOPE) * flow, density


def first_kernel(parts, count, kinds, opening, scalar_ref, *refs):
    if opening:
        piece_ref, *tables, total_ref, out_ref, potential_ref, field_ref = refs[:10]
        scratch = refs[10:]
    else:
        here_ref, pieces, refs = refs[0], refs[1 : 1 + parts], refs[1 + parts :]
        potential_ref, *tables, sums_ref, total_ref, out_ref, field_ref = refs[:10]
        scratch = refs[10:]
    width = total_ref.shape[1]
    planes = width // parts
    for step in range(parts):
        if opening:
            piece, start = piece_ref.at[step], step * planes
        else:
            piece, start = pieces[step], lax.rem(here_ref[0] + parts - step, parts) * planes
        for index in range(planes):
            rows = pl.ds(index, ROWS, stride=planes)
            for orbital in range(count):
                for part in range(2):
                    value = piece[part * count + orbital, rows, :]
                    field_ref[2 * orbital + part, start + index] = value
                    total_ref[2 * orbital + part, start + index] = value
            if opening:
                potential_ref[start + index] = piece[2 * count, rows, :]
    propagate_in_kernel(
        count, scalar_ref[0], field_ref, field_ref, total_ref, potential_ref, tables, scratch, width, kinds
    )
    flow, density = sums_in_kernel(count, total_ref, width)
    if not opening:
        flow, density = sums_ref[0] + flow, sums_ref[1] + density
    out_ref[0] = flow
    out_ref[1] = density


def second_kernel(parts, count, kinds, points, opening, closing, scalar_ref, *refs):
    if opening:
        seen, refs = refs[:parts], refs[parts:]
        first_sums_ref = seen[0]
    else:
        vector_ref, first_sums_ref, sums_ref, *refs = refs
    psi_ref, potential_ref, *tables = refs[:7]
    refs = refs[7:]
    piece_ref, *refs = refs
    if opening and not closing:
        vector_ref, *refs = refs
    out_ref, field_ref, total_ref = refs[:3]
    scratch = refs[3:]
    width = total_ref.shape[1]
    planes = width // parts
    if opening:
        flow = jnp.sum(fold([ref[0] for ref in seen]))
        density = jnp.sum(fold([ref[1] for ref in seen]))
        current = (flow + scalar_ref[0] * density) * (1.0 / points)
        vector_value = scalar_ref[1] - source_weight * current
        if not closing:
            vector_ref[0] = vector_value
    else:
        vector_value = vector_ref[0]
    propagate_in_kernel(
        count, vector_value, psi_ref, field_ref, total_ref, potential_ref, tables, scratch, width, kinds
    )
    for step in range(parts):
        piece, start = piece_ref.at[step], step * planes
        for index in range(planes):
            rows = pl.ds(index, ROWS, stride=planes)
            for orbital in range(count):
                for part in range(2):
                    piece[part * count + orbital, rows, :] = total_ref[2 * orbital + part, start + index]
    flow, density = sums_in_kernel(count, total_ref, width)
    if not opening:
        flow, density = sums_ref[0] + flow, sums_ref[1] + density
    if closing:
        row = lax.broadcasted_iota(jnp.int32, (ROWS, LANES), 0)
        own = first_sums_ref[0] + scalar_ref[0] * first_sums_ref[1]
        own = jnp.sum(own, axis=0, keepdims=True) * (1.0 / points)
        new = jnp.sum(flow + vector_value * density, axis=0, keepdims=True) * (1.0 / points)
        host = scalar_ref[2] * (1.0 / parts)
        out_ref[...] = jnp.where(row == 0, own, jnp.where(row == 1, new, host))
    else:
        out_ref[0] = flow
        out_ref[1] = density


def fields_kernel(blocks, owned, here_ref, window_ref, *refs):
    messages, out_ref = refs[:blocks], refs[blocks]
    edge = (LANES - owned) // 2
    length = blocks * owned
    position = lax.broadcasted_iota(jnp.int32, (1, LANES), 1) + (here_ref[0] * owned - edge)
    inside = (position >= 0) & (position < length)
    previous = jnp.where(inside, window_ref[0:1, :], 0.0)
    present = jnp.where(inside, window_ref[1:2, :], 0.0)
    place = position.astype(jnp.float32)
    for step in range(STEPS):
        source = jnp.zeros((1, LANES), jnp.float32)
        for message in messages:
            current = jnp.sum(message[step : step + 1, :])
            source = source + jnp.where(place == message[2:3, :], current, 0.0)
        beside = pltpu.roll(present, 1, 1) + pltpu.roll(present, LANES - 1, 1)
        following = (
            2.0 * present - previous + courant_square * (beside - 2.0 * present) - source_weight * source
        )
        previous, present = present, jnp.where(inside, following, 0.0)
    out_ref[0:1, :] = pltpu.roll(previous, LANES - edge, 1)[:, :owned]
    out_ref[1:2, :] = pltpu.roll(present, LANES - edge, 1)[:, :owned]


def vmem():
    return pl.BlockSpec(memory_space=pltpu.VMEM)


def smem():
    return pl.BlockSpec(memory_space=pltpu.SMEM)


def anywhere():
    return pl.BlockSpec(memory_space=pl.ANY)


def hbm():
    return pl.BlockSpec(memory_space=pltpu.HBM)


def float_array(*shape):
    return jax.ShapeDtypeStruct(shape, jnp.float32)


def exchanged(value, axes):
    return lax.all_to_all(value, axes, split_axis=0, concat_axis=0, tiled=True)


def shifted(value, axis_name, count, shift):
    return lax.ppermute(value, axis_name, [((index + shift) % count, index) for index in range(count)])


def per_device(parts, blocks, orbitals, local_potential, atom_sites, host_point, fields):
    norb = orbitals.shape[2]
    planes, points = local_potential.shape
    width = planes * parts
    share = norb // parts
    last_count = share // 2
    main_count = share - last_count
    owned = fields.shape[1]
    atoms = atom_sites.shape[0]
    kinds = 2 * atoms
    held = ROWS * planes
    total_points = float(width**3 * norb)
    here = lax.axis_index("grid").astype(jnp.int32)[None]
    block = lax.axis_index("macro").astype(jnp.int32)
    params = pltpu.CompilerParams(vmem_limit_bytes=LIMIT)
    whole_params = pltpu.CompilerParams(vmem_limit_bytes=WHOLE)

    def rows_of(value):
        lead = value.shape[:-2]
        value = value.reshape(*lead, planes, ROWS, LANES)
        return jnp.swapaxes(value, -3, -2).reshape(*lead, held, LANES)

    def planes_of(value):
        lead = value.shape[:-2]
        value = value.reshape(*lead, ROWS, planes, LANES)
        return jnp.swapaxes(value, -3, -2)

    source = rows_of(orbitals[0])
    packed = pl.pallas_call(
        functools.partial(pack_kernel, parts, share, main_count, 0),
        out_shape=float_array(parts, 2 * main_count + 1, held, LANES),
        in_specs=[hbm(), hbm()],
        out_specs=vmem(),
        scratch_shapes=[pltpu.SemaphoreType.DMA((parts * 3,))],
        compiler_params=whole_params,
    )(source, rows_of(local_potential))
    main = exchanged(packed, "grid")
    fields, packed = lax.optimization_barrier((fields, packed))
    field_blocks = [fields] + [shifted(fields, "macro", blocks, step) for step in range(1, blocks)]

    tables = pl.pallas_call(
        functools.partial(tables_kernel, atoms),
        out_shape=[
            jax.ShapeDtypeStruct((2 * LANES, 4 * LANES), jnp.bfloat16),
            jax.ShapeDtypeStruct((2 * LANES, LANES), jnp.bfloat16),
            float_array(width, ROWS, LANES),
            float_array(width, ROWS, LANES),
            float_array(5, ROWS, LANES),
        ],
        in_specs=[smem(), vmem()],
        out_specs=[vmem()] * 5,
        compiler_params=params,
    )(atom_sites, stencil_weights(width))

    scalars = pl.pallas_call(
        functools.partial(vector_kernel, blocks),
        out_shape=float_array(3),
        in_specs=[smem(), smem()] + [vmem()] * blocks,
        out_specs=smem(),
        compiler_params=params,
    )(host_point, block[None], *field_blocks)

    source, scalars = lax.optimization_barrier((source, scalars))
    if last_count:
        last = pl.pallas_call(
            functools.partial(pack_pieces_kernel, parts, share, last_count, main_count),
            out_shape=[float_array(2 * last_count, held, LANES)] * parts,
            in_specs=[smem(), hbm()],
            out_specs=[vmem()] * parts,
            scratch_shapes=[pltpu.SemaphoreType.DMA((parts * 2,))],
            compiler_params=whole_params,
        )(here, source)
        last = [last[0]] + [shifted(last[step], "grid", parts, -step) for step in range(1, parts)]
    edge = (LANES - owned) // 2
    window = jnp.concatenate(
        [field_blocks[-1][:, owned - edge :], field_blocks[0], field_blocks[1 % blocks][:, :edge]], axis=1
    )

    def micro_call(kernel, count, inputs, scalar_inputs, outputs, scalar_outputs, cells):
        rows = 2 * count * width * ROWS
        cell = pltpu.VMEM((2 * count, width, ROWS, LANES), jnp.float32)
        return pl.pallas_call(
            kernel,
            out_shape=outputs,
            in_specs=[smem() if number < scalar_inputs else vmem() for number in range(len(inputs))],
            out_specs=[smem() if number in scalar_outputs else vmem() for number in range(len(outputs))],
            scratch_shapes=[cell] * cells
            + [
                pltpu.VMEM((rows, 2 * LANES), jnp.bfloat16),
                pltpu.VMEM((rows, 4 * LANES), jnp.float32),
                cell,
                pltpu.VMEM((rows, 2 * LANES), jnp.bfloat16),
                pltpu.VMEM((width, ROWS, LANES), jnp.float32),
            ],
            compiler_params=params,
            cost_estimate=pl.CostEstimate(
                flops=count * 3 * 2 * 512 * 256 * 256 * ORDER, bytes_accessed=4 * 1024 * 1024, transcendentals=0
            ),
        )(*inputs)

    def cells_of(count):
        return float_array(2 * count, width, ROWS, LANES)

    sums_shape = float_array(2, ROWS, LANES)
    main_psi, sums, potential = micro_call(
        functools.partial(first_kernel, parts, main_count, kinds, True),
        main_count,
        [scalars, main, *tables],
        1,
        [cells_of(main_count), sums_shape, float_array(width, ROWS, LANES)],
        (),
        1,
    )
    if last_count:
        last_psi, sums = micro_call(
            functools.partial(first_kernel, parts, last_count, kinds, False),
            last_count,
            [scalars, here, *last, potential, *tables, sums],
            2,
            [cells_of(last_count), sums_shape],
            (),
            1,
        )
    seen = [sums] + [shifted(sums, "grid", parts, step) for step in range(1, parts)]

    whole_shape = float_array(2, norb, held, LANES)
    message_shape = float_array(ROWS, LANES)
    result = []

    def give_back(pieces, count, first):
        return pl.pallas_call(
            functools.partial(unpack_kernel, parts, share, count, first),
            out_shape=whole_shape,
            in_specs=[anywhere()] + [hbm()] * len(result),
            out_specs=hbm(),
            scratch_shapes=[pltpu.SemaphoreType.DMA((parts * 2,))],
            input_output_aliases={1: 0} if result else {},
            compiler_params=params,
        )(exchanged(pieces, "grid"), *result)

    main_pieces, *rest = micro_call(
        functools.partial(second_kernel, parts, main_count, kinds, total_points, True, not last_count),
        main_count,
        [scalars, *seen, main_psi, potential, *tables],
        1,
        [float_array(parts, 2 * main_count, held, LANES)]
        + ([float_array(1), sums_shape] if last_count else [message_shape]),
        (1,) if last_count else (),
        2,
    )
    result = [give_back(main_pieces, main_count, 0)]
    message = rest[-1]
    if last_count:
        vector_value, second_sums = rest
        last_pieces, message = micro_call(
            functools.partial(second_kernel, parts, last_count, kinds, total_points, False, True),
            last_count,
            [scalars, vector_value, sums, second_sums, last_psi, potential, *tables],
            2,
            [float_array(parts, 2 * last_count, held, LANES), message_shape],
            (),
            2,
        )
    message = fold([message] + [shifted(message, "grid", parts, step) for step in range(1, parts)])
    if last_count:
        last_pieces, message = lax.optimization_barrier((last_pieces, message))
        result = [give_back(last_pieces, last_count, main_count)]
    result = result[0]
    orbitals_out = planes_of(result).reshape(2, norb, planes, points)

    messages = [message] + [shifted(message, "macro", blocks, step) for step in range(1, blocks)]
    fields_out = pl.pallas_call(
        functools.partial(fields_kernel, blocks, owned),
        out_shape=float_array(2, owned),
        in_specs=[smem()] + [vmem()] * (1 + blocks),
        out_specs=vmem(),
        compiler_params=params,
    )(block[None], window, *messages)
    return orbitals_out[None], fields_out


def solution(mesh):
    in_specs = (
        P("macro", None, None, "grid", None),
        P("grid", None),
        P(),
        P("macro"),
        P(None, "macro"),
    )
    out_specs = (P("macro", None, None, "grid", None), P(None, "macro"))
    return jax.shard_map(
        functools.partial(per_device, mesh.shape["grid"], mesh.shape["macro"]),
        mesh=mesh,
        in_specs=in_specs,
        out_specs=out_specs,
        check_vma=False,
    )
```
